32 devices in a mesh: groups: 2 (over y), sy: 4 (over z), sx: 2 (over core), ta: 2 (over x).
Axes of the slice: x: 2, y: 2, z: 4, core: 2. Of those that a mesh axis runs over, the one named last changes fastest.
Arguments:
- state_field: bfloat16 [8, 64, 32, 384], P(('groups', 'ta'), 'sy', 'sx'), parts along dimension 0, may hold values from -80 to 80
- outlier_flags: int32 [8, 64, 32], P(('groups', 'ta'), 'sy', 'sx'), parts along dimension 0, may hold values 0 or 1
- window_shift: int32 [2], replicated, may hold values from 1 to 8, as said below
- layer_norm_gain: float32 [384], replicated, may hold values from 0.1 to 1.9
- qkv_weight: bfloat16 [384, 1152], replicated, may hold values from -0.3125 to 0.3125
- out_weight: bfloat16 [384, 384], replicated, may hold values from -1.25 to 1.25
- position_bias: float32 [6, 2883], replicated, may hold values from -4 to 300
- cotangent: bfloat16 [8, 64, 32, 384], P(('groups', 'ta'), 'sy', 'sx'), parts along dimension 0, may hold values from -6 to 6
Outputs:
- update: bfloat16 [8, 64, 32, 384], P(('groups', 'ta'), 'sy', 'sx'), parts along dimension 0
- field_grad: bfloat16 [8, 64, 32, 384], P(('groups', 'ta'), 'sy', 'sx'), parts along dimension 0
- qkv_grad: float32 [768, 1152], P('groups'), parts along dimension 0
- out_grad: float32 [768, 384], P('groups'), parts along dimension 0
- norm_gain_gradient: float32 [768], P('groups'), parts along dimension 0
The draws below stay inside these ranges and needn't reach their ends.
There are 2 independent parts, one for each index of `groups`. The reference program is written for one: setup_inputs(seed, part) draws one part's arguments, and reference() takes and returns one part's arrays. A program takes and returns all parts, laid end to end along the dimension named above; an argument that names none is the same for every part. Nothing has to cross between parts.
Inputs may be any that keep to these rules, and one draw needn't show every extreme that they name: `window_shift`: one of the two shifts equals 8, the other is smaller.
All inputs are finite; a program needn't handle non-finite values. No bound on the sum of `outlier_flags` on one device may be relied on, other than what follows from the above.
Results may differ from the reference program's by a relative error of at most 0.011.
Values may be sent and summed in bfloat16 or wider, within the bound.
No kernel may reach another device: no remote copies, remote signals or barrier semaphores. Data moves between devices by JAX's collectives and lax.ppermute only.
A program may use at most 256 MiB of HBM per device.

```python
import math
import jax
import jax.numpy as jnp
from jax import lax

MODEL_WIDTH = 384
HEADS = 6
RIM = 8
RELS = 2883
FRAMES = 4
ROWS = 64
COLS = 32
N_SY = 4
N_SX = 2
N_TA = 2


def draw_state_field(key, part):
    key_base, key_chan, key_token = jax.random.split(key, 3)
    shape = (FRAMES, ROWS, COLS, MODEL_WIDTH)
    channel_scale = jnp.exp(jax.random.uniform(key_chan, (MODEL_WIDTH,), jnp.float32, 0.0, math.log(10.0)))
    token_scale = jnp.exp(jax.random.uniform(key_token, (FRAMES, ROWS, COLS, 1), jnp.float32, -0.5, 0.5))
    base_values = jnp.clip(jax.random.normal(key_base, shape, jnp.float32), -4.0, 4.0)
    return (base_values * channel_scale * token_scale).astype(jnp.bfloat16)


def draw_window_shift(key, part):
    key_other, key_which = jax.random.split(key, 2)
    other = jax.random.randint(key_other, (), 1, RIM)
    which = jax.random.randint(key_which, (), 0, 2)
    return jnp.where(jnp.arange(2) == which, RIM, other).astype(jnp.int32)


def draw_position_bias(key, part):
    base_values = jnp.clip(jax.random.normal(key, (HEADS, RELS), jnp.float32), -4.0, 4.0)
    return base_values


def touch_ends(entries, own_key, least, top_value):
    shape = entries.shape
    spot = [jax.random.randint(jax.random.fold_in(own_key, axis), (), 0, shape[axis]) for axis in range(len(shape))]
    entries = entries.at[tuple(spot)].set(least)
    longest = shape.index(max(shape))
    spot[longest] = (spot[longest] + 1) % shape[longest]
    return entries.at[tuple(spot)].set(top_value)


def block_levels(own_key, shape, pieces, smallest, top_value):
    loudness = 1.0
    for dim, blocks in pieces:
        steps = jax.random.uniform(jax.random.fold_in(jax.random.fold_in(own_key, 6), dim), (blocks,), jnp.float32, smallest / len(pieces), top_value / len(pieces))
        loudness = loudness * jnp.repeat(jnp.exp(steps), shape[dim] // blocks).reshape((-1,) + (1,) * (len(shape) - 1 - dim))
    return loudness


def bell_draw(own_key, extent, scale, reach, pieces=(), kind=jnp.bfloat16):
    level = block_levels(own_key, extent, pieces, -0.22, 0.18) if pieces else 1.0
    drawn = jax.random.normal(own_key, extent, jnp.float32) * scale * level
    return jnp.minimum(jnp.maximum(drawn, -reach), reach).astype(kind)


def setup_inputs(seed: int = 0, part: int = 0) -> dict:
    key_of = jax.random.split(jax.random.key(seed), 9)
    own_keys = jax.random.split(jax.random.fold_in(key_of[8], part), 9)
    state_field = draw_state_field(jax.random.fold_in(jax.random.fold_in(key_of[8], part), 71), part)
    outlier_flags = touch_ends((jax.random.randint(own_keys[1], (FRAMES, ROWS, COLS), 0, 8) < 1).astype(jnp.int32), jax.random.fold_in(own_keys[1], 1), 0, 1)
    window_shift = draw_window_shift(jax.random.fold_in(key_of[8], 71), part)
    layer_norm_gain = jnp.clip(1.0 + 0.18 * jax.random.normal(key_of[3], (MODEL_WIDTH,), jnp.float32), 0.1, 1.9)
    qkv_weight = bell_draw(key_of[4], (MODEL_WIDTH, 3 * MODEL_WIDTH), MODEL_WIDTH ** -0.5, 0.3125)
    out_weight = bell_draw(key_of[5], (MODEL_WIDTH, MODEL_WIDTH), (MODEL_WIDTH // 16) ** -0.5, 1.25)
    position_bias = draw_position_bias(jax.random.fold_in(key_of[8], 71), part)
    cotangent = bell_draw(own_keys[7], (FRAMES, ROWS, COLS, MODEL_WIDTH), 1.0, 6.0, ((0, 2), (1, 4), (2, 2)))
    return {"state_field": state_field, "outlier_flags": outlier_flags, "window_shift": window_shift, "layer_norm_gain": layer_norm_gain, "qkv_weight": qkv_weight, "out_weight": out_weight, "position_bias": position_bias, "cotangent": cotangent}


EPS = 1e-05

def position_table(position_bias):
    position = jnp.arange(512)
    frame_in = position // 256
    row_in = position // 16 % 16
    col_in = position % 16
    offset = (frame_in[None, :] - frame_in[:, None] + 1) * 961 + (row_in[None, :] - row_in[:, None] + 15) * 31 + (col_in[None, :] - col_in[:, None] + 15)
    return jnp.take(position_bias, offset, axis=1)

def to_cubes(grid):
    frame_total, row_total, col_total, channel_count = grid.shape
    shaped = grid.reshape(frame_total // 2, 2, row_total // 16, 16, col_total // 16, 16, channel_count)
    return shaped.transpose(0, 2, 4, 1, 3, 5, 6).reshape(-1, 512, channel_count)

def from_cubes(cubes, frame_total, row_total, col_total):
    channel_count = cubes.shape[-1]
    shaped = cubes.reshape(frame_total // 2, row_total // 16, col_total // 16, 2, 16, 16, channel_count)
    return shaped.transpose(0, 3, 1, 4, 2, 5, 6).reshape(frame_total, row_total, col_total, channel_count)

def split_heads(block_rows):
    token_count, head_all = block_rows.shape
    return block_rows.reshape(token_count, HEADS, head_all // HEADS).transpose(1, 0, 2)

def merge_heads(block_rows):
    head_count, token_count, head_width = block_rows.shape
    return block_rows.transpose(1, 0, 2).reshape(token_count, head_count * head_width)

def cube_probs(queries, key_rows, flag_cube, bias_table):
    score_scale = (MODEL_WIDTH // HEADS) ** (-0.5)
    raw_scores = jnp.einsum('hqd,hkd->hqk', queries.astype(jnp.float32), key_rows.astype(jnp.float32))
    diagonal = jnp.arange(512)[:, None] == jnp.arange(512)[None, :]
    allowed = (flag_cube == 0)[None, :] | diagonal
    scores = jnp.where(allowed[None], raw_scores * score_scale + bias_table, -1e+30)
    row_max = lax.optimization_barrier(jnp.max(scores, -1, keepdims=True))
    exponent = jnp.exp(scores - row_max)
    return exponent / lax.optimization_barrier(jnp.sum(exponent, -1, keepdims=True))

def cube_parts(qkv_cube):
    return (split_heads(qkv_cube[:, :MODEL_WIDTH]), split_heads(qkv_cube[:, MODEL_WIDTH:2 * MODEL_WIDTH]), split_heads(qkv_cube[:, 2 * MODEL_WIDTH:]))

def cube_forward(qkv_cube, flag_cube, bias_table):
    queries, key_rows, values = cube_parts(qkv_cube)
    probs_b = cube_probs(queries, key_rows, flag_cube, bias_table).astype(jnp.bfloat16)
    context = jnp.einsum('hqk,hkd->hqd', probs_b.astype(jnp.float32), values.astype(jnp.float32))
    return merge_heads(context).astype(jnp.bfloat16)

def cube_backward(qkv_cube, flag_cube, d_cube, bias_table):
    score_scale = (MODEL_WIDTH // HEADS) ** (-0.5)
    queries, key_rows, values = cube_parts(qkv_cube)
    probs = cube_probs(queries, key_rows, flag_cube, bias_table)
    probs_b = probs.astype(jnp.bfloat16).astype(jnp.float32)
    d_heads = split_heads(d_cube).astype(jnp.float32)
    d_probs = jnp.einsum('hqd,hkd->hqk', d_heads, values.astype(jnp.float32))
    d_scores = probs * (d_probs - lax.optimization_barrier(jnp.sum(probs * d_probs, -1, keepdims=True))) * score_scale
    d_scores = d_scores.astype(jnp.bfloat16).astype(jnp.float32)
    d_query = jnp.einsum('hqk,hkd->hqd', d_scores, key_rows.astype(jnp.float32))
    d_key = jnp.einsum('hqk,hqd->hkd', d_scores, queries.astype(jnp.float32))
    d_value = jnp.einsum('hqk,hqd->hkd', probs_b, d_heads)
    joined = jnp.concatenate([merge_heads(d_query), merge_heads(d_key), merge_heads(d_value)], 1)
    return joined.astype(jnp.bfloat16)

def roll_forward(grid, row_shift, col_shift):
    row_total = grid.shape[1]
    col_total = grid.shape[2]
    twice = jnp.concatenate([grid, grid], 1)
    grid = lax.dynamic_slice_in_dim(twice, row_shift.astype(jnp.int32), row_total, 1)
    twice = jnp.concatenate([grid, grid], 2)
    return lax.dynamic_slice_in_dim(twice, col_shift.astype(jnp.int32), col_total, 2)

def reference(state_field, outlier_flags, window_shift, layer_norm_gain, qkv_weight, out_weight, position_bias, cotangent):
    row_shift = window_shift[0]
    col_shift = window_shift[1]
    frame_total, row_total, col_total = (FRAMES, ROWS, COLS)
    rolled = roll_forward(state_field, row_shift, col_shift)
    rolled_flags = roll_forward(outlier_flags, row_shift, col_shift)
    values_f = rolled.astype(jnp.float32)
    row_mean = lax.optimization_barrier(jnp.mean(values_f, -1, keepdims=True))
    centred_input = values_f - row_mean
    inverse_deviation = lax.rsqrt(lax.optimization_barrier(jnp.mean(centred_input * centred_input, -1, keepdims=True)) + EPS)
    standardized_input = centred_input * inverse_deviation
    normed_output = (standardized_input * layer_norm_gain).astype(jnp.bfloat16)
    flattened = normed_output.reshape(-1, MODEL_WIDTH)
    qkv = jnp.dot(flattened, qkv_weight, preferred_element_type=jnp.float32).astype(jnp.bfloat16)
    cubes = to_cubes(qkv.reshape(frame_total, row_total, col_total, 3 * MODEL_WIDTH))
    flag_cubes = to_cubes(rolled_flags[..., None])[..., 0]
    bias_table = position_table(position_bias)
    context = lax.map(lambda members: cube_forward(members[0], members[1], bias_table), (cubes, flag_cubes))
    context_rows = from_cubes(context, frame_total, row_total, col_total).reshape(-1, MODEL_WIDTH)
    cot_rows = cotangent.reshape(-1, MODEL_WIDTH)
    update = jnp.dot(context_rows, out_weight, preferred_element_type=jnp.float32).astype(jnp.bfloat16)
    update = update.reshape(frame_total, row_total, col_total, MODEL_WIDTH)
    window_tile_count = N_TA * N_SY * N_SX
    out_grad = jnp.dot(context_rows.T, cot_rows, preferred_element_type=jnp.float32) / window_tile_count
    d_context = jnp.dot(cot_rows, out_weight.T, preferred_element_type=jnp.float32).astype(jnp.bfloat16)
    d_cubes = to_cubes(d_context.reshape(frame_total, row_total, col_total, MODEL_WIDTH))
    d_qkv = lax.map(lambda members: cube_backward(members[0], members[1], members[2], bias_table), (cubes, flag_cubes, d_cubes))
    d_qkv_rows = from_cubes(d_qkv, frame_total, row_total, col_total).reshape(-1, 3 * MODEL_WIDTH)
    qkv_grad = jnp.dot(flattened.T, d_qkv_rows, preferred_element_type=jnp.float32) / window_tile_count
    normed_gradient = jnp.dot(d_qkv_rows, qkv_weight.T, preferred_element_type=jnp.float32)
    standardized_rows = standardized_input.reshape(-1, MODEL_WIDTH)
    norm_gain_gradient = lax.optimization_barrier(jnp.sum(normed_gradient * standardized_rows, 0)) / window_tile_count
    standardized_gradient = normed_gradient * layer_norm_gain
    inverse_row_count = inverse_deviation.reshape(-1, 1)
    rolled_gradient = inverse_row_count * (standardized_gradient - lax.optimization_barrier(jnp.mean(standardized_gradient, -1, keepdims=True)) - standardized_rows * lax.optimization_barrier(jnp.mean(standardized_gradient * standardized_rows, -1, keepdims=True)))
    rolled_gradient = rolled_gradient.astype(jnp.bfloat16).reshape(frame_total, row_total, col_total, MODEL_WIDTH)
    twice = jnp.concatenate([rolled_gradient, rolled_gradient], 2)
    back = lax.dynamic_slice_in_dim(twice, (col_total - col_shift).astype(jnp.int32), col_total, 2)
    twice = jnp.concatenate([back, back], 1)
    field_grad = lax.dynamic_slice_in_dim(twice, (row_total - row_shift).astype(jnp.int32), row_total, 1)
    return (update, field_grad, qkv_grad, out_grad, norm_gain_gradient)
```

```python
import functools
import math

import jax
import jax.numpy as jnp
from jax import lax
from jax.experimental import pallas as pl
from jax.experimental.pallas import tpu as pltpu
from jax.sharding import PartitionSpec as P

MODEL_WIDTH = 384
HEADS = 6
HEAD_WIDTH = 64
RIM = 8
SIDE = 16
TOKENS = 512
HALF = 256
EPS = 1e-05
LOG2E = math.log2(math.e)
VMEM_LIMIT = 48 * 1024 * 1024

bf16 = jnp.bfloat16
f32 = jnp.float32


def nn(a, b):
    return lax.dot_general(a, b, (((1,), (0,)), ((), ())), preferred_element_type=f32)


def nt(a, b):
    return lax.dot_general(a, b, (((1,), (1,)), ((), ())), preferred_element_type=f32)


def tn(a, b):
    return lax.dot_general(a, b, (((0,), (0,)), ((), ())), preferred_element_type=f32)


def iota(shape, dim):
    return lax.broadcasted_iota(jnp.int32, shape, dim)


def prepare_kernel(strips, cot, out_weight, qkv_weight, bias_blocks, d_context_t, qkv_weight_t):
    lane = iota((SIDE, TOKENS), 1)
    for entry in range(HEADS * 3):
        even = jnp.broadcast_to(strips[2 * entry : 2 * entry + 1, :], (SIDE, TOKENS))
        odd = jnp.broadcast_to(strips[2 * entry + 1 : 2 * entry + 2, :], (SIDE, TOKENS))
        even = pltpu.roll(even, TOKENS - 15, 1, stride=1, stride_axis=0)
        odd = pltpu.roll(odd, 1, 1, stride=1, stride_axis=0)
        rows = jnp.where(lane % 32 < 16, even, odd) * LOG2E
        for row in range(SIDE):
            first = (15 - row) * SIDE
            bias_blocks[entry, row * SIDE : (row + 1) * SIDE, :] = rows[:, first : first + HALF]
    d_context_t[...] = nt(out_weight[...], cot[...]).astype(bf16)
    qkv_weight_t[...] = qkv_weight[...].T


def source_onehots(row_shift, col_shift, sign):
    token = iota((HALF, 1), 0)
    row = token // SIDE + sign * row_shift
    col = token % SIDE + sign * col_shift
    if sign > 0:
        row_out, col_out = row >= SIDE, col >= SIDE
        near_row, near_col = row - SIDE, col - SIDE
    else:
        row_out, col_out = row < 0, col < 0
        near_row, near_col = row + RIM, col + RIM
    inner = jnp.where(row_out | col_out, -1, row * SIDE + col)
    rows = jnp.where(row_out & ~col_out, near_row * SIDE + col, -1)
    cols = jnp.where(col_out & ~row_out, row * RIM + near_col, -1)
    corner = jnp.where(row_out & col_out, near_row * RIM + near_col, -1)
    return [
        (iota((HALF, count), 1) == place).astype(f32).astype(bf16)
        for place, count in ((inner, HALF), (rows, 128), (cols, 128), (corner, 64))
    ]


def flag_strip(flags, first, count, width):
    total = count * width
    repeat = (iota((width, total), 1) % width == iota((width, total), 0)).astype(f32).astype(bf16)
    spread = nn(flags[first : first + count, :], repeat)
    keep = iota((count, total), 1) // width == iota((count, total), 0)
    strip = jnp.sum(jnp.where(keep, spread, 0.0), 0, keepdims=True)
    return jnp.broadcast_to(strip, (128, total)).astype(bf16)


def attention_kernel(
    shift,
    inner,
    rows,
    cols,
    corner,
    inner_flags,
    gain,
    qkv_weight,
    qkv_weight_t,
    out_weight,
    cot,
    d_context_t,
    bias_blocks,
    update,
    grads,
    d_rolled,
    penalty,
    context_t,
    d_qkv,
):
    onehots = source_onehots(shift[0], shift[1], 1)
    rolled = []
    on_diagonal = iota((HALF, HALF), 0) == iota((HALF, HALF), 1)
    for t in range(2):
        parts = (
            inner[t * 256 : t * 256 + 256, :],
            rows[t * 128 : t * 128 + 128, :],
            cols[t * 128 : t * 128 + 128, :],
            corner[t * 64 : t * 64 + 64, :],
        )
        rolled.append(sum(nn(hot, part) for hot, part in zip(onehots, parts)))
        strips = (
            flag_strip(inner_flags, t * 16, 16, 16),
            flag_strip(rows[256:272, :16], t * 8, 8, 16),
            flag_strip(cols[256:288, :8], t * 16, 16, 8),
            flag_strip(corner[128:144, :8], t * 8, 8, 8),
        )
        marks = sum(nt(hot, strip) for hot, strip in zip(onehots, strips))
        column = jnp.where(marks > 0.5, -1e30, 0.0)
        wide = jnp.concatenate([column, column], 1)
        own = jnp.where(on_diagonal, 0.0, wide)
        penalty[t * HALF : (t + 1) * HALF, t * HALF : (t + 1) * HALF] = own
        penalty[t * HALF : (t + 1) * HALF, (1 - t) * HALF : (2 - t) * HALF] = wide
    rolled = jnp.concatenate(rolled, 0)
    centred = rolled - jnp.mean(rolled, -1, keepdims=True)
    inv_std = lax.rsqrt(jnp.mean(centred * centred, -1, keepdims=True) + EPS)
    xhat = centred * inv_std
    normed = (xhat * gain[...]).astype(bf16)
    normed_t = normed.T
    qkv_t = nt(qkv_weight_t[...], normed).astype(bf16)
    kv = nn(normed, qkv_weight[:, MODEL_WIDTH:]).astype(bf16)
    scale = LOG2E * HEAD_WIDTH ** (-0.5)
    zeros = jnp.zeros((HEAD_WIDTH, TOKENS), bf16)
    for pair in range(HEADS // 2):
        key_pair = kv[:, pair * 128 : pair * 128 + 128]
        value_pair = kv[:, MODEL_WIDTH + pair * 128 : MODEL_WIDTH + pair * 128 + 128]
        d_pair = [[], [], []]
        for side in range(2):
            head = 2 * pair + side
            at = head * HEAD_WIDTH
            q_t = qkv_t[at : at + HEAD_WIDTH, :]
            k_t = qkv_t[MODEL_WIDTH + at : MODEL_WIDTH + at + HEAD_WIDTH, :]
            v_t = qkv_t[2 * MODEL_WIDTH + at : 2 * MODEL_WIDTH + at + HEAD_WIDTH, :]
            d_t = d_context_t[at : at + HEAD_WIDTH, :]
            d_eighth = d_t * 0.125
            q_wide = jnp.concatenate([q_t, zeros] if side == 0 else [zeros, q_t], 0)
            d_wide = jnp.concatenate([d_eighth, zeros] if side == 0 else [zeros, d_eighth], 0)
            dq_parts = []
            dk_parts = [0.0, 0.0]
            dv_parts = [0.0, 0.0]
            for b in range(2):
                lanes = slice(b * HALF, (b + 1) * HALF)
                scores = nn(key_pair, q_wide[:, lanes])
                d_probs = nn(value_pair, d_wide[:, lanes])
                halves = [slice(a * HALF, (a + 1) * HALF) for a in range(2)]
                s = [
                    scores[halves[a]] * scale
                    + bias_blocks[head * 3 + b - a + 1]
                    + penalty[halves[a], lanes]
                    for a in range(2)
                ]
                top = jnp.maximum(
                    jnp.max(s[0], 0, keepdims=True), jnp.max(s[1], 0, keepdims=True)
                )
                e = [jnp.exp2(s[a] - top) for a in range(2)]
                total = jnp.sum(e[0], 0, keepdims=True) + jnp.sum(e[1], 0, keepdims=True)
                inverse = 1.0 / total
                p = [e[a] * inverse for a in range(2)]
                pb = [p[a].astype(bf16) for a in range(2)]
                context_t[at : at + HEAD_WIDTH, lanes] = (
                    nn(v_t[:, :HALF], pb[0]) + nn(v_t[:, HALF:], pb[1])
                ).astype(bf16)
                dp = [d_probs[halves[a]] for a in range(2)]
                delta = jnp.sum(p[0] * dp[0], 0, keepdims=True) + jnp.sum(
                    p[1] * dp[1], 0, keepdims=True
                )
                ds = [(p[a] * (dp[a] - delta)).astype(bf16) for a in range(2)]
                dq_parts.append(nn(k_t[:, :HALF], ds[0]) + nn(k_t[:, HALF:], ds[1]))
                for a in range(2):
                    dk_parts[a] = dk_parts[a] + nt(q_t[:, lanes], ds[a])
                    dv_parts[a] = dv_parts[a] + nt(d_t[:, lanes], pb[a])
            for kind, pieces in enumerate((dq_parts, dk_parts, dv_parts)):
                d_pair[kind].append(jnp.concatenate(pieces, 1).astype(bf16))
        for kind in range(3):
            first = kind * MODEL_WIDTH + pair * 128
            d_qkv[:, first : first + 128] = jnp.concatenate(d_pair[kind], 0).T
    update[...] = tn(context_t[...], out_weight[...]).astype(bf16)
    grads[:MODEL_WIDTH, :] = nn(context_t[...], cot[...]).astype(bf16)
    d_rows = d_qkv[...]
    for kind in range(3):
        columns = d_rows[:, kind * MODEL_WIDTH : (kind + 1) * MODEL_WIDTH]
        first = (kind + 1) * MODEL_WIDTH
        grads[first : first + MODEL_WIDTH, :] = nn(normed_t, columns).astype(bf16)
    d_xhat = nn(d_rows, qkv_weight_t[...]) * gain[...]
    d_rolled[...] = (
        inv_std
        * (
            d_xhat
            - jnp.mean(d_xhat, -1, keepdims=True)
            - xhat * jnp.mean(d_xhat * xhat, -1, keepdims=True)
        )
    ).astype(bf16)


def unroll_kernel(shift, inner, rows, cols, corner, field_grad):
    onehots = source_onehots(shift[0], shift[1], -1)
    for t in range(2):
        parts = (
            inner[t * 256 : t * 256 + 256, :],
            rows[t * 128 : t * 128 + 128, :],
            cols[t * 128 : t * 128 + 128, :],
            corner[t * 64 : t * 64 + 64, :],
        )
        field_grad[t * 256 : t * 256 + 256, :] = sum(
            nn(hot, part) for hot, part in zip(onehots, parts)
        ).astype(bf16)


def in_vmem(count):
    return [pl.BlockSpec(memory_space=pltpu.VMEM)] * count


def local_call(kernel, shapes, inputs, scratch=(), scalars=0):
    return pl.pallas_call(
        kernel,
        out_shape=[jax.ShapeDtypeStruct(shape, dtype) for shape, dtype in shapes],
        in_specs=[pl.BlockSpec(memory_space=pltpu.SMEM)] * scalars
        + in_vmem(len(inputs) - scalars),
        out_specs=in_vmem(len(shapes)),
        scratch_shapes=list(scratch),
        compiler_params=pltpu.CompilerParams(vmem_limit_bytes=VMEM_LIMIT),
    )(*inputs)


def passed_along(block, axis, distance):
    count = lax.axis_size(axis)
    return lax.ppermute(block, axis, [((i - distance) % count, i) for i in range(count)])


def scatter_sum(block, axis):
    count = lax.axis_size(axis)
    me = lax.axis_index(axis)
    share = block.shape[0] // count
    pick = lambda owner: lax.dynamic_slice_in_dim(block, owner * share, share, 0)
    arrived = [
        passed_along(pick(lax.rem(me + step, count)), axis, step) for step in range(1, count)
    ]
    total = pick(me).astype(f32)
    for piece in arrived:
        total = total + piece.astype(f32)
    return total.astype(bf16)


def gather_shares(block, axis):
    count = lax.axis_size(axis)
    me = lax.axis_index(axis)
    share = block.shape[0]
    pieces = [passed_along(block, axis, step) for step in range(count - 1, 0, -1)] + [block]
    ring = jnp.concatenate(pieces + pieces[:-1], 0)
    return lax.dynamic_slice_in_dim(ring, (count - 1 - me) * share, count * share, 0)


def shards(
    state_field,
    outlier_flags,
    window_shift,
    layer_norm_gain,
    qkv_weight,
    out_weight,
    position_bias,
    cotangent,
):
    width = MODEL_WIDTH
    marks = outlier_flags.astype(bf16)
    pad_marks = lambda m: jnp.pad(m, ((0, 0), (0, width - m.shape[1])))
    row_message = jnp.concatenate(
        [
            state_field[:, :RIM].reshape(2 * RIM * SIDE, width),
            pad_marks(marks[:, :RIM].reshape(2 * RIM, SIDE)),
        ],
        0,
    )
    col_message = jnp.concatenate(
        [
            state_field[:, :, :RIM].reshape(2 * SIDE * RIM, width),
            pad_marks(marks[:, :, :RIM].reshape(2 * SIDE, RIM)),
        ],
        0,
    )
    rows = passed_along(row_message, "sy", -1)
    cols = passed_along(col_message, "sx", -1)
    strips = position_bias[:, ::-1].reshape(HEADS, 3, 31, 31)
    strips = jnp.pad(strips, ((0, 0), (0, 0), (0, 1), (0, 1)))
    strips = strips.reshape(HEADS, 3, 16, 2, 32).transpose(0, 1, 3, 2, 4).reshape(36, TOKENS)
    cot_rows = cotangent.reshape(TOKENS, width)
    bias_blocks, d_context_t, qkv_weight_t = local_call(
        prepare_kernel,
        [((18, HALF, HALF), f32), ((width, TOKENS), bf16), ((3 * width, width), bf16)],
        [strips, cot_rows, out_weight, qkv_weight],
    )
    corner_message = jnp.concatenate(
        [
            rows[: 2 * RIM * SIDE].reshape(2 * RIM, SIDE, width)[:, :RIM].reshape(-1, width),
            rows[2 * RIM * SIDE :],
        ],
        0,
    )
    corner = passed_along(corner_message, "sx", -1)
    gain = layer_norm_gain.reshape(1, width)
    update, grads, d_rolled = local_call(
        attention_kernel,
        [((TOKENS, width), bf16), ((4 * width, width), bf16), ((TOKENS, width), bf16)],
        [
            window_shift,
            state_field.reshape(TOKENS, width),
            rows,
            cols,
            corner,
            marks.reshape(2 * SIDE, SIDE),
            gain,
            qkv_weight,
            qkv_weight_t,
            out_weight,
            cot_rows,
            d_context_t,
            bias_blocks,
        ],
        scratch=[
            pltpu.VMEM((TOKENS, TOKENS), f32),
            pltpu.VMEM((width, TOKENS), bf16),
            pltpu.VMEM((TOKENS, 3 * width), bf16),
        ],
        scalars=1,
    )
    grid = d_rolled.reshape(2, SIDE, SIDE, width)
    below = passed_along(grid[:, RIM:].reshape(-1, width), "sy", 1)
    beside = passed_along(grid[:, :, RIM:].reshape(-1, width), "sx", 1)
    across = passed_along(
        below.reshape(2 * RIM, SIDE, width)[:, RIM:].reshape(-1, width), "sx", 1
    )
    axes = ("sx", "ta", "sy")
    for axis in axes:
        grads = scatter_sum(grads, axis)
    for axis in reversed(axes):
        grads = gather_shares(grads, axis)
    (field_grad,) = local_call(
        unroll_kernel,
        [((TOKENS, width), bf16)],
        [window_shift, d_rolled, below, beside, across],
        scalars=1,
    )
    tiles = lax.axis_size("sy") * lax.axis_size("sx") * lax.axis_size("ta")
    grads = grads.astype(f32) / tiles
    out_grad = grads[:width]
    qkv_grad = jnp.concatenate([grads[width * k : width * (k + 1)] for k in (1, 2, 3)], 1)
    gain_grad = jnp.sum(qkv_grad * qkv_weight.astype(f32), 1) / layer_norm_gain
    shape = state_field.shape
    return (update.reshape(shape), field_grad.reshape(shape), qkv_grad, out_grad, gain_grad)


def solution(mesh):
    in_specs = (
        P(("groups", "ta"), "sy", "sx", None),
        P(("groups", "ta"), "sy", "sx"),
        P(),
        P(),
        P(),
        P(),
        P(),
        P(("groups", "ta"), "sy", "sx", None),
    )
    out_specs = (
        P(("groups", "ta"), "sy", "sx", None),
        P(("groups", "ta"), "sy", "sx", None),
        P("groups", None),
        P("groups", None),
        P("groups"),
    )
    return jax.shard_map(shards, mesh=mesh, in_specs=in_specs, out_specs=out_specs, check_vma=False)
```

```python
import functools
import math

import jax
import jax.numpy as jnp
from jax import lax
from jax.experimental import pallas as pl
from jax.experimental.pallas import tpu as pltpu
from jax.sharding import PartitionSpec as P

MODEL_WIDTH = 384
HEADS = 6
HEAD_WIDTH = 64
RIM = 8
SIDE = 16
TOKENS = 512
HALF = 256
EPS = 1e-05
LOG2E = math.log2(math.e)

bf16 = jnp.bfloat16
f32 = jnp.float32


def nn(a, b):
    return lax.dot_general(a, b, (((1,), (0,)), ((), ())), preferred_element_type=f32)


def nt(a, b):
    return lax.dot_general(a, b, (((1,), (1,)), ((), ())), preferred_element_type=f32)


def tn(a, b):
    return lax.dot_general(a, b, (((0,), (0,)), ((), ())), preferred_element_type=f32)


def iota(shape, dim):
    return lax.broadcasted_iota(jnp.int32, shape, dim)


def prepare_kernel(strips, cot, out_weight, qkv_weight, *outs):
    bias_blocks, d_context_t, qkv_weight_t = outs[:3], outs[3], outs[4]
    plain = strips[...] * LOG2E
    high = plain.astype(bf16)
    rest = plain - high.astype(f32)
    middle = rest.astype(bf16)
    low = (rest - middle.astype(f32)).astype(bf16)
    turn = iota((TOKENS, TOKENS), 0) + iota((TOKENS, TOKENS), 1) == TOKENS - 2
    turn = turn.astype(f32).astype(bf16)
    turned = nn(high, turn) + nn(middle, turn) + nn(low, turn)
    lane = iota((SIDE, TOKENS), 1)
    for entry in range(HEADS * 3):
        head, frame = divmod(entry, 3)
        first = 2 * (head * 3 + 2 - frame)
        even = jnp.broadcast_to(turned[first : first + 1, :], (SIDE, TOKENS))
        odd = jnp.broadcast_to(turned[first + 1 : first + 2, :], (SIDE, TOKENS))
        even = pltpu.roll(even, TOKENS - 15, 1, stride=1, stride_axis=0)
        odd = pltpu.roll(odd, TOKENS - 31, 1, stride=1, stride_axis=0)
        rows = jnp.where(lane % 32 < 16, even, odd)
        for row in range(SIDE):
            start = (15 - row) * SIDE
            bias_blocks[head // 2][entry % 6, row * SIDE : (row + 1) * SIDE, :] = rows[
                :, start : start + HALF
            ]
    d_context_t[...] = nt(out_weight[...], cot[...]).astype(bf16)
    qkv_weight_t[...] = qkv_weight[...].T


def source_onehots(row_shift, col_shift, sign):
    token = iota((HALF, 1), 0)
    row = token // SIDE + sign * row_shift
    col = token % SIDE + sign * col_shift
    if sign > 0:
        row_out, col_out = row >= SIDE, col >= SIDE
        near_row, near_col = row - SIDE, col - SIDE
    else:
        row_out, col_out = row < 0, col < 0
        near_row, near_col = row + RIM, col + RIM
    inner = jnp.where(row_out | col_out, -1, row * SIDE + col)
    rows = jnp.where(row_out & ~col_out, near_row * SIDE + col, -1)
    cols = jnp.where(col_out & ~row_out, row * RIM + near_col, -1)
    corner = jnp.where(row_out & col_out, near_row * RIM + near_col, -1)
    return [
        (iota((HALF, count), 1) == place).astype(f32).astype(bf16)
        for place, count in ((inner, HALF), (rows, 128), (cols, 128), (corner, 64))
    ]


def flag_strip(flags, first, count, width):
    total = count * width
    repeat = (iota((width, total), 1) % width == iota((width, total), 0)).astype(f32).astype(bf16)
    spread = nn(flags[first : first + count, :], repeat)
    keep = iota((count, total), 1) // width == iota((count, total), 0)
    strip = jnp.sum(jnp.where(keep, spread, 0.0), 0, keepdims=True)
    return jnp.broadcast_to(strip, (128, total)).astype(bf16)


def layer_norm(rolled):
    centred = rolled - jnp.mean(rolled, -1, keepdims=True)
    inv_std = lax.rsqrt(jnp.mean(centred * centred, -1, keepdims=True) + EPS)
    return centred * inv_std, inv_std


def attention_head(head, qkv_t, kv, penalty, bias_blocks, d_context_t):
    pair, side = divmod(head, 2)
    at = head * HEAD_WIDTH
    scale = LOG2E * HEAD_WIDTH ** (-0.5)
    zeros = jnp.zeros((HEAD_WIDTH, TOKENS), bf16)
    key_pair = kv[:, pair * 128 : pair * 128 + 128]
    value_pair = kv[:, MODEL_WIDTH + pair * 128 : MODEL_WIDTH + pair * 128 + 128]
    q_t = qkv_t[at : at + HEAD_WIDTH, :]
    k_t = qkv_t[MODEL_WIDTH + at : MODEL_WIDTH + at + HEAD_WIDTH, :]
    v_t = qkv_t[2 * MODEL_WIDTH + at : 2 * MODEL_WIDTH + at + HEAD_WIDTH, :]
    d_t = d_context_t[at : at + HEAD_WIDTH, :]
    d_eighth = d_t * 0.125
    q_wide = jnp.concatenate([q_t, zeros] if side == 0 else [zeros, q_t], 0)
    d_wide = jnp.concatenate([d_eighth, zeros] if side == 0 else [zeros, d_eighth], 0)
    context_parts = []
    dq_parts = []
    dk_parts = [0.0, 0.0]
    dv_parts = [0.0, 0.0]
    for b in range(2):
        lanes = slice(b * HALF, (b + 1) * HALF)
        scores = nn(key_pair, q_wide[:, lanes])
        d_probs = nn(value_pair, d_wide[:, lanes])
        halves = [slice(a * HALF, (a + 1) * HALF) for a in range(2)]
        s = [
            scores[halves[a]] * scale
            + bias_blocks[side * 3 + b - a + 1]
            + penalty[halves[a], lanes]
            for a in range(2)
        ]
        top = jnp.maximum(jnp.max(s[0], 0, keepdims=True), jnp.max(s[1], 0, keepdims=True))
        e = [jnp.exp2(s[a] - top) for a in range(2)]
        total = jnp.sum(e[0], 0, keepdims=True) + jnp.sum(e[1], 0, keepdims=True)
        inverse = 1.0 / total
        p = [e[a] * inverse for a in range(2)]
        pb = [p[a].astype(bf16) for a in range(2)]
        context_parts.append(nn(v_t[:, :HALF], pb[0]) + nn(v_t[:, HALF:], pb[1]))
        dp = [d_probs[halves[a]] for a in range(2)]
        delta = jnp.sum(p[0] * dp[0], 0, keepdims=True) + jnp.sum(p[1] * dp[1], 0, keepdims=True)
        ds = [(p[a] * (dp[a] - delta)).astype(bf16) for a in range(2)]
        dq_parts.append(nn(k_t[:, :HALF], ds[0]) + nn(k_t[:, HALF:], ds[1]))
        for a in range(2):
            dk_parts[a] = dk_parts[a] + nt(q_t[:, lanes], ds[a])
            dv_parts[a] = dv_parts[a] + nt(d_t[:, lanes], pb[a])
    return [
        jnp.concatenate(parts, 1).astype(bf16)
        for parts in (context_parts, dq_parts, dk_parts, dv_parts)
    ]


def finish_pair(left, right, normed_t, cot, grads, d_qkv, context_t):
    context, *d_parts = [jnp.concatenate(both, 0) for both in zip(left, right)]
    context_t[...] = context
    for kind in range(3):
        d_qkv[:, kind * 128 : kind * 128 + 128] = d_parts[kind].T
    grads[:128, :] = nn(context, cot[...]).astype(bf16)
    grads[128:, :] = nn(normed_t[...], d_qkv[...]).astype(bf16)


def first_kernel(
    shift,
    inner,
    halo,
    flags,
    gain,
    qkv_weight,
    qkv_weight_t,
    bias_blocks,
    d_context_t,
    cot,
    grads,
    d_qkv,
    context_t,
    rolled_out,
    qkv_t,
    kv,
    normed_t,
    penalty,
):
    onehots = source_onehots(shift[0], shift[1], 1)
    rolled = []
    on_diagonal = iota((HALF, HALF), 0) == iota((HALF, HALF), 1)
    for t in range(2):
        parts = (
            inner[t * 256 : t * 256 + 256, :],
            halo[t * 128 : t * 128 + 128, :],
            halo[256 + t * 128 : 384 + t * 128, :],
            halo[512 + t * 64 : 576 + t * 64, :],
        )
        rolled.append(sum(nn(hot, part) for hot, part in zip(onehots, parts)))
        strips = (
            flag_strip(flags[:32, :16], t * 16, 16, 16),
            flag_strip(flags[32:48, :16], t * 8, 8, 16),
            flag_strip(flags[48:80, :8], t * 16, 16, 8),
            flag_strip(flags[80:96, :8], t * 8, 8, 8),
        )
        marks = sum(nt(hot, strip) for hot, strip in zip(onehots, strips))
        column = jnp.where(marks > 0.5, -1e30, 0.0)
        wide = jnp.concatenate([column, column], 1)
        own = jnp.where(on_diagonal, 0.0, wide)
        penalty[t * HALF : (t + 1) * HALF, t * HALF : (t + 1) * HALF] = own
        penalty[t * HALF : (t + 1) * HALF, (1 - t) * HALF : (2 - t) * HALF] = wide
    rolled = jnp.concatenate(rolled, 0)
    rolled_out[...] = rolled.astype(bf16)
    xhat, _ = layer_norm(rolled)
    normed = (xhat * gain[...]).astype(bf16)
    normed_t[...] = normed.T
    qkv_t[...] = nt(qkv_weight_t[...], normed).astype(bf16)
    kv[...] = nn(normed, qkv_weight[:, MODEL_WIDTH:]).astype(bf16)
    heads = [attention_head(h, qkv_t, kv, penalty, bias_blocks, d_context_t) for h in range(2)]
    finish_pair(*heads, normed_t, cot, grads, d_qkv, context_t)


def left_kernel(pair, qkv_t, kv, penalty, bias_blocks, d_context_t, left):
    parts = attention_head(2 * pair, qkv_t, kv, penalty, bias_blocks, d_context_t)
    left[...] = jnp.concatenate(parts, 0)


def right_kernel(
    pair, qkv_t, kv, penalty, bias_blocks, d_context_t, left, normed_t, cot, *outs
):
    right = attention_head(2 * pair + 1, qkv_t, kv, penalty, bias_blocks, d_context_t)
    parts = [left[k * HEAD_WIDTH : (k + 1) * HEAD_WIDTH, :] for k in range(4)]
    finish_pair(parts, right, normed_t, cot, *outs)


def token_kernel(
    rolled, gain, qkv_weight, out_weight, d0, d1, d2, c0, c1, c2, update, d_rolled
):
    xhat, inv_std = layer_norm(rolled[...].astype(f32))
    d_normed = 0.0
    for pair, d_qkv in enumerate((d0, d1, d2)):
        columns = [
            qkv_weight[:, k * MODEL_WIDTH + pair * 128 : k * MODEL_WIDTH + pair * 128 + 128]
            for k in range(3)
        ]
        d_normed = d_normed + nt(d_qkv[...], jnp.concatenate(columns, 1))
    d_xhat = d_normed * gain[...]
    d_rolled[...] = (
        inv_std
        * (
            d_xhat
            - jnp.mean(d_xhat, -1, keepdims=True)
            - xhat * jnp.mean(d_xhat * xhat, -1, keepdims=True)
        )
    ).astype(bf16)
    context_t = jnp.concatenate([c0[...], c1[...], c2[...]], 0)
    update[...] = tn(context_t, out_weight[...]).astype(bf16)


def finish_kernel(pair, scale, *refs):
    core, mine, other, weight, gain = refs[:5]
    qkv_grad, out_grad, partial, gain_grad = refs[-4:]
    before = refs[-5] if pair else None
    first = core[0] == 0
    own, far = mine[...].astype(f32), other[...].astype(f32)
    upper = jnp.where(first, own, far) * scale
    lower = jnp.where(first, far, own) * scale
    out_grad[...] = upper[:128]
    block = jnp.concatenate([upper[128:], lower], 0)
    qkv_grad[...] = block
    product = block * weight[...].astype(f32)
    kind = pl.program_id(0)

    @pl.when(kind == 0)
    def _():
        partial[...] = (product + before[...]) if pair else product

    @pl.when(kind > 0)
    def _():
        partial[...] += product

    gain_grad[...] = jnp.sum(partial[...].T, 0, keepdims=True) / gain[...]


def unroll_kernel(shift, inner, halo, field_grad):
    onehots = source_onehots(shift[0], shift[1], -1)
    for t in range(2):
        parts = (
            inner[t * 256 : t * 256 + 256, :],
            halo[t * 128 : t * 128 + 128, :],
            halo[256 + t * 128 : 384 + t * 128, :],
            halo[512 + t * 64 : 576 + t * 64, :],
        )
        field_grad[t * 256 : t * 256 + 256, :] = sum(
            nn(hot, part) for hot, part in zip(onehots, parts)
        ).astype(bf16)


def local_call(kernel, shapes, inputs, scalars=0, micros=1, limit=24, after=(), hold=False):
    vmem = pl.BlockSpec(memory_space=pltpu.VMEM)
    smem = pl.BlockSpec(memory_space=pltpu.SMEM)
    anywhere = [pl.BlockSpec(memory_space=pl.ANY)] * len(after)
    count = len(inputs)
    held = list(after) if hold else []

    def body(*refs):
        kernel(*refs[:count], *refs[count + len(after) : len(refs) - len(held)])

    return pl.pallas_call(
        body,
        out_shape=[jax.ShapeDtypeStruct(shape, dtype) for shape, dtype in shapes]
        + [jax.ShapeDtypeStruct(array.shape, array.dtype) for array in held],
        in_specs=[smem] * scalars + [vmem] * (count - scalars) + anywhere,
        out_specs=[vmem] * len(shapes) + anywhere[: len(held)],
        input_output_aliases={count + i: len(shapes) + i for i in range(len(held))},
        compiler_params=pltpu.CompilerParams(vmem_limit_bytes=limit * 2**20),
        cost_estimate=pl.CostEstimate(
            flops=micros * 10**9, bytes_accessed=10**6, transcendentals=0
        ),
    )(*inputs, *after)


def finish_call(pair, scale, core, mine, other, qkv_weight, gain, earlier):
    width = MODEL_WIDTH
    half = pl.BlockSpec((256, 128), lambda k: (0, k))
    whole = pl.BlockSpec((width, 128), lambda k: (0, 0))
    row = pl.BlockSpec((1, width), lambda k: (0, 0))
    columns = pl.BlockSpec((width, 128), lambda k: (0, 3 * k + pair))
    in_specs = [pl.BlockSpec(memory_space=pltpu.SMEM), half, half, columns, row]
    inputs = [core, mine, other, qkv_weight, gain]
    aliases = {}
    if pair:
        in_specs += [pl.BlockSpec(memory_space=pl.ANY)] * 2 + [whole]
        inputs += list(earlier[:3])
        aliases = {5: 0, 6: 1}
    return pl.pallas_call(
        functools.partial(finish_kernel, pair, scale),
        grid=(3,),
        out_shape=[
            jax.ShapeDtypeStruct((width, 3 * width), f32),
            jax.ShapeDtypeStruct((width, width), f32),
            jax.ShapeDtypeStruct((width, 128), f32),
            jax.ShapeDtypeStruct((1, width), f32),
        ],
        in_specs=in_specs,
        out_specs=[columns, pl.BlockSpec((128, 128), lambda k: (pair, k)), whole, row],
        input_output_aliases=aliases,
        compiler_params=pltpu.CompilerParams(vmem_limit_bytes=16 * 2**20),
    )(*inputs)


def passed_along(block, axis, distance):
    count = lax.axis_size(axis)
    return lax.ppermute(block, axis, [((i - distance) % count, i) for i in range(count)])


def swapped(block, axis, bit):
    return lax.ppermute(block, axis, [(i, i ^ bit) for i in range(lax.axis_size(axis))])


def upper_side(axis, bit):
    return (lax.axis_index(axis) & bit) // bit


def halve(block, axis, bit):
    side = upper_side(axis, bit)
    share = block.shape[0] // 2
    far = lax.dynamic_slice_in_dim(block, (1 - side) * share, share, 0)
    own = lax.dynamic_slice_in_dim(block, side * share, share, 0)
    return (own.astype(f32) + swapped(far, axis, bit).astype(f32)).astype(bf16)


def double(block, axis, bit):
    other = swapped(block, axis, bit)
    above = upper_side(axis, bit) == 1
    return jnp.concatenate([jnp.where(above, other, block), jnp.where(above, block, other)], 0)


def axis_bits(axis):
    count = lax.axis_size(axis)
    return [(axis, 1 << k) for k in range(count.bit_length() - 1)]


def shards(
    state_field,
    outlier_flags,
    window_shift,
    layer_norm_gain,
    qkv_weight,
    out_weight,
    position_bias,
    cotangent,
):
    width = MODEL_WIDTH
    wide = lambda tokens: ((tokens, width), bf16)
    rows = passed_along(state_field[:, :RIM].reshape(-1, width), "sy", -1)
    marks = outlier_flags.astype(bf16)
    row_marks = passed_along(marks[:, :RIM].reshape(2 * RIM, SIDE), "sy", -1)
    cols = passed_along(state_field[:, :, :RIM].reshape(-1, width), "sx", -1)
    col_marks = passed_along(marks[:, :, :RIM].reshape(2 * SIDE, RIM), "sx", -1)
    strips = jnp.pad(
        position_bias.reshape(HEADS, 3, 31, 31), ((0, 0), (0, 0), (0, 1), (0, 1))
    )
    strips = strips.reshape(HEADS, 3, 16, 2, 32).transpose(0, 1, 3, 2, 4).reshape(36, TOKENS)
    cot_rows = cotangent.reshape(TOKENS, width)
    *bias_blocks, d_context_t, qkv_weight_t = local_call(
        prepare_kernel,
        [((6, HALF, HALF), f32)] * 3 + [((width, TOKENS), bf16), wide(3 * width)],
        [strips, cot_rows, out_weight, qkv_weight],
        micros=3,
    )
    corner = passed_along(
        rows.reshape(2 * RIM, SIDE, width)[:, :RIM].reshape(-1, width), "sx", -1
    )
    corner_marks = passed_along(row_marks[:, :RIM], "sx", -1)
    halo = jnp.concatenate([rows, cols, corner], 0)
    all_marks = jnp.concatenate(
        [jnp.pad(m, ((0, 0), (0, 128 - m.shape[1])))
         for m in (marks.reshape(2 * SIDE, SIDE), row_marks, col_marks, corner_marks)],
        0,
    )
    gain = layer_norm_gain.reshape(1, width)
    pair_shapes = [wide(TOKENS), wide(TOKENS), ((128, TOKENS), bf16)]
    grads, d_qkv, context_t, rolled, *shared = local_call(
        first_kernel,
        pair_shapes
        + [
            wide(TOKENS),
            ((3 * width, TOKENS), bf16),
            ((TOKENS, 2 * width), bf16),
            ((width, TOKENS), bf16),
            ((TOKENS, TOKENS), f32),
        ],
        [
            window_shift,
            state_field.reshape(TOKENS, width),
            halo,
            all_marks,
            gain,
            qkv_weight,
            qkv_weight_t,
            bias_blocks[0],
            d_context_t,
            cot_rows,
        ],
        scalars=1,
        micros=6,
    )
    bits = axis_bits("sx") + axis_bits("ta") + axis_bits("sy")
    results = [(grads, d_qkv, context_t)]
    qkv_t, kv, normed_t, penalty = shared
    common = lambda pair: [qkv_t, kv, penalty, bias_blocks[pair], d_context_t]
    left = lambda pair, after: local_call(
        functools.partial(left_kernel, pair),
        [((4 * HEAD_WIDTH, TOKENS), bf16)],
        common(pair),
        micros=2,
        after=after,
    )
    right = lambda pair, part, after: local_call(
        functools.partial(right_kernel, pair),
        pair_shapes,
        [*common(pair), *part, normed_t, cot_rows],
        micros=3,
        after=after,
    )
    part = left(1, [])
    first = halve(grads, *bits[0])
    results.append(right(1, part, [first]))
    first = halve(first, *bits[1])
    part = left(2, [first])
    first = halve(first, *bits[2])
    second = halve(results[1][0], *bits[0])
    results.append(right(2, part, [first, second]))
    first = halve(first, *bits[3])
    second = halve(second, *bits[1])
    update, d_rolled, first, second = local_call(
        token_kernel,
        [wide(TOKENS), wide(TOKENS)],
        [rolled, gain, qkv_weight, out_weight]
        + [r[1] for r in results]
        + [r[2] for r in results],
        micros=2,
        after=[first, second],
        hold=True,
    )
    shares = [first, second, results[2][0]]
    grid = d_rolled.reshape(2, SIDE, SIDE, width)
    below = passed_along(grid[:, RIM:].reshape(-1, width), "sy", 1)
    beside = passed_along(grid[:, :, RIM:].reshape(-1, width), "sx", 1)
    across = passed_along(
        below.reshape(2 * RIM, SIDE, width)[:, RIM:].reshape(-1, width), "sx", 1
    )
    (field_grad,) = local_call(
        unroll_kernel,
        [wide(TOKENS)],
        [window_shift, d_rolled, jnp.concatenate([below, beside, across], 0)],
        scalars=1,
    )
    scale = 1.0 / (lax.axis_size("sy") * lax.axis_size("sx") * lax.axis_size("ta"))
    core = lax.axis_index("sx").astype(jnp.int32).reshape(1)
    done = None
    for pair in range(3):
        share = shares[pair]
        for axis, bit in bits[(4, 2, 0)[pair] :]:
            share = halve(share, axis, bit)
        for axis, bit in bits[:0:-1]:
            share = double(share, axis, bit)
        other = swapped(share, *bits[0])
        done = finish_call(pair, scale, core, share, other, qkv_weight, gain, done)
    qkv_grad, out_grad, _, gain_grad = done
    shape = state_field.shape
    return (
        update.reshape(shape),
        field_grad.reshape(shape),
        qkv_grad,
        out_grad,
        gain_grad.reshape(width),
    )


def solution(mesh):
    in_specs = (
        P(("groups", "ta"), "sy", "sx", None),
        P(("groups", "ta"), "sy", "sx"),
        P(),
        P(),
        P(),
        P(),
        P(),
        P(("groups", "ta"), "sy", "sx", None),
    )
    out_specs = (
        P(("groups", "ta"), "sy", "sx", None),
        P(("groups", "ta"), "sy", "sx", None),
        P("groups", None),
        P("groups", None),
        P("groups"),
    )
    return jax.shard_map(shards, mesh=mesh, in_specs=in_specs, out_specs=out_specs, check_vma=False)
```

```python
import math

import jax
import jax.numpy as jnp
from jax import lax
from jax.experimental import pallas as pl
from jax.experimental.pallas import tpu as pltpu
from jax.sharding import PartitionSpec as P

MODEL_WIDTH = 384
HEADS = 6
HEAD_WIDTH = 64
RIM = 8
SIDE = 16
TOKENS = 512
HALF = 256
EPS = 1e-05
LOG2E = math.log2(math.e)

bf16 = jnp.bfloat16
f32 = jnp.float32


def nn(a, b):
    return lax.dot_general(a, b, (((1,), (0,)), ((), ())), preferred_element_type=f32)


def nt(a, b):
    return lax.dot_general(a, b, (((1,), (1,)), ((), ())), preferred_element_type=f32)


def tn(a, b):
    return lax.dot_general(a, b, (((0,), (0,)), ((), ())), preferred_element_type=f32)


def iota(shape, dim):
    return lax.broadcasted_iota(jnp.int32, shape, dim)


def prepare_kernel(strips, cot, out_weight, qkv_weight, *refs):
    outs, (bias_blocks, d_context_t, qkv_weight_t), sems = refs[:5], refs[5:8], refs[8]
    parts = [bias_blocks.at[k] for k in range(3)] + [d_context_t, qkv_weight_t]
    copies = [pltpu.make_async_copy(part, outs[k], sems.at[k]) for k, part in enumerate(parts)]
    qkv_weight_t[...] = qkv_weight[...].T
    copies[4].start()
    d_context_t[...] = nt(out_weight[...], cot[...]).astype(bf16)
    copies[3].start()
    plain = strips[...] * LOG2E
    high = plain.astype(bf16)
    rest = plain - high.astype(f32)
    middle = rest.astype(bf16)
    low = (rest - middle.astype(f32)).astype(bf16)
    turn = iota((TOKENS, TOKENS), 0) + iota((TOKENS, TOKENS), 1) == TOKENS - 2
    turn = turn.astype(f32).astype(bf16)
    turned = nn(high, turn) + nn(middle, turn) + nn(low, turn)
    lane = iota((SIDE, TOKENS), 1)
    for entry in range(HEADS * 3):
        head, frame = divmod(entry, 3)
        first = 2 * (head * 3 + 2 - frame)
        even = jnp.broadcast_to(turned[first : first + 1, :], (SIDE, TOKENS))
        odd = jnp.broadcast_to(turned[first + 1 : first + 2, :], (SIDE, TOKENS))
        even = pltpu.roll(even, TOKENS - 15, 1, stride=1, stride_axis=0)
        odd = pltpu.roll(odd, TOKENS - 31, 1, stride=1, stride_axis=0)
        rows = jnp.where(lane % 32 < 16, even, odd)
        for row in range(SIDE):
            start = (15 - row) * SIDE
            bias_blocks[head // 2, entry % 6, row * SIDE : (row + 1) * SIDE, :] = rows[
                :, start : start + HALF
            ]
        if entry % 6 == 5:
            copies[head // 2].start()
    for copy in copies:
        copy.wait()


def source_onehots(row_shift, col_shift, sign):
    token = iota((HALF, 1), 0)
    row = token // SIDE + sign * row_shift
    col = token % SIDE + sign * col_shift
    if sign > 0:
        row_out, col_out = row >= SIDE, col >= SIDE
        near_row, near_col = row - SIDE, col - SIDE
    else:
        row_out, col_out = row < 0, col < 0
        near_row, near_col = row + RIM, col + RIM
    inner = jnp.where(row_out | col_out, -1, row * SIDE + col)
    rows = jnp.where(row_out & ~col_out, near_row * SIDE + col, -1)
    cols = jnp.where(col_out & ~row_out, row * RIM + near_col, -1)
    corner = jnp.where(row_out & col_out, near_row * RIM + near_col, -1)
    return [
        (iota((HALF, count), 1) == place).astype(f32).astype(bf16)
        for place, count in ((inner, HALF), (rows, 128), (cols, 128), (corner, 64))
    ]


def flag_strip(flags, first, count, width):
    total = count * width
    repeat = (iota((width, total), 1) % width == iota((width, total), 0)).astype(f32).astype(bf16)
    spread = nn(flags[first : first + count, :], repeat)
    keep = iota((count, total), 1) // width == iota((count, total), 0)
    strip = jnp.sum(jnp.where(keep, spread, 0.0), 0, keepdims=True)
    return jnp.broadcast_to(strip, (128, total)).astype(bf16)


def layer_norm(rolled):
    centred = rolled - jnp.mean(rolled, -1, keepdims=True)
    inv_std = lax.rsqrt(jnp.mean(centred * centred, -1, keepdims=True) + EPS)
    return centred * inv_std, inv_std


def attention_head(head, qkv_t, kv, penalty, bias_blocks, d_context_t):
    pair, side = divmod(head, 2)
    at = head * HEAD_WIDTH
    scale = LOG2E * HEAD_WIDTH ** (-0.5)
    zeros = jnp.zeros((HEAD_WIDTH, TOKENS), bf16)
    key_pair = kv[:, pair * 128 : pair * 128 + 128]
    value_pair = kv[:, MODEL_WIDTH + pair * 128 : MODEL_WIDTH + pair * 128 + 128]
    q_t = qkv_t[at : at + HEAD_WIDTH, :]
    k_t = qkv_t[MODEL_WIDTH + at : MODEL_WIDTH + at + HEAD_WIDTH, :]
    v_t = qkv_t[2 * MODEL_WIDTH + at : 2 * MODEL_WIDTH + at + HEAD_WIDTH, :]
    d_t = d_context_t[at : at + HEAD_WIDTH, :]
    d_eighth = d_t * 0.125
    q_wide = jnp.concatenate([q_t, zeros] if side == 0 else [zeros, q_t], 0)
    d_wide = jnp.concatenate([d_eighth, zeros] if side == 0 else [zeros, d_eighth], 0)
    context_parts = []
    dq_parts = []
    dk_parts = [0.0, 0.0]
    dv_parts = [0.0, 0.0]
    for b in range(2):
        lanes = slice(b * HALF, (b + 1) * HALF)
        scores = nn(key_pair, q_wide[:, lanes])
        d_probs = nn(value_pair, d_wide[:, lanes])
        halves = [slice(a * HALF, (a + 1) * HALF) for a in range(2)]
        s = [
            scores[halves[a]] * scale
            + bias_blocks[side * 3 + b - a + 1]
            + penalty[halves[a], lanes]
            for a in range(2)
        ]
        top = jnp.maximum(jnp.max(s[0], 0, keepdims=True), jnp.max(s[1], 0, keepdims=True))
        e = [jnp.exp2(s[a] - top) for a in range(2)]
        total = jnp.sum(e[0], 0, keepdims=True) + jnp.sum(e[1], 0, keepdims=True)
        inverse = 1.0 / total
        p = [e[a] * inverse for a in range(2)]
        pb = [p[a].astype(bf16) for a in range(2)]
        context_parts.append(nn(v_t[:, :HALF], pb[0]) + nn(v_t[:, HALF:], pb[1]))
        dp = [d_probs[halves[a]] for a in range(2)]
        delta = jnp.sum(p[0] * dp[0], 0, keepdims=True) + jnp.sum(p[1] * dp[1], 0, keepdims=True)
        ds = [(p[a] * (dp[a] - delta)).astype(bf16) for a in range(2)]
        dq_parts.append(nn(k_t[:, :HALF], ds[0]) + nn(k_t[:, HALF:], ds[1]))
        for a in range(2):
            dk_parts[a] = dk_parts[a] + nt(q_t[:, lanes], ds[a])
            dv_parts[a] = dv_parts[a] + nt(d_t[:, lanes], pb[a])
    return [
        jnp.concatenate(parts, 1).astype(bf16)
        for parts in (context_parts, dq_parts, dk_parts, dv_parts)
    ]


def main_kernel(
    shift,
    inner,
    halo,
    flags,
    gain,
    qkv_weight,
    cot,
    weight_t_far,
    d_context_far,
    bias0_far,
    bias1_far,
    bias2_far,
    grads,
    d_rolled,
    kept_far,
    context_far,
    penalty,
    qkv_weight_t,
    d_context_t,
    bias_blocks,
    context_t,
    d_qkv,
    sems,
):
    sources = (weight_t_far, d_context_far, bias0_far, bias1_far, bias2_far)
    places = [qkv_weight_t, d_context_t] + [bias_blocks.at[k] for k in range(3)]
    arrivals = [
        pltpu.make_async_copy(source, place, sems.at[k])
        for k, (source, place) in enumerate(zip(sources, places))
    ]
    for copy in arrivals:
        copy.start()
    onehots = source_onehots(shift[0], shift[1], 1)
    rolled = []
    on_diagonal = iota((HALF, HALF), 0) == iota((HALF, HALF), 1)
    for t in range(2):
        parts = (
            inner[t * 256 : t * 256 + 256, :],
            halo[t * 128 : t * 128 + 128, :],
            halo[256 + t * 128 : 384 + t * 128, :],
            halo[512 + t * 64 : 576 + t * 64, :],
        )
        rolled.append(sum(nn(hot, part) for hot, part in zip(onehots, parts)))
        strips = (
            flag_strip(flags[:32, :16], t * 16, 16, 16),
            flag_strip(flags[32:48, :16], t * 8, 8, 16),
            flag_strip(flags[48:80, :8], t * 16, 16, 8),
            flag_strip(flags[80:96, :8], t * 8, 8, 8),
        )
        marks = sum(nt(hot, strip) for hot, strip in zip(onehots, strips))
        column = jnp.where(marks > 0.5, -1e30, 0.0)
        wide = jnp.concatenate([column, column], 1)
        own = jnp.where(on_diagonal, 0.0, wide)
        penalty[t * HALF : (t + 1) * HALF, t * HALF : (t + 1) * HALF] = own
        penalty[t * HALF : (t + 1) * HALF, (1 - t) * HALF : (2 - t) * HALF] = wide
    xhat, inv_std = layer_norm(jnp.concatenate(rolled, 0))
    normed = (xhat * gain[...]).astype(bf16)
    normed_t = normed.T
    kv = nn(normed, qkv_weight[:, MODEL_WIDTH:]).astype(bf16)
    arrivals[0].wait()
    qkv_t = nt(qkv_weight_t[...], normed).astype(bf16)
    arrivals[1].wait()
    for pair in range(HEADS // 2):
        arrivals[2 + pair].wait()
        heads = [
            attention_head(2 * pair + side, qkv_t, kv, penalty, bias_blocks.at[pair], d_context_t)
            for side in range(2)
        ]
        context, *d_parts = [jnp.concatenate(both, 0) for both in zip(*heads)]
        context_t[pair * 128 : pair * 128 + 128, :] = context
        d_pair = jnp.concatenate([part.T for part in d_parts], 1)
        for kind in range(3):
            first = kind * MODEL_WIDTH + pair * 128
            d_qkv[:, first : first + 128] = d_pair[:, kind * 128 : kind * 128 + 128]
        first = pair * TOKENS
        grads[first : first + 128, :] = nn(context, cot[...]).astype(bf16)
        grads[first + 128 : first + TOKENS, :] = nn(normed_t, d_pair).astype(bf16)
    keep_context = pltpu.make_async_copy(context_t, context_far, sems.at[0])
    keep_context.start()
    d_xhat = nt(d_qkv[...], qkv_weight[...]) * gain[...]
    d_rolled[...] = (
        inv_std
        * (
            d_xhat
            - jnp.mean(d_xhat, -1, keepdims=True)
            - xhat * jnp.mean(d_xhat * xhat, -1, keepdims=True)
        )
    ).astype(bf16)
    keep = pltpu.make_async_copy(d_rolled, kept_far, sems.at[1])
    keep.start()
    keep_context.wait()
    keep.wait()


def place_kernel(
    shift, halo, out_weight, kept_far, context_far, field_grad, update, kept, context_t, sems
):
    copies = [
        pltpu.make_async_copy(kept_far, kept, sems.at[0]),
        pltpu.make_async_copy(context_far, context_t, sems.at[1]),
    ]
    for copy in copies:
        copy.start()
    onehots = source_onehots(shift[0], shift[1], -1)
    for copy in copies:
        copy.wait()
    for t in range(2):
        parts = (
            kept[t * 256 : t * 256 + 256, :],
            halo[t * 128 : t * 128 + 128, :],
            halo[256 + t * 128 : 384 + t * 128, :],
            halo[512 + t * 64 : 576 + t * 64, :],
        )
        field_grad[t * 256 : t * 256 + 256, :] = sum(
            nn(hot, part) for hot, part in zip(onehots, parts)
        ).astype(bf16)
    update[...] = tn(context_t[...], out_weight[...]).astype(bf16)


def finish_kernel(scale, place, *refs):
    mine, other, (weight, gain) = refs[:4], refs[4:8], refs[8:10]
    qkv_far, out_far, gain_grad, qkv_grad, out_grad, sems = refs[10:]
    first_core, bit_one, bit_two = place[0] == 0, place[1] == 1, place[2] == 1
    sides = []
    for shares in (mine, other):
        shares = [share[...].astype(f32) * scale for share in shares]
        shares = [jnp.where(bit_one, shares[k ^ 1], shares[k]) for k in range(4)]
        sides.append([jnp.where(bit_two, shares[k ^ 2], shares[k]) for k in range(4)])
    lower = [jnp.where(first_core, a, b) for a, b in zip(*sides)]
    upper = [jnp.where(first_core, b, a) for a, b in zip(*sides)]
    whole = jnp.concatenate(lower + upper, 0)
    copies = []
    partial = 0.0
    for kind in range(3):
        columns = slice(kind * MODEL_WIDTH, (kind + 1) * MODEL_WIDTH)
        block = jnp.concatenate(
            [
                whole[pair * TOKENS + 128 : (pair + 1) * TOKENS, kind * 128 : kind * 128 + 128]
                for pair in range(3)
            ],
            1,
        )
        qkv_grad[:, columns] = block
        copies.append(
            pltpu.make_async_copy(
                qkv_grad.at[:, columns], qkv_far.at[:, columns], sems.at[kind]
            )
        )
        copies[-1].start()
        product = block * weight[:, columns].astype(f32)
        partial = partial + product[:, :128] + product[:, 128:256] + product[:, 256:]
    for pair in range(3):
        out_grad[pair * 128 : pair * 128 + 128, :] = whole[pair * TOKENS : pair * TOKENS + 128]
    copies.append(pltpu.make_async_copy(out_grad, out_far, sems.at[3]))
    copies[-1].start()
    gain_grad[...] = jnp.sum(partial.T, 0, keepdims=True) / gain[...]
    for copy in copies:
        copy.wait()


def local_call(kernel, shapes, inputs, far_in=0, far_out=0, scratch=(), copies=0, micros=1):
    vmem = pl.BlockSpec(memory_space=pltpu.VMEM)
    smem = pl.BlockSpec(memory_space=pltpu.SMEM)
    far = pl.BlockSpec(memory_space=pltpu.HBM)
    return pl.pallas_call(
        kernel,
        out_shape=[jax.ShapeDtypeStruct(shape, dtype) for shape, dtype in shapes],
        in_specs=[smem if array.dtype == jnp.int32 else vmem for array in inputs[: len(inputs) - far_in]]
        + [far] * far_in,
        out_specs=[vmem] * (len(shapes) - far_out) + [far] * far_out,
        scratch_shapes=[pltpu.VMEM(shape, dtype) for shape, dtype in scratch]
        + [pltpu.SemaphoreType.DMA((copies,))],
        compiler_params=pltpu.CompilerParams(vmem_limit_bytes=32 * 2**20),
        cost_estimate=pl.CostEstimate(
            flops=micros * 10**9, bytes_accessed=10**6, transcendentals=0
        ),
    )(*inputs)


def passed_along(block, axis, distance):
    count = lax.axis_size(axis)
    return lax.ppermute(block, axis, [((i - distance) % count, i) for i in range(count)])


def index_bit(axis, bit):
    return (lax.axis_index(axis) & bit) // bit


def swapped(block, *bits):
    axes = tuple(axis for axis, _ in bits)
    sizes = [lax.axis_size(axis) for axis in axes]
    route = []
    for source in range(math.prod(sizes)):
        rest, places = source, []
        for size in sizes[::-1]:
            rest, place = divmod(rest, size)
            places.append(place)
        target = 0
        for size, place, (_, bit) in zip(sizes, places[::-1], bits):
            target = target * size + (place ^ bit)
        route.append((source, target))
    return lax.ppermute(block, axes, route)


def add_up(*pieces):
    return sum(piece.astype(f32) for piece in pieces).astype(bf16)


def all_sum(block):
    core, one, two = ("sx", 1), ("ta", 1), ("sy", 1)
    rest = [
        (axis, 1 << k)
        for axis in ("ta", "sy")
        for k in range(1, lax.axis_size(axis).bit_length() - 1)
    ]
    half = block.shape[0] // 2
    side = index_bit(*core)
    pick = lambda array, place, size: lax.dynamic_slice_in_dim(array, place * size, size, 0)
    block = add_up(pick(block, side, half), swapped(pick(block, 1 - side, half), core))
    share = half // 4
    mine = 2 * index_bit(*one) + index_bit(*two)
    groups = [[two], [one], [two, one]]
    arrived = [
        swapped(pick(block, mine ^ offset, share), *group)
        for offset, group in zip((1, 2, 3), groups)
    ]
    quarter = add_up(pick(block, mine, share), *arrived)
    for bit in rest:
        quarter = add_up(quarter, swapped(quarter, bit))
    quarters = [quarter] + [swapped(quarter, *group) for group in groups]
    return quarters, [swapped(quarter, core) for quarter in quarters]


def shards(
    state_field,
    outlier_flags,
    window_shift,
    layer_norm_gain,
    qkv_weight,
    out_weight,
    position_bias,
    cotangent,
):
    width = MODEL_WIDTH
    wide = lambda tokens: ((tokens, width), bf16)
    rows = passed_along(state_field[:, :RIM].reshape(-1, width), "sy", -1)
    cols = passed_along(state_field[:, :, :RIM].reshape(-1, width), "sx", -1)
    marks = outlier_flags.astype(bf16)
    row_marks = passed_along(marks[:, :RIM].reshape(2 * RIM, SIDE), "sy", -1)
    col_marks = passed_along(marks[:, :, :RIM].reshape(2 * SIDE, RIM), "sx", -1)
    strips = jnp.pad(
        position_bias.reshape(HEADS, 3, 31, 31), ((0, 0), (0, 0), (0, 1), (0, 1))
    )
    strips = strips.reshape(HEADS, 3, 16, 2, 32).transpose(0, 1, 3, 2, 4).reshape(36, TOKENS)
    cot_rows = cotangent.reshape(TOKENS, width)
    pair_bias = ((6, HALF, HALF), f32)
    *bias_blocks, d_context_t, qkv_weight_t = local_call(
        prepare_kernel,
        [pair_bias] * 3 + [((width, TOKENS), bf16), wide(3 * width)],
        [strips, cot_rows, out_weight, qkv_weight],
        far_out=5,
        scratch=[((3, 6, HALF, HALF), f32), ((width, TOKENS), bf16), wide(3 * width)],
        copies=5,
        micros=3,
    )
    corner = passed_along(
        rows.reshape(2 * RIM, SIDE, width)[:, :RIM].reshape(-1, width), "sx", -1
    )
    corner_marks = passed_along(row_marks[:, :RIM], "sx", -1)
    halo = jnp.concatenate([rows, cols, corner], 0)
    all_marks = jnp.concatenate(
        [
            jnp.pad(m, ((0, 0), (0, 128 - m.shape[1])))
            for m in (marks.reshape(2 * SIDE, SIDE), row_marks, col_marks, corner_marks)
        ],
        0,
    )
    gain = layer_norm_gain.reshape(1, width)
    grads, d_rolled, kept, context_t = local_call(
        main_kernel,
        [wide(3 * TOKENS), wide(TOKENS), wide(TOKENS), ((width, TOKENS), bf16)],
        [
            window_shift,
            state_field.reshape(TOKENS, width),
            halo,
            all_marks,
            gain,
            qkv_weight,
            cot_rows,
            qkv_weight_t,
            d_context_t,
            *bias_blocks,
        ],
        far_in=5,
        far_out=2,
        scratch=[
            ((TOKENS, TOKENS), f32),
            wide(3 * width),
            ((width, TOKENS), bf16),
            ((3, 6, HALF, HALF), f32),
            ((width, TOKENS), bf16),
            ((TOKENS, 3 * width), bf16),
        ],
        copies=5,
        micros=12,
    )
    grid = d_rolled.reshape(2, SIDE, SIDE, width)
    below = passed_along(grid[:, RIM:].reshape(-1, width), "sy", 1)
    beside = passed_along(grid[:, :, RIM:].reshape(-1, width), "sx", 1)
    across = passed_along(
        below.reshape(2 * RIM, SIDE, width)[:, RIM:].reshape(-1, width), "sx", 1
    )
    field_grad, update = local_call(
        place_kernel,
        [wide(TOKENS), wide(TOKENS)],
        [
            window_shift,
            jnp.concatenate([below, beside, across], 0),
            out_weight,
            kept,
            context_t,
        ],
        far_in=2,
        scratch=[wide(TOKENS), ((width, TOKENS), bf16)],
        copies=2,
        micros=2,
    )
    quarters, others = all_sum(grads)
    tiles = lax.axis_size("sy") * lax.axis_size("sx") * lax.axis_size("ta")
    place = jnp.stack([index_bit("sx", 1), index_bit("sy", 1), index_bit("ta", 1)])
    gain_grad, qkv_grad, out_grad = finish_call(
        1.0 / tiles, [place.astype(jnp.int32), *quarters, *others, qkv_weight, gain]
    )
    shape = state_field.shape
    return (
        update.reshape(shape),
        field_grad.reshape(shape),
        qkv_grad,
        out_grad,
        gain_grad.reshape(width),
    )


def finish_call(scale, inputs):
    width = MODEL_WIDTH

    def kernel(*refs):
        gain_grad, qkv_far, out_far, *scratch = refs[len(inputs) :]
        finish_kernel(scale, *refs[: len(inputs)], qkv_far, out_far, gain_grad, *scratch)

    return local_call(
        kernel,
        [((1, width), f32), ((width, 3 * width), f32), ((width, width), f32)],
        inputs,
        far_out=2,
        scratch=[((width, 3 * width), f32), ((width, width), f32)],
        copies=4,
    )


def solution(mesh):
    in_specs = (
        P(("groups", "ta"), "sy", "sx", None),
        P(("groups", "ta"), "sy", "sx"),
        P(),
        P(),
        P(),
        P(),
        P(),
        P(("groups", "ta"), "sy", "sx", None),
    )
    out_specs = (
        P(("groups", "ta"), "sy", "sx", None),
        P(("groups", "ta"), "sy", "sx", None),
        P("groups", None),
        P("groups", None),
        P("groups"),
    )
    return jax.shard_map(shards, mesh=mesh, in_specs=in_specs, out_specs=out_specs, check_vma=False)
```

```python
import functools
import math

import jax
import jax.numpy as jnp
from jax import lax
from jax.experimental import pallas as pl
from jax.experimental.pallas import tpu as pltpu
from jax.sharding import PartitionSpec as P

MODEL_WIDTH = 384
HEADS = 6
HEAD_WIDTH = 64
RIM = 8
SIDE = 16
TOKENS = 512
HALF = 256
EPS = 1e-05
LOG2E = math.log2(math.e)

bf16 = jnp.bfloat16
f32 = jnp.float32


def nn(a, b):
    return lax.dot_general(a, b, (((1,), (0,)), ((), ())), preferred_element_type=f32)


def nt(a, b):
    return lax.dot_general(a, b, (((1,), (1,)), ((), ())), preferred_element_type=f32)


def tn(a, b):
    return lax.dot_general(a, b, (((0,), (0,)), ((), ())), preferred_element_type=f32)


def iota(shape, dim):
    return lax.broadcasted_iota(jnp.int32, shape, dim)


def prepare_kernel(strips, cot, out_weight, qkv_weight, *refs):
    outs, (bias_blocks, d_context_t, qkv_weight_t), sems = refs[:5], refs[5:8], refs[8]
    parts = [bias_blocks.at[k] for k in range(3)] + [d_context_t, qkv_weight_t]
    copies = [pltpu.make_async_copy(part, outs[k], sems.at[k]) for k, part in enumerate(parts)]
    qkv_weight_t[...] = qkv_weight[...].T
    copies[4].start()
    d_context_t[...] = nt(out_weight[...], cot[...]).astype(bf16)
    copies[3].start()
    plain = strips[...] * LOG2E
    high = plain.astype(bf16)
    rest = plain - high.astype(f32)
    middle = rest.astype(bf16)
    low = (rest - middle.astype(f32)).astype(bf16)
    turn = iota((TOKENS, TOKENS), 0) + iota((TOKENS, TOKENS), 1) == TOKENS - 2
    turn = turn.astype(f32).astype(bf16)
    turned = nn(high, turn) + nn(middle, turn) + nn(low, turn)
    lane = iota((SIDE, TOKENS), 1)
    for entry in range(HEADS * 3):
        head, frame = divmod(entry, 3)
        first = 2 * (head * 3 + 2 - frame)
        even = jnp.broadcast_to(turned[first : first + 1, :], (SIDE, TOKENS))
        odd = jnp.broadcast_to(turned[first + 1 : first + 2, :], (SIDE, TOKENS))
        even = pltpu.roll(even, TOKENS - 15, 1, stride=1, stride_axis=0)
        odd = pltpu.roll(odd, TOKENS - 31, 1, stride=1, stride_axis=0)
        rows = jnp.where(lane % 32 < 16, even, odd)
        for row in range(SIDE):
            start = (15 - row) * SIDE
            bias_blocks[head // 2, entry % 6, row * SIDE : (row + 1) * SIDE, :] = rows[
                :, start : start + HALF
            ]
        if entry % 6 == 5:
            copies[head // 2].start()
    for copy in copies:
        copy.wait()


def source_onehots(row_shift, col_shift, sign):
    token = iota((HALF, 1), 0)
    row = token // SIDE + sign * row_shift
    col = token % SIDE + sign * col_shift
    if sign > 0:
        row_out, col_out = row >= SIDE, col >= SIDE
        near_row, near_col = row - SIDE, col - SIDE
    else:
        row_out, col_out = row < 0, col < 0
        near_row, near_col = row + RIM, col + RIM
    inner = jnp.where(row_out | col_out, -1, row * SIDE + col)
    rows = jnp.where(row_out & ~col_out, near_row * SIDE + col, -1)
    cols = jnp.where(col_out & ~row_out, row * RIM + near_col, -1)
    corner = jnp.where(row_out & col_out, near_row * RIM + near_col, -1)
    return [
        (iota((HALF, count), 1) == place).astype(f32).astype(bf16)
        for place, count in ((inner, HALF), (rows, 128), (cols, 128), (corner, 64))
    ]


def flag_strip(flags, first, count, width):
    total = count * width
    repeat = (iota((width, total), 1) % width == iota((width, total), 0)).astype(f32).astype(bf16)
    spread = nn(flags[first : first + count, :], repeat)
    keep = iota((count, total), 1) // width == iota((count, total), 0)
    strip = jnp.sum(jnp.where(keep, spread, 0.0), 0, keepdims=True)
    return jnp.broadcast_to(strip, (128, total)).astype(bf16)


def layer_norm(rolled):
    centred = rolled - jnp.mean(rolled, -1, keepdims=True)
    inv_std = lax.rsqrt(jnp.mean(centred * centred, -1, keepdims=True) + EPS)
    return centred * inv_std, inv_std


def attention_head(head, qkv_t, kv, penalty, bias_blocks, d_context_t):
    pair, side = divmod(head, 2)
    at = head * HEAD_WIDTH
    scale = LOG2E * HEAD_WIDTH ** (-0.5)
    zeros = jnp.zeros((HEAD_WIDTH, TOKENS), bf16)
    key_pair = kv[:, pair * 128 : pair * 128 + 128]
    value_pair = kv[:, MODEL_WIDTH + pair * 128 : MODEL_WIDTH + pair * 128 + 128]
    q_t = qkv_t[at : at + HEAD_WIDTH, :]
    k_t = qkv_t[MODEL_WIDTH + at : MODEL_WIDTH + at + HEAD_WIDTH, :]
    v_t = qkv_t[2 * MODEL_WIDTH + at : 2 * MODEL_WIDTH + at + HEAD_WIDTH, :]
    d_t = d_context_t[at : at + HEAD_WIDTH, :]
    d_eighth = d_t * 0.125
    q_wide = jnp.concatenate([q_t, zeros] if side == 0 else [zeros, q_t], 0)
    d_wide = jnp.concatenate([d_eighth, zeros] if side == 0 else [zeros, d_eighth], 0)
    context_parts = []
    dq_parts = []
    dk_parts = [0.0, 0.0]
    dv_parts = [0.0, 0.0]
    for b in range(2):
        lanes = slice(b * HALF, (b + 1) * HALF)
        scores = nn(key_pair, q_wide[:, lanes])
        d_probs = nn(value_pair, d_wide[:, lanes])
        halves = [slice(a * HALF, (a + 1) * HALF) for a in range(2)]
        s = [
            scores[halves[a]] * scale
            + bias_blocks[side * 3 + b - a + 1]
            + penalty[halves[a], lanes]
            for a in range(2)
        ]
        top = jnp.maximum(jnp.max(s[0], 0, keepdims=True), jnp.max(s[1], 0, keepdims=True))
        e = [jnp.exp2(s[a] - top) for a in range(2)]
        total = jnp.sum(e[0], 0, keepdims=True) + jnp.sum(e[1], 0, keepdims=True)
        inverse = 1.0 / total
        p = [e[a] * inverse for a in range(2)]
        pb = [p[a].astype(bf16) for a in range(2)]
        context_parts.append(nn(v_t[:, :HALF], pb[0]) + nn(v_t[:, HALF:], pb[1]))
        dp = [d_probs[halves[a]] for a in range(2)]
        delta = jnp.sum(p[0] * dp[0], 0, keepdims=True) + jnp.sum(p[1] * dp[1], 0, keepdims=True)
        ds = [(p[a] * (dp[a] - delta)).astype(bf16) for a in range(2)]
        dq_parts.append(nn(k_t[:, :HALF], ds[0]) + nn(k_t[:, HALF:], ds[1]))
        for a in range(2):
            dk_parts[a] = dk_parts[a] + nt(q_t[:, lanes], ds[a])
            dv_parts[a] = dv_parts[a] + nt(d_t[:, lanes], pb[a])
    return [
        jnp.concatenate(parts, 1).astype(bf16)
        for parts in (context_parts, dq_parts, dk_parts, dv_parts)
    ]


def main_kernel(
    shift,
    inner,
    halo,
    flags,
    gain,
    core,
    weight_far,
    weight_t_far,
    d_context_far,
    bias0_far,
    cot_far,
    bias1_far,
    bias2_far,
    keep_far,
    send_far,
    d_rolled_far,
    context_far,
    penalty,
    qkv_weight,
    qkv_weight_t,
    d_context_t,
    bias_blocks,
    cot,
    context_t,
    d_qkv,
    grads,
    d_rolled,
    sems,
):
    sources = (
        weight_far, weight_t_far, d_context_far, bias0_far, cot_far, bias1_far, bias2_far
    )
    places = [qkv_weight, qkv_weight_t, d_context_t, bias_blocks.at[0], cot]
    places += [bias_blocks.at[1], bias_blocks.at[2]]
    arrivals = [
        pltpu.make_async_copy(source, place, sems.at[k])
        for k, (source, place) in enumerate(zip(sources, places))
    ]
    for copy in arrivals:
        copy.start()
    onehots = source_onehots(shift[0], shift[1], 1)
    rolled = []
    on_diagonal = iota((HALF, HALF), 0) == iota((HALF, HALF), 1)
    for t in range(2):
        parts = (
            inner[t * 256 : t * 256 + 256, :],
            halo[t * 128 : t * 128 + 128, :],
            halo[256 + t * 128 : 384 + t * 128, :],
            halo[512 + t * 64 : 576 + t * 64, :],
        )
        rolled.append(sum(nn(hot, part) for hot, part in zip(onehots, parts)))
        strips = (
            flag_strip(flags[:32, :16], t * 16, 16, 16),
            flag_strip(flags[32:48, :16], t * 8, 8, 16),
            flag_strip(flags[48:80, :8], t * 16, 16, 8),
            flag_strip(flags[80:96, :8], t * 8, 8, 8),
        )
        marks = sum(nt(hot, strip) for hot, strip in zip(onehots, strips))
        column = jnp.where(marks > 0.5, -1e30, 0.0)
        wide = jnp.concatenate([column, column], 1)
        own = jnp.where(on_diagonal, 0.0, wide)
        penalty[t * HALF : (t + 1) * HALF, t * HALF : (t + 1) * HALF] = own
        penalty[t * HALF : (t + 1) * HALF, (1 - t) * HALF : (2 - t) * HALF] = wide
    xhat, inv_std = layer_norm(jnp.concatenate(rolled, 0))
    normed = (xhat * gain[...]).astype(bf16)
    normed_t = normed.T
    arrivals[0].wait()
    kv = nn(normed, qkv_weight[:, MODEL_WIDTH:]).astype(bf16)
    arrivals[1].wait()
    qkv_t = nt(qkv_weight_t[...], normed).astype(bf16)
    arrivals[2].wait()
    for pair in range(HEADS // 2):
        arrivals[(3, 5, 6)[pair]].wait()
        heads = [
            attention_head(2 * pair + side, qkv_t, kv, penalty, bias_blocks.at[pair], d_context_t)
            for side in range(2)
        ]
        context, *d_parts = [jnp.concatenate(both, 0) for both in zip(*heads)]
        context_t[pair * 128 : pair * 128 + 128, :] = context
        d_pair = jnp.concatenate([part.T for part in d_parts], 1)
        for kind in range(3):
            first = kind * MODEL_WIDTH + pair * 128
            d_qkv[:, first : first + 128] = d_pair[:, kind * 128 : kind * 128 + 128]
        first = pair * TOKENS
        if pair == 0:
            arrivals[4].wait()
        grads[first : first + 128, :] = nn(context, cot[...]).astype(bf16)
        grads[first + 128 : first + TOKENS, :] = nn(normed_t, d_pair).astype(bf16)
        for block in (2 * pair, 2 * pair + 1):
            to_half(grads, block, core[0], keep_far, send_far, sems)
    keep_context = pltpu.make_async_copy(context_t, context_far, sems.at[0])
    keep_context.start()
    d_xhat = nt(d_qkv[...], qkv_weight[...]) * gain[...]
    d_rolled[...] = (
        inv_std
        * (
            d_xhat
            - jnp.mean(d_xhat, -1, keepdims=True)
            - xhat * jnp.mean(d_xhat * xhat, -1, keepdims=True)
        )
    ).astype(bf16)
    keep = pltpu.make_async_copy(d_rolled, d_rolled_far, sems.at[1])
    keep.start()
    for block in range(6):
        source, target = half_block(grads, block, keep_far)
        pltpu.make_async_copy(source, target, sems.at[7 + block]).wait()
    keep_context.wait()
    keep.wait()


def half_block(grads, block, half):
    place = block % 3 * HALF
    return grads.at[pl.ds(block * HALF, HALF), :], half.at[pl.ds(place, HALF), :]


def to_half(grads, block, core, keep_far, send_far, sems):
    for half, side in ((keep_far, block // 3), (send_far, 1 - block // 3)):

        @pl.when(core == side)
        def _():
            source, target = half_block(grads, block, half)
            pltpu.make_async_copy(source, target, sems.at[7 + block]).start()


def place_kernel(
    shift,
    halo,
    out_weight,
    kept_far,
    context_far,
    field_grad,
    update,
    kept,
    context_t,
    sems,
):
    copies = [
        pltpu.make_async_copy(kept_far, kept, sems.at[0]),
        pltpu.make_async_copy(context_far, context_t, sems.at[1]),
    ]
    for copy in copies:
        copy.start()
    onehots = source_onehots(shift[0], shift[1], -1)
    for copy in copies:
        copy.wait()
    for t in range(2):
        parts = (
            kept[t * 256 : t * 256 + 256, :],
            halo[t * 128 : t * 128 + 128, :],
            halo[256 + t * 128 : 384 + t * 128, :],
            halo[512 + t * 64 : 576 + t * 64, :],
        )
        field_grad[t * 256 : t * 256 + 256, :] = sum(
            nn(hot, part) for hot, part in zip(onehots, parts)
        ).astype(bf16)
    update[...] = tn(context_t[...], out_weight[...]).astype(bf16)


def finish_kernel(scale, place, *refs):
    mine, other, (weight, gain) = refs[:4], refs[4:8], refs[8:10]
    gain_grad, qkv_far, out_far, shares, qkv_grad, out_grad, sems = refs[10:]
    for side, group in ((place[0], mine), (1 - place[0], other)):
        for offset in range(4):
            shares[side * 4 + (offset ^ place[1])] = group[offset][...]
    whole = shares[...].reshape(3 * TOKENS, MODEL_WIDTH).astype(f32) * scale
    copies = []
    partial = 0.0
    for kind in range(3):
        columns = slice(kind * MODEL_WIDTH, (kind + 1) * MODEL_WIDTH)
        block = jnp.concatenate(
            [
                whole[pair * TOKENS + 128 : (pair + 1) * TOKENS, kind * 128 : kind * 128 + 128]
                for pair in range(3)
            ],
            1,
        )
        qkv_grad[:, columns] = block
        copies.append(
            pltpu.make_async_copy(
                qkv_grad.at[:, columns], qkv_far.at[:, columns], sems.at[kind]
            )
        )
        copies[-1].start()
        product = block * weight[:, columns].astype(f32)
        partial = partial + product[:, :128] + product[:, 128:256] + product[:, 256:]
    for pair in range(3):
        out_grad[pair * 128 : pair * 128 + 128, :] = whole[pair * TOKENS : pair * TOKENS + 128]
    copies.append(pltpu.make_async_copy(out_grad, out_far, sems.at[3]))
    copies[-1].start()
    gain_grad[...] = (jnp.sum(partial.T, 0, keepdims=True) / gain[...]).reshape(MODEL_WIDTH)
    for copy in copies:
        copy.wait()


def local_call(
    kernel, shapes, inputs, far_in=0, far_out=0, scratch=(), copies=0, micros=1, limit=24
):
    vmem = pl.BlockSpec(memory_space=pltpu.VMEM)
    smem = pl.BlockSpec(memory_space=pltpu.SMEM)
    far = pl.BlockSpec(memory_space=pl.ANY)
    near = inputs[: len(inputs) - far_in]
    return pl.pallas_call(
        kernel,
        out_shape=[jax.ShapeDtypeStruct(shape, dtype) for shape, dtype in shapes],
        in_specs=[smem if array.dtype == jnp.int32 else vmem for array in near] + [far] * far_in,
        out_specs=[vmem] * (len(shapes) - far_out) + [far] * far_out,
        scratch_shapes=[pltpu.VMEM(shape, dtype) for shape, dtype in scratch]
        + [pltpu.SemaphoreType.DMA((copies,))],
        compiler_params=pltpu.CompilerParams(vmem_limit_bytes=limit * 2**20),
        cost_estimate=pl.CostEstimate(
            flops=micros * 10**9, bytes_accessed=10**6, transcendentals=0
        ),
    )(*inputs)


def passed_along(block, axis, distance):
    count = lax.axis_size(axis)
    return lax.ppermute(block, axis, [((i - distance) % count, i) for i in range(count)])


CORE = ("sx", 1)
GROUPS = ([("sy", 1)], [("ta", 1)], [("sy", 1), ("ta", 1)])


def index_bit(axis, bit):
    return (lax.axis_index(axis) & bit) // bit


def swapped(block, *bits):
    axes = tuple(axis for axis, _ in bits)
    sizes = [lax.axis_size(axis) for axis in axes]
    route = []
    for source in range(math.prod(sizes)):
        rest, places = source, []
        for size in sizes[::-1]:
            rest, place = divmod(rest, size)
            places.append(place)
        target = 0
        for size, place, (_, bit) in zip(sizes, places[::-1], bits):
            target = target * size + (place ^ bit)
        route.append((source, target))
    return lax.ppermute(block, axes, route)


def add_up(*pieces):
    return sum(piece.astype(f32) for piece in pieces).astype(bf16)


def sum_quarter(keep, send):
    block = add_up(keep, swapped(send, CORE))
    share = block.shape[0] // 4
    mine = quarter_index()
    pick = lambda place: lax.dynamic_slice_in_dim(block, place * share, share, 0)
    arrived = [swapped(pick(mine ^ k), *GROUPS[k - 1]) for k in (1, 2, 3)]
    return add_up(pick(mine), *arrived)


def sum_rest(quarter):
    rest = [
        (axis, 1 << k)
        for axis in ("ta", "sy")
        for k in range(1, lax.axis_size(axis).bit_length() - 1)
    ]
    for bit in rest:
        quarter = add_up(quarter, swapped(quarter, bit))
    return quarter


def quarter_index():
    return 2 * index_bit("ta", 1) + index_bit("sy", 1)


def shards(
    state_field,
    outlier_flags,
    window_shift,
    layer_norm_gain,
    qkv_weight,
    out_weight,
    position_bias,
    cotangent,
):
    width = MODEL_WIDTH
    wide = lambda tokens: ((tokens, width), bf16)
    first_rows = state_field[:, :RIM].reshape(-1, width)
    rows = passed_along(first_rows, "sy", -1)
    marks = outlier_flags.astype(bf16) + first_rows[0, 0] * 0
    row_marks = passed_along(marks[:, :RIM].reshape(2 * RIM, SIDE), "sy", -1)
    cols = passed_along(state_field[:, :, :RIM].reshape(-1, width), "sx", -1)
    col_marks = passed_along(marks[:, :, :RIM].reshape(2 * SIDE, RIM), "sx", -1)
    strips = jnp.pad(
        position_bias.reshape(HEADS, 3, 31, 31), ((0, 0), (0, 0), (0, 1), (0, 1))
    )
    strips = strips.reshape(HEADS, 3, 16, 2, 32).transpose(0, 1, 3, 2, 4).reshape(36, TOKENS)
    cot_rows = cotangent.reshape(TOKENS, width)
    pair_bias = ((6, HALF, HALF), f32)
    *bias_blocks, d_context_t, qkv_weight_t = local_call(
        prepare_kernel,
        [pair_bias] * 3 + [((width, TOKENS), bf16), wide(3 * width)],
        [strips, cot_rows, out_weight, qkv_weight],
        far_out=5,
        scratch=[((3, 6, HALF, HALF), f32), ((width, TOKENS), bf16), wide(3 * width)],
        copies=5,
        micros=3,
        limit=60,
    )
    corner = passed_along(
        rows.reshape(2 * RIM, SIDE, width)[:, :RIM].reshape(-1, width), "sx", -1
    )
    corner_marks = passed_along(row_marks[:, :RIM], "sx", -1)
    halo = jnp.concatenate([rows, cols, corner], 0)
    all_marks = jnp.concatenate(
        [
            jnp.pad(m, ((0, 0), (0, 128 - m.shape[1])))
            for m in (marks.reshape(2 * SIDE, SIDE), row_marks, col_marks, corner_marks)
        ],
        0,
    )
    gain = layer_norm_gain.reshape(1, width)
    core = index_bit(*CORE).astype(jnp.int32).reshape(1)
    keep, send, d_rolled, context_t = local_call(
        main_kernel,
        [wide(2 * width)] * 2 + [wide(TOKENS), ((width, TOKENS), bf16)],
        [
            window_shift,
            state_field.reshape(TOKENS, width),
            halo,
            all_marks,
            gain,
            core,
            qkv_weight,
            qkv_weight_t,
            d_context_t,
            bias_blocks[0],
            cot_rows,
            bias_blocks[1],
            bias_blocks[2],
        ],
        far_in=7,
        far_out=4,
        scratch=[
            ((TOKENS, TOKENS), f32),
            ((width, 3 * width), bf16),
            wide(3 * width),
            ((width, TOKENS), bf16),
            ((3, 6, HALF, HALF), f32),
            wide(TOKENS),
            ((width, TOKENS), bf16),
            ((TOKENS, 3 * width), bf16),
            wide(3 * TOKENS),
            wide(TOKENS),
        ],
        copies=13,
        micros=12,
        limit=60,
    )
    grid = d_rolled.reshape(2, SIDE, SIDE, width)
    below = passed_along(grid[:, RIM:].reshape(-1, width), "sy", 1)
    beside = passed_along(grid[:, :, RIM:].reshape(-1, width), "sx", 1)
    across = passed_along(
        below.reshape(2 * RIM, SIDE, width)[:, RIM:].reshape(-1, width), "sx", 1
    )
    quarter = sum_quarter(keep, send)
    field_grad, update = local_call(
        place_kernel,
        [wide(TOKENS), wide(TOKENS)],
        [
            window_shift,
            jnp.concatenate([below, beside, across], 0),
            out_weight,
            d_rolled,
            context_t,
        ],
        far_in=2,
        scratch=[wide(TOKENS), ((width, TOKENS), bf16)],
        copies=2,
        micros=2,
    )
    quarter = sum_rest(quarter)
    quarters = [quarter] + [swapped(quarter, *group) for group in GROUPS]
    others = [swapped(piece, CORE) for piece in quarters]
    tiles = lax.axis_size("sy") * lax.axis_size("sx") * lax.axis_size("ta")
    place = jnp.stack([index_bit(*CORE), quarter_index()]).astype(jnp.int32)
    gain_grad, qkv_grad, out_grad = finish_call(
        1.0 / tiles, [place, *quarters, *others, qkv_weight, gain]
    )
    shape = state_field.shape
    return (
        update.reshape(shape),
        field_grad.reshape(shape),
        qkv_grad,
        out_grad,
        gain_grad,
    )


def finish_call(scale, inputs):
    width = MODEL_WIDTH
    return local_call(
        functools.partial(finish_kernel, scale),
        [((width,), f32), ((width, 3 * width), f32), ((width, width), f32)],
        inputs,
        far_out=2,
        scratch=[
            ((8, width // 2, width), bf16),
            ((width, 3 * width), f32),
            ((width, width), f32),
        ],
        copies=4,
    )


def solution(mesh):
    in_specs = (
        P(("groups", "ta"), "sy", "sx", None),
        P(("groups", "ta"), "sy", "sx"),
        P(),
        P(),
        P(),
        P(),
        P(),
        P(("groups", "ta"), "sy", "sx", None),
    )
    out_specs = (
        P(("groups", "ta"), "sy", "sx", None),
        P(("groups", "ta"), "sy", "sx", None),
        P("groups", None),
        P("groups", None),
        P("groups"),
    )
    return jax.shard_map(shards, mesh=mesh, in_specs=in_specs, out_specs=out_specs, check_vma=False)
```

```python
import functools
import math

import jax
import jax.numpy as jnp
from jax import lax
from jax.experimental import pallas as pl
from jax.experimental.pallas import tpu as pltpu
from jax.sharding import PartitionSpec as P

MODEL_WIDTH = 384
HEADS = 6
HEAD_WIDTH = 64
RIM = 8
SIDE = 16
TOKENS = 512
HALF = 256
EPS = 1e-05
LOG2E = math.log2(math.e)

bf16 = jnp.bfloat16
f32 = jnp.float32


def nn(a, b):
    return lax.dot_general(a, b, (((1,), (0,)), ((), ())), preferred_element_type=f32)


def nt(a, b):
    return lax.dot_general(a, b, (((1,), (1,)), ((), ())), preferred_element_type=f32)


def tn(a, b):
    return lax.dot_general(a, b, (((0,), (0,)), ((), ())), preferred_element_type=f32)


def iota(shape, dim):
    return lax.broadcasted_iota(jnp.int32, shape, dim)


def prepare_kernel(
    shift,
    strips,
    cot,
    out_weight,
    qkv_weight,
    inner_flags,
    row_flags,
    col_flags,
    corner_flags,
    nothing,
    *refs,
):
    outs, (bias_blocks, d_context_t, qkv_weight_t, penalty), sems = refs[:6], refs[6:10], refs[10]
    nothing[...] = jnp.zeros_like(nothing)
    parts = [bias_blocks.at[k] for k in range(3)] + [d_context_t, qkv_weight_t, penalty]
    copies = [pltpu.make_async_copy(part, outs[k], sems.at[k]) for k, part in enumerate(parts)]
    qkv_weight_t[...] = qkv_weight[...].T
    copies[4].start()
    d_context_t[...] = nt(out_weight[...], cot[...]).astype(bf16)
    copies[3].start()
    plain = strips[...] * LOG2E
    high = plain.astype(bf16)
    rest = plain - high.astype(f32)
    middle = rest.astype(bf16)
    low = (rest - middle.astype(f32)).astype(bf16)
    turn = iota((TOKENS, TOKENS), 0) + iota((TOKENS, TOKENS), 1) == TOKENS - 2
    turn = turn.astype(f32).astype(bf16)
    turned = nn(high, turn) + nn(middle, turn) + nn(low, turn)
    lane = iota((SIDE, TOKENS), 1)
    for entry in range(HEADS * 3):
        head, frame = divmod(entry, 3)
        first = 2 * (head * 3 + 2 - frame)
        even = jnp.broadcast_to(turned[first : first + 1, :], (SIDE, TOKENS))
        odd = jnp.broadcast_to(turned[first + 1 : first + 2, :], (SIDE, TOKENS))
        even = pltpu.roll(even, TOKENS - 15, 1, stride=1, stride_axis=0)
        odd = pltpu.roll(odd, TOKENS - 31, 1, stride=1, stride_axis=0)
        rows = jnp.where(lane % 32 < 16, even, odd)
        for row in range(SIDE):
            start = (15 - row) * SIDE
            bias_blocks[head // 2, entry % 6, row * SIDE : (row + 1) * SIDE, :] = rows[
                :, start : start + HALF
            ]
        if entry % 6 == 5:
            copies[head // 2].start()
    onehots = source_onehots(shift[0], shift[1], 1)
    on_diagonal = iota((HALF, HALF), 0) == iota((HALF, HALF), 1)
    for t in range(2):
        parts = (
            flag_strip(inner_flags[t], SIDE),
            flag_strip(row_flags[t], RIM),
            flag_strip(col_flags[t], SIDE),
            flag_strip(corner_flags[t], RIM, RIM),
        )
        marks = sum(nt(hot, strip) for hot, strip in zip(onehots, parts))
        column = jnp.where(marks > 0.5, -1e30, 0.0)
        wide = jnp.concatenate([column, column], 1)
        own = jnp.where(on_diagonal, 0.0, wide)
        penalty[t * HALF : (t + 1) * HALF, t * HALF : (t + 1) * HALF] = own
        penalty[t * HALF : (t + 1) * HALF, (1 - t) * HALF : (2 - t) * HALF] = wide
    copies[5].start()
    for copy in copies:
        copy.wait()


def source_onehots(row_shift, col_shift, sign):
    token = iota((HALF, 1), 0)
    row = token // SIDE + sign * row_shift
    col = token % SIDE + sign * col_shift
    if sign > 0:
        row_out, col_out = row >= SIDE, col >= SIDE
        near_row, near_col, span = row - SIDE, col - SIDE, SIDE
    else:
        row_out, col_out = row < 0, col < 0
        near_row, near_col, span = row + RIM, col + RIM, RIM
    inner = jnp.where(row_out | col_out, -1, row * SIDE + col)
    rows = jnp.where(row_out & ~col_out, near_row * SIDE + col, -1)
    cols = jnp.where(col_out & ~row_out, row * span + near_col, -1)
    corner = jnp.where(row_out & col_out, near_row * RIM + near_col, -1)
    return [
        (iota((HALF, count), 1) == place).astype(f32).astype(bf16)
        for place, count in ((inner, HALF), (rows, 128), (cols, SIDE * span), (corner, 64))
    ]


def flag_strip(flags, count, span=SIDE):
    total = count * span
    repeat = (iota((SIDE, total), 1) % span == iota((SIDE, total), 0)).astype(f32).astype(bf16)
    spread = nn(flags[:count, :].astype(f32).astype(bf16), repeat)
    keep = iota((count, total), 1) // span == iota((count, total), 0)
    strip = jnp.sum(jnp.where(keep, spread, 0.0), 0, keepdims=True)
    return jnp.broadcast_to(strip, (128, total)).astype(bf16)


def layer_norm(rolled):
    centred = rolled - jnp.mean(rolled, -1, keepdims=True)
    inv_std = lax.rsqrt(jnp.mean(centred * centred, -1, keepdims=True) + EPS)
    return centred * inv_std, inv_std


def attention_head(head, qkv_t, kv, penalty, bias_blocks, d_context_t):
    pair, side = divmod(head, 2)
    at = head * HEAD_WIDTH
    scale = LOG2E * HEAD_WIDTH ** (-0.5)
    zeros = jnp.zeros((HEAD_WIDTH, TOKENS), bf16)
    key_pair = kv[:, pair * 128 : pair * 128 + 128]
    value_pair = kv[:, MODEL_WIDTH + pair * 128 : MODEL_WIDTH + pair * 128 + 128]
    q_t = qkv_t[at : at + HEAD_WIDTH, :]
    k_t = qkv_t[MODEL_WIDTH + at : MODEL_WIDTH + at + HEAD_WIDTH, :]
    v_t = qkv_t[2 * MODEL_WIDTH + at : 2 * MODEL_WIDTH + at + HEAD_WIDTH, :]
    d_t = d_context_t[at : at + HEAD_WIDTH, :]
    d_eighth = d_t * 0.125
    q_wide = jnp.concatenate([q_t, zeros] if side == 0 else [zeros, q_t], 0)
    d_wide = jnp.concatenate([d_eighth, zeros] if side == 0 else [zeros, d_eighth], 0)
    context_parts = []
    dq_parts = []
    dk_parts = [0.0, 0.0]
    dv_parts = [0.0, 0.0]
    for b in range(2):
        lanes = slice(b * HALF, (b + 1) * HALF)
        scores = nn(key_pair, q_wide[:, lanes])
        d_probs = nn(value_pair, d_wide[:, lanes])
        halves = [slice(a * HALF, (a + 1) * HALF) for a in range(2)]
        s = [
            scores[halves[a]] * scale
            + bias_blocks[side * 3 + b - a + 1]
            + penalty[halves[a], lanes]
            for a in range(2)
        ]
        top = jnp.maximum(jnp.max(s[0], 0, keepdims=True), jnp.max(s[1], 0, keepdims=True))
        e = [jnp.exp2(s[a] - top) for a in range(2)]
        total = jnp.sum(e[0], 0, keepdims=True) + jnp.sum(e[1], 0, keepdims=True)
        inverse = 1.0 / total
        p = [e[a] * inverse for a in range(2)]
        pb = [p[a].astype(bf16) for a in range(2)]
        context_parts.append(nn(v_t[:, :HALF], pb[0]) + nn(v_t[:, HALF:], pb[1]))
        dp = [d_probs[halves[a]] for a in range(2)]
        delta = jnp.sum(p[0] * dp[0], 0, keepdims=True) + jnp.sum(p[1] * dp[1], 0, keepdims=True)
        ds = [(p[a] * (dp[a] - delta)).astype(bf16) for a in range(2)]
        dq_parts.append(nn(k_t[:, :HALF], ds[0]) + nn(k_t[:, HALF:], ds[1]))
        for a in range(2):
            dk_parts[a] = dk_parts[a] + nt(q_t[:, lanes], ds[a])
            dv_parts[a] = dv_parts[a] + nt(d_t[:, lanes], pb[a])
    return [
        jnp.concatenate(parts, 1).astype(bf16)
        for parts in (context_parts, dq_parts, dk_parts, dv_parts)
    ]


def main_kernel(
    shift,
    core,
    gain,
    inner_far,
    rows_far,
    cols_far,
    corner_far,
    weight_far,
    weight_t_far,
    d_context_far,
    bias0_far,
    cot_far,
    bias1_far,
    bias2_far,
    penalty_far,
    keep_far,
    send_far,
    d_rolled_far,
    context_far,
    lower_far,
    right_far,
    penalty,
    inner,
    rows,
    cols,
    corner,
    qkv_weight,
    qkv_weight_t,
    d_context_t,
    bias_blocks,
    cot,
    context_t,
    d_qkv,
    grads,
    d_rolled,
    right,
    sems,
):
    sources = (inner_far, rows_far, cols_far, corner_far, weight_far, weight_t_far)
    sources += (d_context_far, bias0_far, cot_far, bias1_far, bias2_far, penalty_far)
    places = [inner, rows, cols, corner, qkv_weight, qkv_weight_t]
    places += [d_context_t, bias_blocks.at[0], cot, bias_blocks.at[1], bias_blocks.at[2]]
    places.append(penalty)
    arrivals = [
        pltpu.make_async_copy(source, place, sems.at[k])
        for k, (source, place) in enumerate(zip(sources, places))
    ]
    for copy in arrivals:
        copy.start()
    onehots = source_onehots(shift[0], shift[1], 1)
    for copy in arrivals[:4]:
        copy.wait()
    rolled = []
    for t in range(2):
        parts = (
            inner[t * 256 : t * 256 + 256, :],
            rows[t * 128 : t * 128 + 128, :],
            cols[t * 256 : t * 256 + 256, :],
            corner[t * 64 : t * 64 + 64, :],
        )
        rolled.append(sum(nn(hot, part) for hot, part in zip(onehots, parts)))
    xhat, inv_std = layer_norm(jnp.concatenate(rolled, 0))
    gain_row = gain[...].reshape(1, MODEL_WIDTH)
    normed = (xhat * gain_row).astype(bf16)
    normed_t = normed.T
    arrivals[4].wait()
    kv = nn(normed, qkv_weight[:, MODEL_WIDTH:]).astype(bf16)
    arrivals[5].wait()
    qkv_t = nt(qkv_weight_t[...], normed).astype(bf16)
    arrivals[6].wait()
    arrivals[11].wait()
    for pair in range(HEADS // 2):
        arrivals[(7, 9, 10)[pair]].wait()
        heads = [
            attention_head(2 * pair + side, qkv_t, kv, penalty, bias_blocks.at[pair], d_context_t)
            for side in range(2)
        ]
        context, *d_parts = [jnp.concatenate(both, 0) for both in zip(*heads)]
        context_t[pair * 128 : pair * 128 + 128, :] = context
        d_pair = jnp.concatenate([part.T for part in d_parts], 1)
        for kind in range(3):
            first = kind * MODEL_WIDTH + pair * 128
            d_qkv[:, first : first + 128] = d_pair[:, kind * 128 : kind * 128 + 128]
        first = pair * TOKENS
        if pair == 0:
            arrivals[8].wait()
        grads[first : first + 128, :] = nn(context, cot[...]).astype(bf16)
        grads[first + 128 : first + TOKENS, :] = nn(normed_t, d_pair).astype(bf16)
        for block in (2 * pair, 2 * pair + 1):
            to_half(grads, block, core[0], keep_far, send_far, sems)
    keep_context = pltpu.make_async_copy(context_t, context_far, sems.at[0])
    keep_context.start()
    d_xhat = nt(d_qkv[...], qkv_weight[...]) * gain_row
    d_tokens = inv_std * (
        d_xhat
        - jnp.mean(d_xhat, -1, keepdims=True)
        - xhat * jnp.mean(d_xhat * xhat, -1, keepdims=True)
    )
    d_rolled[...] = d_tokens.astype(bf16)
    last_columns = d_tokens.reshape(2 * SIDE, SIDE, MODEL_WIDTH)[:, RIM:, :]
    right[...] = last_columns.reshape(HALF, MODEL_WIDTH).astype(bf16)
    copies = [
        pltpu.make_async_copy(d_rolled, d_rolled_far, sems.at[1]),
        pltpu.make_async_copy(right, right_far, sems.at[2]),
    ]
    for t in range(2):
        source = d_rolled.at[pl.ds(t * HALF + 128, 128), :]
        target = lower_far.at[pl.ds(t * 128, 128), :]
        copies.append(pltpu.make_async_copy(source, target, sems.at[3 + t]))
    for copy in copies:
        copy.start()
    for block in range(6):
        source, target = half_block(grads, block, keep_far)
        pltpu.make_async_copy(source, target, sems.at[12 + block]).wait()
    keep_context.wait()
    for copy in copies:
        copy.wait()


def half_block(grads, block, half):
    place = block % 3 * HALF
    return grads.at[pl.ds(block * HALF, HALF), :], half.at[pl.ds(place, HALF), :]


def to_half(grads, block, core, keep_far, send_far, sems):
    for half, side in ((keep_far, block // 3), (send_far, 1 - block // 3)):

        @pl.when(core == side)
        def _():
            source, target = half_block(grads, block, half)
            pltpu.make_async_copy(source, target, sems.at[12 + block]).start()


def place_kernel(
    shift,
    halo,
    out_weight,
    kept_far,
    context_far,
    field_grad,
    update,
    nothing,
    kept,
    context_t,
    sems,
):
    nothing[...] = jnp.zeros_like(nothing)
    copies = [
        pltpu.make_async_copy(kept_far, kept, sems.at[0]),
        pltpu.make_async_copy(context_far, context_t, sems.at[1]),
    ]
    for copy in copies:
        copy.start()
    onehots = source_onehots(shift[0], shift[1], -1)
    for copy in copies:
        copy.wait()
    for t in range(2):
        parts = (
            kept[t * 256 : t * 256 + 256, :],
            halo[t * 128 : t * 128 + 128, :],
            halo[256 + t * 128 : 384 + t * 128, :],
            halo[512 + t * 64 : 576 + t * 64, :],
        )
        field_grad[t * 256 : t * 256 + 256, :] = sum(
            nn(hot, part) for hot, part in zip(onehots, parts)
        ).astype(bf16)
    update[...] = tn(context_t[...], out_weight[...]).astype(bf16)


def finish_kernel(scale, place, *refs):
    mine, other, (weight, gain) = refs[:4], refs[4:8], refs[8:10]
    gain_grad, qkv_far, out_far, shares, qkv_grad, out_grad, sems = refs[10:]
    for side, group in ((place[0], mine), (1 - place[0], other)):
        for offset in range(4):
            shares[side * 4 + (offset ^ place[1])] = group[offset][...]
    whole = shares[...].reshape(3 * TOKENS, MODEL_WIDTH).astype(f32) * scale
    copies = []
    partial = 0.0
    for kind in range(3):
        columns = slice(kind * MODEL_WIDTH, (kind + 1) * MODEL_WIDTH)
        block = jnp.concatenate(
            [
                whole[pair * TOKENS + 128 : (pair + 1) * TOKENS, kind * 128 : kind * 128 + 128]
                for pair in range(3)
            ],
            1,
        )
        qkv_grad[:, columns] = block
        copies.append(
            pltpu.make_async_copy(
                qkv_grad.at[:, columns], qkv_far.at[:, columns], sems.at[kind]
            )
        )
        copies[-1].start()
        product = block * weight[:, columns].astype(f32)
        partial = partial + product[:, :128] + product[:, 128:256] + product[:, 256:]
    for pair in range(3):
        out_grad[pair * 128 : pair * 128 + 128, :] = whole[pair * TOKENS : pair * TOKENS + 128]
    copies.append(pltpu.make_async_copy(out_grad, out_far, sems.at[3]))
    copies[-1].start()
    gain_row = gain[...].reshape(1, MODEL_WIDTH)
    gain_grad[...] = (jnp.sum(partial.T, 0, keepdims=True) / gain_row).reshape(MODEL_WIDTH)
    for copy in copies:
        copy.wait()


def local_call(
    kernel, shapes, inputs, far_in=0, far_out=0, scratch=(), copies=0, micros=1, limit=24
):
    vmem = pl.BlockSpec(memory_space=pltpu.VMEM)
    smem = pl.BlockSpec(memory_space=pltpu.SMEM)
    far = pl.BlockSpec(memory_space=pl.ANY)
    near = inputs[: len(inputs) - far_in]
    return pl.pallas_call(
        kernel,
        out_shape=[jax.ShapeDtypeStruct(shape, dtype) for shape, dtype in shapes],
        in_specs=[smem if array.dtype == jnp.int32 and array.ndim == 1 else vmem for array in near]
        + [far] * far_in,
        out_specs=[vmem] * (len(shapes) - far_out) + [far] * far_out,
        scratch_shapes=[pltpu.VMEM(shape, dtype) for shape, dtype in scratch]
        + [pltpu.SemaphoreType.DMA((copies,))],
        compiler_params=pltpu.CompilerParams(vmem_limit_bytes=limit * 2**20),
        cost_estimate=pl.CostEstimate(
            flops=micros * 10**9, bytes_accessed=10**6, transcendentals=0
        ),
    )(*inputs)


def passed_along(block, axis, distance):
    count = lax.axis_size(axis)
    return lax.ppermute(block, axis, [((i - distance) % count, i) for i in range(count)])


def passed_across(block, axis, other, distance):
    count, width = lax.axis_size(axis), lax.axis_size(other)
    route = [
        (((i - distance) % count) * width + (j - distance) % width, i * width + j)
        for i in range(count)
        for j in range(width)
    ]
    return lax.ppermute(block, (axis, other), route)


CORE = ("sx", 1)
GROUPS = ([("sy", 1)], [("ta", 1)], [("sy", 1), ("ta", 1)])


def index_bit(axis, bit):
    return (lax.axis_index(axis) & bit) // bit


def swapped(block, *bits):
    axes = tuple(axis for axis, _ in bits)
    sizes = [lax.axis_size(axis) for axis in axes]
    route = []
    for source in range(math.prod(sizes)):
        rest, places = source, []
        for size in sizes[::-1]:
            rest, place = divmod(rest, size)
            places.append(place)
        target = 0
        for size, place, (_, bit) in zip(sizes, places[::-1], bits):
            target = target * size + (place ^ bit)
        route.append((source, target))
    return lax.ppermute(block, axes, route)


def add_up(*pieces):
    return sum(piece.astype(f32) for piece in pieces).astype(bf16)


def sum_quarter(block):
    share = block.shape[0] // 4
    mine = quarter_index()
    pick = lambda place: lax.dynamic_slice_in_dim(block, place * share, share, 0)
    arrived = [swapped(pick(mine ^ k), *GROUPS[k - 1]) for k in (1, 2, 3)]
    return add_up(pick(mine), *arrived)


def sum_rest(quarter, zero):
    rest = [
        (axis, 1 << k)
        for axis in ("ta", "sy")
        for k in range(1, lax.axis_size(axis).bit_length() - 1)
    ]
    for bit in rest:
        quarter = add_up(quarter, swapped(quarter, bit), zero)
    return quarter


def quarter_index():
    return 2 * index_bit("ta", 1) + index_bit("sy", 1)


def shards(
    state_field,
    outlier_flags,
    window_shift,
    layer_norm_gain,
    qkv_weight,
    out_weight,
    position_bias,
    cotangent,
):
    width = MODEL_WIDTH
    wide = lambda tokens: ((tokens, width), bf16)
    rows = passed_along(state_field[:, :RIM].reshape(-1, width), "sy", -1)
    row_flags = passed_along(outlier_flags, "sy", -1)
    cols = passed_along(state_field, "sx", -1)
    col_flags = passed_along(outlier_flags, "sx", -1)
    corner_flags = passed_across(outlier_flags, "sy", "sx", -1)
    strips = jnp.pad(
        position_bias.reshape(HEADS, 3, 31, 31), ((0, 0), (0, 0), (0, 1), (0, 1))
    )
    strips = strips.reshape(HEADS, 3, 16, 2, 32).transpose(0, 1, 3, 2, 4).reshape(36, TOKENS)
    cot_rows = cotangent.reshape(TOKENS, width)
    pair_bias = ((6, HALF, HALF), f32)
    nothing, *bias_blocks, d_context_t, qkv_weight_t, penalty = local_call(
        prepare_kernel,
        [((16, 128), bf16)] + [pair_bias] * 3 + [((width, TOKENS), bf16), wide(3 * width), ((TOKENS, TOKENS), f32)],
        [
            window_shift,
            strips,
            cot_rows,
            out_weight,
            qkv_weight,
            outlier_flags,
            row_flags,
            col_flags,
            corner_flags,
        ],
        far_out=6,
        scratch=[
            ((3, 6, HALF, HALF), f32),
            ((width, TOKENS), bf16),
            wide(3 * width),
            ((TOKENS, TOKENS), f32),
        ],
        copies=6,
        micros=3,
        limit=62,
    )
    corner_message = rows.reshape(2 * RIM, SIDE, width)[:, :RIM] + nothing[0, 0]
    corner = passed_along(corner_message.reshape(-1, width), "sx", -1)
    core = index_bit(*CORE).astype(jnp.int32).reshape(1)
    keep, send, d_rolled, context_t, lower, right = local_call(
        main_kernel,
        [wide(2 * width)] * 2
        + [wide(TOKENS), ((width, TOKENS), bf16), wide(HALF), wide(HALF)],
        [
            window_shift,
            core,
            layer_norm_gain,
            state_field.reshape(TOKENS, width),
            rows,
            cols.reshape(TOKENS, width),
            corner,
            qkv_weight,
            qkv_weight_t,
            d_context_t,
            bias_blocks[0],
            cot_rows,
            bias_blocks[1],
            bias_blocks[2],
            penalty,
        ],
        far_in=12,
        far_out=6,
        scratch=[
            ((TOKENS, TOKENS), f32),
            wide(TOKENS),
            wide(HALF),
            wide(TOKENS),
            wide(128),
            ((width, 3 * width), bf16),
            wide(3 * width),
            ((width, TOKENS), bf16),
            ((3, 6, HALF, HALF), f32),
            wide(TOKENS),
            ((width, TOKENS), bf16),
            ((TOKENS, 3 * width), bf16),
            wide(3 * TOKENS),
            wide(TOKENS),
            wide(HALF),
        ],
        copies=18,
        micros=12,
        limit=62,
    )
    below = passed_along(lower, "sy", 1)
    beside = passed_along(right, "sx", 1)
    block = add_up(keep, swapped(send, CORE))
    across = below.reshape(2 * RIM, SIDE, width)[:, RIM:] + block[0, 0] * 0
    across = passed_along(across.reshape(-1, width), "sx", 1)
    quarter = sum_quarter(block)
    field_grad, update, nothing = local_call(
        place_kernel,
        [wide(TOKENS), wide(TOKENS), ((16, 128), bf16)],
        [
            window_shift,
            jnp.concatenate([below, beside, across], 0),
            out_weight,
            d_rolled,
            context_t,
        ],
        far_in=2,
        scratch=[wide(TOKENS), ((width, TOKENS), bf16)],
        copies=2,
        micros=2,
    )
    quarter = sum_rest(quarter, nothing[0, 0])
    quarters = [quarter] + [swapped(quarter, *group) for group in GROUPS]
    others = [swapped(piece, CORE) for piece in quarters]
    tiles = lax.axis_size("sy") * lax.axis_size("sx") * lax.axis_size("ta")
    place = jnp.stack([index_bit(*CORE), quarter_index()]).astype(jnp.int32)
    gain_grad, qkv_grad, out_grad = finish_call(
        1.0 / tiles, [place, *quarters, *others, qkv_weight, layer_norm_gain]
    )
    shape = state_field.shape
    return (
        update.reshape(shape),
        field_grad.reshape(shape),
        qkv_grad,
        out_grad,
        gain_grad,
    )


def finish_call(scale, inputs):
    width = MODEL_WIDTH
    return local_call(
        functools.partial(finish_kernel, scale),
        [((width,), f32), ((width, 3 * width), f32), ((width, width), f32)],
        inputs,
        far_out=2,
        scratch=[
            ((8, width // 2, width), bf16),
            ((width, 3 * width), f32),
            ((width, width), f32),
        ],
        copies=4,
    )


def solution(mesh):
    in_specs = (
        P(("groups", "ta"), "sy", "sx", None),
        P(("groups", "ta"), "sy", "sx"),
        P(),
        P(),
        P(),
        P(),
        P(),
        P(("groups", "ta"), "sy", "sx", None),
    )
    out_specs = (
        P(("groups", "ta"), "sy", "sx", None),
        P(("groups", "ta"), "sy", "sx", None),
        P("groups", None),
        P("groups", None),
        P("groups"),
    )
    return jax.shard_map(shards, mesh=mesh, in_specs=in_specs, out_specs=out_specs, check_vma=False)
```

```python
import functools
import math

import jax
import jax.numpy as jnp
from jax import lax
from jax.experimental import pallas as pl
from jax.experimental.pallas import tpu as pltpu
from jax.sharding import PartitionSpec as P

MODEL_WIDTH = 384
HEADS = 6
HEAD_WIDTH = 64
RIM = 8
RELS = 2883
SIDE = 16
TOKENS = 512
HALF = 256
EPS = 1e-05
LOG2E = math.log2(math.e)

bf16 = jnp.bfloat16
f32 = jnp.float32


def nn(a, b):
    return lax.dot_general(a, b, (((1,), (0,)), ((), ())), preferred_element_type=f32)


def nt(a, b):
    return lax.dot_general(a, b, (((1,), (1,)), ((), ())), preferred_element_type=f32)


def tn(a, b):
    return lax.dot_general(a, b, (((0,), (0,)), ((), ())), preferred_element_type=f32)


def iota(shape, dim):
    return lax.broadcasted_iota(jnp.int32, shape, dim)


def prepare_kernel(position_bias, cot_far, out_far, weight_far, blank, *refs):
    blank[...] = jnp.zeros_like(blank)
    outs, (table, cot, out_weight, qkv_weight), refs = refs[:5], refs[5:9], refs[9:]
    bias_blocks, d_context_t, qkv_weight_t, sems = refs
    arrivals = [
        pltpu.make_async_copy(source, place, sems.at[5 + k])
        for k, (source, place) in enumerate(
            ((weight_far, qkv_weight), (out_far, out_weight), (cot_far, cot))
        )
    ]
    for copy in arrivals:
        copy.start()
    parts = [bias_blocks.at[k] for k in range(3)] + [d_context_t, qkv_weight_t]
    copies = [pltpu.make_async_copy(part, outs[k], sems.at[k]) for k, part in enumerate(parts)]
    table[...] = jnp.zeros_like(table)
    table[:HEADS, :RELS] = position_bias[...] * LOG2E
    plain = table[...]
    frames = [plain[:, :1024]] + [
        pltpu.roll(plain, plain.shape[1] - frame * 961, 1)[:, :1024] for frame in (1, 2)
    ]
    plain = jnp.concatenate(frames, 0)
    high = plain.astype(bf16)
    rest = plain - high.astype(f32)
    middle = rest.astype(bf16)
    low = (rest - middle.astype(f32)).astype(bf16)
    slot = iota((1, 1024), 1)
    source = 960 - 62 * (slot // 32 % 16) - 31 * (slot // 512) - slot % 32
    pick = (iota((1024, 1024), 0) == source).astype(f32).astype(bf16)
    turned = nn(high, pick) + nn(middle, pick) + nn(low, pick)
    lane = iota((SIDE, TOKENS), 1)
    for entry in range(HEADS * 3):
        head, frame = divmod(entry, 3)
        first = (2 - frame) * 8 + head
        even = jnp.broadcast_to(turned[first : first + 1, :TOKENS], (SIDE, TOKENS))
        odd = jnp.broadcast_to(turned[first : first + 1, TOKENS:], (SIDE, TOKENS))
        even = pltpu.roll(even, TOKENS - 15, 1, stride=1, stride_axis=0)
        odd = pltpu.roll(odd, 1, 1, stride=1, stride_axis=0)
        rows = jnp.where(lane % 32 < 16, even, odd)
        for row in range(SIDE):
            start = (15 - row) * SIDE
            bias_blocks[head // 2, entry % 6, row * SIDE : (row + 1) * SIDE, :] = rows[
                :, start : start + HALF
            ]
        if entry % 6 == 5:
            copies[head // 2].start()
        if entry == 5:
            arrivals[0].wait()
            qkv_weight_t[...] = qkv_weight[...].T
            copies[4].start()
        if entry == 11:
            arrivals[1].wait()
            arrivals[2].wait()
            d_context_t[...] = nt(out_weight[...], cot[...]).astype(bf16)
            copies[3].start()
    for copy in copies:
        copy.wait()


def source_onehots(row_shift, col_shift, sign):
    token = iota((HALF, 1), 0)
    row = token // SIDE + sign * row_shift
    col = token % SIDE + sign * col_shift
    if sign > 0:
        row_out, col_out = row >= SIDE, col >= SIDE
        near_row, near_col, span = row - SIDE, col - SIDE, SIDE
    else:
        row_out, col_out = row < 0, col < 0
        near_row, near_col, span = row + RIM, col + RIM, RIM
    inner = jnp.where(row_out | col_out, -1, row * SIDE + col)
    rows = jnp.where(row_out & ~col_out, near_row * SIDE + col, -1)
    cols = jnp.where(col_out & ~row_out, row * span + near_col, -1)
    corner = jnp.where(row_out & col_out, near_row * RIM + near_col, -1)
    return [
        (iota((HALF, count), 1) == place).astype(f32).astype(bf16)
        for place, count in ((inner, HALF), (rows, 128), (cols, SIDE * span), (corner, 64))
    ]


def flag_strip(flags, count, span=SIDE):
    total = count * span
    repeat = (iota((SIDE, total), 1) % span == iota((SIDE, total), 0)).astype(f32).astype(bf16)
    spread = nn(flags[:count, :].astype(f32).astype(bf16), repeat)
    keep = iota((count, total), 1) // span == iota((count, total), 0)
    strip = jnp.sum(jnp.where(keep, spread, 0.0), 0, keepdims=True)
    return jnp.broadcast_to(strip, (128, total)).astype(bf16)


def layer_norm(rolled):
    centred = rolled - jnp.mean(rolled, -1, keepdims=True)
    inv_std = lax.rsqrt(jnp.mean(centred * centred, -1, keepdims=True) + EPS)
    return centred * inv_std, inv_std


def attention_head(head, qkv_t, kv, penalty, bias_blocks, d_context_t):
    pair, side = divmod(head, 2)
    at = head * HEAD_WIDTH
    scale = LOG2E * HEAD_WIDTH ** (-0.5)
    zeros = jnp.zeros((HEAD_WIDTH, TOKENS), bf16)
    key_pair = kv[:, pair * 128 : pair * 128 + 128]
    value_pair = kv[:, MODEL_WIDTH + pair * 128 : MODEL_WIDTH + pair * 128 + 128]
    q_t = qkv_t[at : at + HEAD_WIDTH, :]
    k_t = qkv_t[MODEL_WIDTH + at : MODEL_WIDTH + at + HEAD_WIDTH, :]
    v_t = qkv_t[2 * MODEL_WIDTH + at : 2 * MODEL_WIDTH + at + HEAD_WIDTH, :]
    d_t = d_context_t[at : at + HEAD_WIDTH, :]
    d_eighth = d_t * 0.125
    q_wide = jnp.concatenate([q_t, zeros] if side == 0 else [zeros, q_t], 0)
    d_wide = jnp.concatenate([d_eighth, zeros] if side == 0 else [zeros, d_eighth], 0)
    context_parts = []
    dq_parts = []
    dk_parts = [0.0, 0.0]
    dv_parts = [0.0, 0.0]
    for b in range(2):
        lanes = slice(b * HALF, (b + 1) * HALF)
        scores = nn(key_pair, q_wide[:, lanes])
        d_probs = nn(value_pair, d_wide[:, lanes])
        halves = [slice(a * HALF, (a + 1) * HALF) for a in range(2)]
        s = [
            scores[halves[a]] * scale
            + bias_blocks[side * 3 + b - a + 1]
            + penalty[halves[a], lanes]
            for a in range(2)
        ]
        top = jnp.maximum(jnp.max(s[0], 0, keepdims=True), jnp.max(s[1], 0, keepdims=True))
        e = [jnp.exp2(s[a] - top) for a in range(2)]
        total = jnp.sum(e[0], 0, keepdims=True) + jnp.sum(e[1], 0, keepdims=True)
        inverse = 1.0 / total
        p = [e[a] * inverse for a in range(2)]
        pb = [p[a].astype(bf16) for a in range(2)]
        context_parts.append(nn(v_t[:, :HALF], pb[0]) + nn(v_t[:, HALF:], pb[1]))
        dp = [d_probs[halves[a]] for a in range(2)]
        delta = jnp.sum(p[0] * dp[0], 0, keepdims=True) + jnp.sum(p[1] * dp[1], 0, keepdims=True)
        ds = [(p[a] * (dp[a] - delta)).astype(bf16) for a in range(2)]
        dq_parts.append(nn(k_t[:, :HALF], ds[0]) + nn(k_t[:, HALF:], ds[1]))
        for a in range(2):
            dk_parts[a] = dk_parts[a] + nt(q_t[:, lanes], ds[a])
            dv_parts[a] = dv_parts[a] + nt(d_t[:, lanes], pb[a])
    return [
        jnp.concatenate(parts, 1).astype(bf16)
        for parts in (context_parts, dq_parts, dk_parts, dv_parts)
    ]


def main_kernel(
    shift,
    core,
    inner_flags,
    row_flags,
    col_flags,
    corner_flags,
    gain,
    inner_far,
    rows_far,
    cols_far,
    corner_far,
    weight_far,
    weight_t_far,
    d_context_far,
    bias0_far,
    cot_far,
    bias1_far,
    bias2_far,
    keep_far,
    send_far,
    d_rolled_far,
    context_far,
    lower_far,
    right_far,
    penalty,
    inner,
    rows,
    cols,
    corner,
    qkv_weight,
    qkv_weight_t,
    d_context_t,
    bias_blocks,
    cot,
    context_t,
    d_qkv,
    grads,
    d_rolled,
    right,
    sems,
):
    sources = (inner_far, rows_far, cols_far, corner_far, weight_far, weight_t_far)
    sources += (d_context_far, bias0_far, cot_far, bias1_far, bias2_far)
    places = [inner, rows, cols, corner, qkv_weight, qkv_weight_t]
    places += [d_context_t, bias_blocks.at[0], cot, bias_blocks.at[1], bias_blocks.at[2]]
    arrivals = [
        pltpu.make_async_copy(source, place, sems.at[k])
        for k, (source, place) in enumerate(zip(sources, places))
    ]
    for copy in arrivals:
        copy.start()
    onehots = source_onehots(shift[0], shift[1], 1)
    on_diagonal = iota((HALF, HALF), 0) == iota((HALF, HALF), 1)
    for t in range(2):
        strips = (
            flag_strip(inner_flags[t], SIDE),
            flag_strip(row_flags[t], RIM),
            flag_strip(col_flags[t], SIDE),
            flag_strip(corner_flags[t], RIM, RIM),
        )
        marks = sum(nt(hot, strip) for hot, strip in zip(onehots, strips))
        column = jnp.where(marks > 0.5, -1e30, 0.0)
        wide = jnp.concatenate([column, column], 1)
        own = jnp.where(on_diagonal, 0.0, wide)
        penalty[t * HALF : (t + 1) * HALF, t * HALF : (t + 1) * HALF] = own
        penalty[t * HALF : (t + 1) * HALF, (1 - t) * HALF : (2 - t) * HALF] = wide
    for copy in arrivals[:4]:
        copy.wait()
    rolled = []
    for t in range(2):
        parts = (
            inner[t * 256 : t * 256 + 256, :],
            rows[t * 128 : t * 128 + 128, :],
            cols[t * 256 : t * 256 + 256, :],
            corner[t * 64 : t * 64 + 64, :],
        )
        rolled.append(sum(nn(hot, part) for hot, part in zip(onehots, parts)))
    xhat, inv_std = layer_norm(jnp.concatenate(rolled, 0))
    gain_row = gain[...].reshape(1, MODEL_WIDTH)
    normed = (xhat * gain_row).astype(bf16)
    normed_t = normed.T
    arrivals[4].wait()
    kv = nn(normed, qkv_weight[:, MODEL_WIDTH:]).astype(bf16)
    arrivals[5].wait()
    qkv_t = nt(qkv_weight_t[...], normed).astype(bf16)
    arrivals[6].wait()
    for pair in range(HEADS // 2):
        arrivals[(7, 9, 10)[pair]].wait()
        heads = [
            attention_head(2 * pair + side, qkv_t, kv, penalty, bias_blocks.at[pair], d_context_t)
            for side in range(2)
        ]
        context, *d_parts = [jnp.concatenate(both, 0) for both in zip(*heads)]
        context_t[pair * 128 : pair * 128 + 128, :] = context
        d_pair = jnp.concatenate([part.T for part in d_parts], 1)
        for kind in range(3):
            first = kind * MODEL_WIDTH + pair * 128
            d_qkv[:, first : first + 128] = d_pair[:, kind * 128 : kind * 128 + 128]
        first = pair * TOKENS
        if pair == 0:
            arrivals[8].wait()
        grads[first : first + 128, :] = nn(context, cot[...]).astype(bf16)
        grads[first + 128 : first + TOKENS, :] = nn(normed_t, d_pair).astype(bf16)
        for block in (2 * pair, 2 * pair + 1):
            to_half(grads, block, core[0], keep_far, send_far, sems)
    keep_context = pltpu.make_async_copy(context_t, context_far, sems.at[0])
    keep_context.start()
    d_xhat = nt(d_qkv[...], qkv_weight[...]) * gain_row
    d_tokens = inv_std * (
        d_xhat
        - jnp.mean(d_xhat, -1, keepdims=True)
        - xhat * jnp.mean(d_xhat * xhat, -1, keepdims=True)
    )
    d_rolled[...] = d_tokens.astype(bf16)
    last_columns = d_tokens.reshape(2 * SIDE, SIDE, MODEL_WIDTH)[:, RIM:, :]
    right[...] = last_columns.reshape(HALF, MODEL_WIDTH).astype(bf16)
    copies = [
        pltpu.make_async_copy(d_rolled, d_rolled_far, sems.at[1]),
        pltpu.make_async_copy(right, right_far, sems.at[2]),
    ]
    for t in range(2):
        source = d_rolled.at[pl.ds(t * HALF + 128, 128), :]
        target = lower_far.at[pl.ds(t * 128, 128), :]
        copies.append(pltpu.make_async_copy(source, target, sems.at[3 + t]))
    for copy in copies:
        copy.start()
    for block in range(6):
        source, target = half_block(grads, block, keep_far)
        pltpu.make_async_copy(source, target, sems.at[11 + block]).wait()
    keep_context.wait()
    for copy in copies:
        copy.wait()


def half_block(grads, block, half):
    place = block % 3 * HALF
    return grads.at[pl.ds(block * HALF, HALF), :], half.at[pl.ds(place, HALF), :]


def to_half(grads, block, core, keep_far, send_far, sems):
    for half, side in ((keep_far, block // 3), (send_far, 1 - block // 3)):

        @pl.when(core == side)
        def _():
            source, target = half_block(grads, block, half)
            pltpu.make_async_copy(source, target, sems.at[11 + block]).start()


def place_kernel(
    shift,
    halo,
    out_weight,
    kept_far,
    context_far,
    field_grad,
    update,
    kept,
    context_t,
    sems,
):
    copies = [
        pltpu.make_async_copy(kept_far, kept, sems.at[0]),
        pltpu.make_async_copy(context_far, context_t, sems.at[1]),
    ]
    for copy in copies:
        copy.start()
    onehots = source_onehots(shift[0], shift[1], -1)
    for copy in copies:
        copy.wait()
    for t in range(2):
        parts = (
            kept[t * 256 : t * 256 + 256, :],
            halo[t * 128 : t * 128 + 128, :],
            halo[256 + t * 128 : 384 + t * 128, :],
            halo[512 + t * 64 : 576 + t * 64, :],
        )
        field_grad[t * 256 : t * 256 + 256, :] = sum(
            nn(hot, part) for hot, part in zip(onehots, parts)
        ).astype(bf16)
    update[...] = tn(context_t[...], out_weight[...]).astype(bf16)


def finish_kernel(scale, place, *refs):
    mine, other, (weight, gain) = refs[:4], refs[4:8], refs[8:10]
    gain_grad, qkv_far, out_far, shares, qkv_grad, out_grad, sems = refs[10:]
    for side, group in ((place[0], mine), (1 - place[0], other)):
        for offset in range(4):
            shares[side * 4 + (offset ^ place[1])] = group[offset][...]
    whole = shares[...].reshape(3 * TOKENS, MODEL_WIDTH).astype(f32) * scale
    copies = []
    partial = 0.0
    for kind in range(3):
        columns = slice(kind * MODEL_WIDTH, (kind + 1) * MODEL_WIDTH)
        block = jnp.concatenate(
            [
                whole[pair * TOKENS + 128 : (pair + 1) * TOKENS, kind * 128 : kind * 128 + 128]
                for pair in range(3)
            ],
            1,
        )
        qkv_grad[:, columns] = block
        copies.append(
            pltpu.make_async_copy(
                qkv_grad.at[:, columns], qkv_far.at[:, columns], sems.at[kind]
            )
        )
        copies[-1].start()
        product = block * weight[:, columns].astype(f32)
        partial = partial + product[:, :128] + product[:, 128:256] + product[:, 256:]
    for pair in range(3):
        out_grad[pair * 128 : pair * 128 + 128, :] = whole[pair * TOKENS : pair * TOKENS + 128]
    copies.append(pltpu.make_async_copy(out_grad, out_far, sems.at[3]))
    copies[-1].start()
    gain_row = gain[...].reshape(1, MODEL_WIDTH)
    gain_grad[...] = (jnp.sum(partial.T, 0, keepdims=True) / gain_row).reshape(MODEL_WIDTH)
    for copy in copies:
        copy.wait()


def local_call(
    kernel, shapes, inputs, far_in=0, far_out=0, scratch=(), copies=0, micros=1, limit=24
):
    vmem = pl.BlockSpec(memory_space=pltpu.VMEM)
    smem = pl.BlockSpec(memory_space=pltpu.SMEM)
    far = pl.BlockSpec(memory_space=pl.ANY)
    near = inputs[: len(inputs) - far_in]
    return pl.pallas_call(
        kernel,
        out_shape=[jax.ShapeDtypeStruct(shape, dtype) for shape, dtype in shapes],
        in_specs=[smem if array.dtype == jnp.int32 and array.ndim == 1 else vmem for array in near]
        + [far] * far_in,
        out_specs=[vmem] * (len(shapes) - far_out) + [far] * far_out,
        scratch_shapes=[pltpu.VMEM(shape, dtype) for shape, dtype in scratch]
        + [pltpu.SemaphoreType.DMA((copies,))],
        compiler_params=pltpu.CompilerParams(vmem_limit_bytes=limit * 2**20),
        cost_estimate=pl.CostEstimate(
            flops=micros * 10**9, bytes_accessed=10**6, transcendentals=0
        ),
    )(*inputs)


def passed_along(block, axis, distance):
    count = lax.axis_size(axis)
    return lax.ppermute(block, axis, [((i - distance) % count, i) for i in range(count)])


def passed_across(block, axis, other, distance):
    count, width = lax.axis_size(axis), lax.axis_size(other)
    route = [
        (((i - distance) % count) * width + (j - distance) % width, i * width + j)
        for i in range(count)
        for j in range(width)
    ]
    return lax.ppermute(block, (axis, other), route)


CORE = ("sx", 1)
GROUPS = ([("sy", 1)], [("ta", 1)], [("sy", 1), ("ta", 1)])


def index_bit(axis, bit):
    return (lax.axis_index(axis) & bit) // bit


def swapped(block, *bits):
    axes = tuple(axis for axis, _ in bits)
    sizes = [lax.axis_size(axis) for axis in axes]
    route = []
    for source in range(math.prod(sizes)):
        rest, places = source, []
        for size in sizes[::-1]:
            rest, place = divmod(rest, size)
            places.append(place)
        target = 0
        for size, place, (_, bit) in zip(sizes, places[::-1], bits):
            target = target * size + (place ^ bit)
        route.append((source, target))
    return lax.ppermute(block, axes, route)


def add_up(*pieces):
    return sum(piece.astype(f32) for piece in pieces).astype(bf16)


def sum_quarter(keep, send):
    block = add_up(keep, swapped(send, CORE))
    share = block.shape[0] // 4
    mine = quarter_index()
    pick = lambda place: lax.dynamic_slice_in_dim(block, place * share, share, 0)
    arrived = [swapped(pick(mine ^ k), *GROUPS[k - 1]) for k in (1, 2, 3)]
    return add_up(pick(mine), *arrived)


def sum_rest(quarter):
    rest = [
        (axis, 1 << k)
        for axis in ("ta", "sy")
        for k in range(1, lax.axis_size(axis).bit_length() - 1)
    ]
    for bit in rest:
        quarter = add_up(quarter, swapped(quarter, bit))
    return quarter


def quarter_index():
    return 2 * index_bit("ta", 1) + index_bit("sy", 1)


def shards(
    state_field,
    outlier_flags,
    window_shift,
    layer_norm_gain,
    qkv_weight,
    out_weight,
    position_bias,
    cotangent,
):
    width = MODEL_WIDTH
    wide = lambda tokens: ((tokens, width), bf16)
    rows = passed_along(state_field[:, :RIM].reshape(-1, width), "sy", -1)
    row_flags = passed_along(outlier_flags, "sy", -1)
    cols = passed_along(state_field, "sx", -1)
    col_flags = passed_along(outlier_flags, "sx", -1)
    corner_flags = passed_across(outlier_flags, "sy", "sx", -1)
    cot_rows = cotangent.reshape(TOKENS, width)
    pair_bias = ((6, HALF, HALF), f32)
    blank, *bias_blocks, d_context_t, qkv_weight_t = local_call(
        prepare_kernel,
        [wide(128)] + [pair_bias] * 3 + [((width, TOKENS), bf16), wide(3 * width)],
        [position_bias, cot_rows, out_weight, qkv_weight],
        far_in=3,
        far_out=5,
        scratch=[
            ((8, 3072), f32),
            wide(TOKENS),
            wide(width),
            ((width, 3 * width), bf16),
            ((3, 6, HALF, HALF), f32),
            ((width, TOKENS), bf16),
            wide(3 * width),
        ],
        copies=8,
        micros=3,
        limit=62,
    )
    corner_message = rows.reshape(2 * RIM, SIDE, width)[:, :RIM].reshape(-1, width) + blank
    corner = passed_along(corner_message, "sx", -1)
    core = index_bit(*CORE).astype(jnp.int32).reshape(1)
    keep, send, d_rolled, context_t, lower, right = local_call(
        main_kernel,
        [wide(2 * width)] * 2
        + [wide(TOKENS), ((width, TOKENS), bf16), wide(HALF), wide(HALF)],
        [
            window_shift,
            core,
            outlier_flags,
            row_flags,
            col_flags,
            corner_flags,
            layer_norm_gain,
            state_field.reshape(TOKENS, width),
            rows,
            cols.reshape(TOKENS, width),
            corner,
            qkv_weight,
            qkv_weight_t,
            d_context_t,
            bias_blocks[0],
            cot_rows,
            bias_blocks[1],
            bias_blocks[2],
        ],
        far_in=11,
        far_out=6,
        scratch=[
            ((TOKENS, TOKENS), f32),
            wide(TOKENS),
            wide(HALF),
            wide(TOKENS),
            wide(128),
            ((width, 3 * width), bf16),
            wide(3 * width),
            ((width, TOKENS), bf16),
            ((3, 6, HALF, HALF), f32),
            wide(TOKENS),
            ((width, TOKENS), bf16),
            ((TOKENS, 3 * width), bf16),
            wide(3 * TOKENS),
            wide(TOKENS),
            wide(HALF),
        ],
        copies=17,
        micros=12,
        limit=62,
    )
    below = passed_along(lower, "sy", 1)
    beside = passed_along(right, "sx", 1)
    across = passed_along(
        below.reshape(2 * RIM, SIDE, width)[:, RIM:].reshape(-1, width), "sx", 1
    )
    quarter = sum_quarter(keep, send)
    field_grad, update = local_call(
        place_kernel,
        [wide(TOKENS), wide(TOKENS)],
        [
            window_shift,
            jnp.concatenate([below, beside, across], 0),
            out_weight,
            d_rolled,
            context_t,
        ],
        far_in=2,
        scratch=[wide(TOKENS), ((width, TOKENS), bf16)],
        copies=2,
        micros=2,
    )
    quarter = sum_rest(quarter)
    quarters = [quarter] + [swapped(quarter, *group) for group in GROUPS]
    others = [swapped(piece, CORE) for piece in quarters]
    tiles = lax.axis_size("sy") * lax.axis_size("sx") * lax.axis_size("ta")
    place = jnp.stack([index_bit(*CORE), quarter_index()]).astype(jnp.int32)
    gain_grad, qkv_grad, out_grad = finish_call(
        1.0 / tiles, [place, *quarters, *others, qkv_weight, layer_norm_gain]
    )
    shape = state_field.shape
    return (
        update.reshape(shape),
        field_grad.reshape(shape),
        qkv_grad,
        out_grad,
        gain_grad,
    )


def finish_call(scale, inputs):
    width = MODEL_WIDTH
    return local_call(
        functools.partial(finish_kernel, scale),
        [((width,), f32), ((width, 3 * width), f32), ((width, width), f32)],
        inputs,
        far_out=2,
        scratch=[
            ((8, width // 2, width), bf16),
            ((width, 3 * width), f32),
            ((width, width), f32),
        ],
        copies=4,
    )


def solution(mesh):
    in_specs = (
        P(("groups", "ta"), "sy", "sx", None),
        P(("groups", "ta"), "sy", "sx"),
        P(),
        P(),
        P(),
        P(),
        P(),
        P(("groups", "ta"), "sy", "sx", None),
    )
    out_specs = (
        P(("groups", "ta"), "sy", "sx", None),
        P(("groups", "ta"), "sy", "sx", None),
        P("groups", None),
        P("groups", None),
        P("groups"),
    )
    return jax.shard_map(shards, mesh=mesh, in_specs=in_specs, out_specs=out_specs, check_vma=False)
```

```python
import functools
import math

import jax
import jax.numpy as jnp
from jax import lax
from jax.experimental import pallas as pl
from jax.experimental.pallas import tpu as pltpu
from jax.sharding import PartitionSpec as P

MODEL_WIDTH = 384
HEADS = 6
HEAD_WIDTH = 64
RIM = 8
RELS = 2883
SIDE = 16
TOKENS = 512
HALF = 256
EPS = 1e-05
LOG2E = math.log2(math.e)

bf16 = jnp.bfloat16
f32 = jnp.float32


def nn(a, b):
    return lax.dot_general(a, b, (((1,), (0,)), ((), ())), preferred_element_type=f32)


def nt(a, b):
    return lax.dot_general(a, b, (((1,), (1,)), ((), ())), preferred_element_type=f32)


def tn(a, b):
    return lax.dot_general(a, b, (((0,), (0,)), ((), ())), preferred_element_type=f32)


def iota(shape, dim):
    return lax.broadcasted_iota(jnp.int32, shape, dim)


def prepare_kernel(position_bias, cot_far, out_far, weight_far, blank, *refs):
    blank[...] = jnp.zeros_like(blank)
    outs, (table, cot, out_weight, qkv_weight), refs = refs[:5], refs[5:9], refs[9:]
    bias_blocks, d_context_t, qkv_weight_t, sems = refs
    arrivals = [
        pltpu.make_async_copy(source, place, sems.at[5 + k])
        for k, (source, place) in enumerate(
            ((weight_far, qkv_weight), (out_far, out_weight), (cot_far, cot))
        )
    ]
    for copy in arrivals:
        copy.start()
    parts = [bias_blocks.at[k] for k in range(3)] + [d_context_t, qkv_weight_t]
    copies = [pltpu.make_async_copy(part, outs[k], sems.at[k]) for k, part in enumerate(parts)]
    table[...] = jnp.zeros_like(table)
    table[:HEADS, :RELS] = position_bias[...] * LOG2E
    plain = table[...]
    frames = [plain[:, :1024]] + [
        pltpu.roll(plain, plain.shape[1] - frame * 961, 1)[:, :1024] for frame in (1, 2)
    ]
    frames = jnp.concatenate(frames, 0)
    plain = jnp.concatenate([frames, pltpu.roll(frames, 31, 1)], 0)
    high = plain.astype(bf16)
    rest = plain - high.astype(f32)
    middle = rest.astype(bf16)
    low = (rest - middle.astype(f32)).astype(bf16)
    slot = iota((1, TOKENS), 1)
    source = 960 - 62 * (slot // 32) - slot % 32
    pick = (iota((1024, TOKENS), 0) == source).astype(f32).astype(bf16)
    turned = nn(jnp.concatenate([high, middle, low], 0), pick)
    turned = turned[:48] + turned[48:96] + turned[96:]
    lane = iota((SIDE, TOKENS), 1)
    for entry in range(HEADS * 3):
        head, frame = divmod(entry, 3)
        first = (2 - frame) * 8 + head
        even = jnp.broadcast_to(turned[first : first + 1, :], (SIDE, TOKENS))
        odd = jnp.broadcast_to(turned[24 + first : 25 + first, :], (SIDE, TOKENS))
        even = pltpu.roll(even, TOKENS - 15, 1, stride=1, stride_axis=0)
        odd = pltpu.roll(odd, 1, 1, stride=1, stride_axis=0)
        rows = jnp.where(lane % 32 < 16, even, odd)
        for row in range(SIDE):
            start = (15 - row) * SIDE
            bias_blocks[head // 2, entry % 6, row * SIDE : (row + 1) * SIDE, :] = rows[
                :, start : start + HALF
            ]
        if entry % 6 == 5:
            copies[head // 2].start()
        if entry == 5:
            arrivals[0].wait()
            qkv_weight_t[...] = qkv_weight[...].T
            copies[4].start()
        if entry == 11:
            arrivals[1].wait()
            arrivals[2].wait()
            d_context_t[...] = nt(out_weight[...], cot[...]).astype(bf16)
            copies[3].start()
    for copy in copies:
        copy.wait()


def source_onehots(row_shift, col_shift, sign):
    token = iota((HALF, 1), 0)
    row = token // SIDE + sign * row_shift
    col = token % SIDE + sign * col_shift
    if sign > 0:
        row_out, col_out = row >= SIDE, col >= SIDE
        near_row, near_col, span = row - SIDE, col - SIDE, SIDE
    else:
        row_out, col_out = row < 0, col < 0
        near_row, near_col, span = row + RIM, col + RIM, RIM
    inner = jnp.where(row_out | col_out, -1, row * SIDE + col)
    rows = jnp.where(row_out & ~col_out, near_row * SIDE + col, -1)
    cols = jnp.where(col_out & ~row_out, row * span + near_col, -1)
    corner = jnp.where(row_out & col_out, near_row * RIM + near_col, -1)
    return [
        (iota((HALF, count), 1) == place).astype(f32).astype(bf16)
        for place, count in ((inner, HALF), (rows, 128), (cols, SIDE * span), (corner, 64))
    ]


def flag_strip(flags, count, span=SIDE):
    total = count * span
    repeat = (iota((SIDE, total), 1) % span == iota((SIDE, total), 0)).astype(f32).astype(bf16)
    spread = nn(flags[:count, :].astype(bf16), repeat)
    keep = iota((count, total), 1) // span == iota((count, total), 0)
    strip = jnp.sum(jnp.where(keep, spread, 0.0), 0, keepdims=True)
    return jnp.broadcast_to(strip, (128, total)).astype(bf16)


def layer_norm(rolled):
    centred = rolled - jnp.mean(rolled, -1, keepdims=True)
    inv_std = lax.rsqrt(jnp.mean(centred * centred, -1, keepdims=True) + EPS)
    return centred * inv_std, inv_std


def attention_head(head, qkv_t, kv, penalty, bias_blocks, d_context_t):
    pair, side = divmod(head, 2)
    at = head * HEAD_WIDTH
    scale = LOG2E * HEAD_WIDTH ** (-0.5)
    zeros = jnp.zeros((HEAD_WIDTH, TOKENS), bf16)
    key_pair = kv[:, pair * 128 : pair * 128 + 128]
    value_pair = kv[:, MODEL_WIDTH + pair * 128 : MODEL_WIDTH + pair * 128 + 128]
    q_t = qkv_t[at : at + HEAD_WIDTH, :]
    k_t = qkv_t[MODEL_WIDTH + at : MODEL_WIDTH + at + HEAD_WIDTH, :]
    v_t = qkv_t[2 * MODEL_WIDTH + at : 2 * MODEL_WIDTH + at + HEAD_WIDTH, :]
    d_t = d_context_t[at : at + HEAD_WIDTH, :]
    d_eighth = d_t * 0.125
    q_wide = jnp.concatenate([q_t, zeros] if side == 0 else [zeros, q_t], 0)
    d_wide = jnp.concatenate([d_eighth, zeros] if side == 0 else [zeros, d_eighth], 0)
    context_parts = []
    dq_parts = []
    dk_parts = [0.0, 0.0]
    dv_parts = [0.0, 0.0]
    for b in range(2):
        lanes = slice(b * HALF, (b + 1) * HALF)
        scores = nn(key_pair, q_wide[:, lanes])
        d_probs = nn(value_pair, d_wide[:, lanes])
        halves = [slice(a * HALF, (a + 1) * HALF) for a in range(2)]
        s = [
            scores[halves[a]] * scale
            + bias_blocks[side * 3 + b - a + 1]
            + penalty[halves[a], lanes]
            for a in range(2)
        ]
        top = jnp.maximum(jnp.max(s[0], 0, keepdims=True), jnp.max(s[1], 0, keepdims=True))
        e = [jnp.exp2(s[a] - top) for a in range(2)]
        total = jnp.sum(e[0], 0, keepdims=True) + jnp.sum(e[1], 0, keepdims=True)
        inverse = 1.0 / total
        p = [e[a] * inverse for a in range(2)]
        pb = [p[a].astype(bf16) for a in range(2)]
        context_parts.append(nn(v_t[:, :HALF], pb[0]) + nn(v_t[:, HALF:], pb[1]))
        dp = [d_probs[halves[a]] for a in range(2)]
        delta = jnp.sum(p[0] * dp[0], 0, keepdims=True) + jnp.sum(p[1] * dp[1], 0, keepdims=True)
        ds = [(p[a] * (dp[a] - delta)).astype(bf16) for a in range(2)]
        dq_parts.append(nn(k_t[:, :HALF], ds[0]) + nn(k_t[:, HALF:], ds[1]))
        for a in range(2):
            dk_parts[a] = dk_parts[a] + nt(q_t[:, lanes], ds[a])
            dv_parts[a] = dv_parts[a] + nt(d_t[:, lanes], pb[a])
    return [
        jnp.concatenate(parts, 1).astype(bf16)
        for parts in (context_parts, dq_parts, dk_parts, dv_parts)
    ]


def main_kernel(
    shift,
    core,
    inner_flags,
    col_flags,
    gain,
    inner_far,
    rows_far,
    cols_far,
    corner_far,
    weight_far,
    weight_t_far,
    d_context_far,
    bias0_far,
    cot_far,
    bias1_far,
    bias2_far,
    keep_far,
    send_far,
    d_rolled_far,
    context_far,
    lower_far,
    right_far,
    penalty,
    inner,
    rows,
    cols,
    corner,
    qkv_weight,
    qkv_weight_t,
    d_context_t,
    bias_blocks,
    cot,
    context_t,
    d_qkv,
    grads,
    d_rolled,
    right,
    sems,
):
    sources = (inner_far, rows_far, cols_far, corner_far, weight_far, weight_t_far)
    sources += (d_context_far, bias0_far, cot_far, bias1_far, bias2_far)
    places = [inner, rows, cols, corner, qkv_weight, qkv_weight_t]
    places += [d_context_t, bias_blocks.at[0], cot, bias_blocks.at[1], bias_blocks.at[2]]
    arrivals = [
        pltpu.make_async_copy(source, place, sems.at[k])
        for k, (source, place) in enumerate(zip(sources, places))
    ]
    for copy in arrivals:
        copy.start()
    onehots = source_onehots(shift[0], shift[1], 1)
    on_diagonal = iota((HALF, HALF), 0) == iota((HALF, HALF), 1)
    for copy in arrivals[:4]:
        copy.wait()
    for t in range(2):
        strips = (
            flag_strip(inner_flags[t].astype(f32), SIDE),
            flag_strip(rows[256:272, :SIDE][t * RIM : (t + 1) * RIM], RIM),
            flag_strip(col_flags[t].astype(f32), SIDE),
            flag_strip(corner[128:144, :SIDE][t * RIM : (t + 1) * RIM], RIM, RIM),
        )
        marks = sum(nt(hot, strip) for hot, strip in zip(onehots, strips))
        column = jnp.where(marks > 0.5, -1e30, 0.0)
        wide = jnp.concatenate([column, column], 1)
        own = jnp.where(on_diagonal, 0.0, wide)
        penalty[t * HALF : (t + 1) * HALF, t * HALF : (t + 1) * HALF] = own
        penalty[t * HALF : (t + 1) * HALF, (1 - t) * HALF : (2 - t) * HALF] = wide
    rolled = []
    for t in range(2):
        parts = (
            inner[t * 256 : t * 256 + 256, :],
            rows[t * 128 : t * 128 + 128, :],
            cols[t * 256 : t * 256 + 256, :],
            corner[t * 64 : t * 64 + 64, :],
        )
        rolled.append(sum(nn(hot, part) for hot, part in zip(onehots, parts)))
    xhat, inv_std = layer_norm(jnp.concatenate(rolled, 0))
    gain_row = gain[...].reshape(1, MODEL_WIDTH)
    normed = (xhat * gain_row).astype(bf16)
    normed_t = normed.T
    arrivals[4].wait()
    kv = nn(normed, qkv_weight[:, MODEL_WIDTH:]).astype(bf16)
    arrivals[5].wait()
    qkv_t = nt(qkv_weight_t[...], normed).astype(bf16)
    arrivals[6].wait()
    for pair in range(HEADS // 2):
        arrivals[(7, 9, 10)[pair]].wait()
        heads = [
            attention_head(2 * pair + side, qkv_t, kv, penalty, bias_blocks.at[pair], d_context_t)
            for side in range(2)
        ]
        context, *d_parts = [jnp.concatenate(both, 0) for both in zip(*heads)]
        context_t[pair * 128 : pair * 128 + 128, :] = context
        d_pair = jnp.concatenate([part.T for part in d_parts], 1)
        for kind in range(3):
            first = kind * MODEL_WIDTH + pair * 128
            d_qkv[:, first : first + 128] = d_pair[:, kind * 128 : kind * 128 + 128]
        first = pair * TOKENS
        if pair == 0:
            arrivals[8].wait()
        grads[first : first + 128, :] = nn(context, cot[...]).astype(bf16)
        grads[first + 128 : first + TOKENS, :] = nn(normed_t, d_pair).astype(bf16)
        for block in (2 * pair, 2 * pair + 1):
            to_half(grads, block, core[0], keep_far, send_far, sems)
    keep_context = pltpu.make_async_copy(context_t, context_far, sems.at[0])
    keep_context.start()
    d_xhat = nt(d_qkv[...], qkv_weight[...]) * gain_row
    d_tokens = inv_std * (
        d_xhat
        - jnp.mean(d_xhat, -1, keepdims=True)
        - xhat * jnp.mean(d_xhat * xhat, -1, keepdims=True)
    )
    d_rolled[...] = d_tokens.astype(bf16)
    last_columns = d_tokens.reshape(2 * SIDE, SIDE, MODEL_WIDTH)[:, RIM:, :]
    right[...] = last_columns.reshape(HALF, MODEL_WIDTH).astype(bf16)
    copies = [
        pltpu.make_async_copy(d_rolled, d_rolled_far, sems.at[1]),
        pltpu.make_async_copy(right, right_far, sems.at[2]),
    ]
    for t in range(2):
        source = d_rolled.at[pl.ds(t * HALF + 128, 128), :]
        target = lower_far.at[pl.ds(t * 128, 128), :]
        copies.append(pltpu.make_async_copy(source, target, sems.at[3 + t]))
    for copy in copies:
        copy.start()
    for block in range(6):
        source, target = half_block(grads, block, keep_far)
        pltpu.make_async_copy(source, target, sems.at[11 + block]).wait()
    keep_context.wait()
    for copy in copies:
        copy.wait()


def half_block(grads, block, half):
    place = block % 3 * HALF
    return grads.at[pl.ds(block * HALF, HALF), :], half.at[pl.ds(place, HALF), :]


def to_half(grads, block, core, keep_far, send_far, sems):
    for half, side in ((keep_far, block // 3), (send_far, 1 - block // 3)):

        @pl.when(core == side)
        def _():
            source, target = half_block(grads, block, half)
            pltpu.make_async_copy(source, target, sems.at[11 + block]).start()


def place_kernel(
    shift,
    halo,
    out_weight,
    kept_far,
    context_far,
    field_grad,
    update,
    kept,
    context_t,
    sems,
):
    copies = [
        pltpu.make_async_copy(kept_far, kept, sems.at[0]),
        pltpu.make_async_copy(context_far, context_t, sems.at[1]),
    ]
    for copy in copies:
        copy.start()
    onehots = source_onehots(shift[0], shift[1], -1)
    for copy in copies:
        copy.wait()
    for t in range(2):
        parts = (
            kept[t * 256 : t * 256 + 256, :],
            halo[t * 128 : t * 128 + 128, :],
            halo[256 + t * 128 : 384 + t * 128, :],
            halo[512 + t * 64 : 576 + t * 64, :],
        )
        field_grad[t * 256 : t * 256 + 256, :] = sum(
            nn(hot, part) for hot, part in zip(onehots, parts)
        ).astype(bf16)
    update[...] = tn(context_t[...], out_weight[...]).astype(bf16)


def finish_kernel(scale, place, *refs):
    mine, other, (weight, gain) = refs[:4], refs[4:8], refs[8:10]
    gain_grad, qkv_far, out_far, shares, qkv_grad, out_grad, sems = refs[10:]
    for side, group in ((place[0], mine), (1 - place[0], other)):
        for offset in range(4):
            shares[side * 4 + (offset ^ place[1])] = group[offset][...]
    whole = shares[...].reshape(3 * TOKENS, MODEL_WIDTH).astype(f32) * scale
    copies = []
    partial = 0.0
    for kind in range(3):
        columns = slice(kind * MODEL_WIDTH, (kind + 1) * MODEL_WIDTH)
        block = jnp.concatenate(
            [
                whole[pair * TOKENS + 128 : (pair + 1) * TOKENS, kind * 128 : kind * 128 + 128]
                for pair in range(3)
            ],
            1,
        )
        qkv_grad[:, columns] = block
        copies.append(
            pltpu.make_async_copy(
                qkv_grad.at[:, columns], qkv_far.at[:, columns], sems.at[kind]
            )
        )
        copies[-1].start()
        product = block * weight[:, columns].astype(f32)
        partial = partial + product[:, :128] + product[:, 128:256] + product[:, 256:]
    for pair in range(3):
        out_grad[pair * 128 : pair * 128 + 128, :] = whole[pair * TOKENS : pair * TOKENS + 128]
    copies.append(pltpu.make_async_copy(out_grad, out_far, sems.at[3]))
    copies[-1].start()
    gain_row = gain[...].reshape(1, MODEL_WIDTH)
    gain_grad[...] = (jnp.sum(partial.T, 0, keepdims=True) / gain_row).reshape(MODEL_WIDTH)
    for copy in copies:
        copy.wait()


def local_call(
    kernel, shapes, inputs, far_in=0, far_out=0, scratch=(), copies=0, micros=1, limit=24
):
    vmem = pl.BlockSpec(memory_space=pltpu.VMEM)
    smem = pl.BlockSpec(memory_space=pltpu.SMEM)
    far = pl.BlockSpec(memory_space=pl.ANY)
    near = inputs[: len(inputs) - far_in]
    return pl.pallas_call(
        kernel,
        out_shape=[jax.ShapeDtypeStruct(shape, dtype) for shape, dtype in shapes],
        in_specs=[smem if array.dtype == jnp.int32 and array.ndim == 1 else vmem for array in near]
        + [far] * far_in,
        out_specs=[vmem] * (len(shapes) - far_out) + [far] * far_out,
        scratch_shapes=[pltpu.VMEM(shape, dtype) for shape, dtype in scratch]
        + [pltpu.SemaphoreType.DMA((copies,))],
        compiler_params=pltpu.CompilerParams(vmem_limit_bytes=limit * 2**20),
        cost_estimate=pl.CostEstimate(
            flops=micros * 10**9, bytes_accessed=10**6, transcendentals=0
        ),
    )(*inputs)


def passed_along(block, axis, distance):
    count = lax.axis_size(axis)
    return lax.ppermute(block, axis, [((i - distance) % count, i) for i in range(count)])


CORE = ("sx", 1)
GROUPS = ([("sy", 1)], [("ta", 1)], [("sy", 1), ("ta", 1)])


def index_bit(axis, bit):
    return (lax.axis_index(axis) & bit) // bit


def swapped(block, *bits):
    axes = tuple(axis for axis, _ in bits)
    sizes = [lax.axis_size(axis) for axis in axes]
    route = []
    for source in range(math.prod(sizes)):
        rest, places = source, []
        for size in sizes[::-1]:
            rest, place = divmod(rest, size)
            places.append(place)
        target = 0
        for size, place, (_, bit) in zip(sizes, places[::-1], bits):
            target = target * size + (place ^ bit)
        route.append((source, target))
    return lax.ppermute(block, axes, route)


def add_up(*pieces):
    return sum(piece.astype(f32) for piece in pieces).astype(bf16)


def sum_quarter(keep, send):
    block = add_up(keep, swapped(send, CORE))
    share = block.shape[0] // 4
    mine = quarter_index()
    pick = lambda place: lax.dynamic_slice_in_dim(block, place * share, share, 0)
    arrived = [swapped(pick(mine ^ k), *GROUPS[k - 1]) for k in (1, 2, 3)]
    return add_up(pick(mine), *arrived)


def sum_rest(quarter):
    rest = [
        (axis, 1 << k)
        for axis in ("ta", "sy")
        for k in range(1, lax.axis_size(axis).bit_length() - 1)
    ]
    for bit in rest:
        quarter = add_up(quarter, swapped(quarter, bit))
    return quarter


def quarter_index():
    return 2 * index_bit("ta", 1) + index_bit("sy", 1)


def shards(
    state_field,
    outlier_flags,
    window_shift,
    layer_norm_gain,
    qkv_weight,
    out_weight,
    position_bias,
    cotangent,
):
    width = MODEL_WIDTH
    wide = lambda tokens: ((tokens, width), bf16)
    row_flags = outlier_flags[:, :RIM].reshape(2 * RIM, SIDE).astype(bf16)
    row_message = jnp.concatenate(
        [
            state_field[:, :RIM].reshape(-1, width),
            jnp.pad(row_flags, ((0, 0), (0, width - SIDE))),
        ],
        0,
    )
    rows = passed_along(row_message, "sy", -1)
    cols = passed_along(state_field, "sx", -1)
    col_flags = passed_along(outlier_flags, "sx", -1)
    cot_rows = cotangent.reshape(TOKENS, width)
    pair_bias = ((6, HALF, HALF), f32)
    blank, *bias_blocks, d_context_t, qkv_weight_t = local_call(
        prepare_kernel,
        [wide(144)] + [pair_bias] * 3 + [((width, TOKENS), bf16), wide(3 * width)],
        [position_bias, cot_rows, out_weight, qkv_weight],
        far_in=3,
        far_out=5,
        scratch=[
            ((8, 3072), f32),
            wide(TOKENS),
            wide(width),
            ((width, 3 * width), bf16),
            ((3, 6, HALF, HALF), f32),
            ((width, TOKENS), bf16),
            wide(3 * width),
        ],
        copies=8,
        micros=3,
        limit=62,
    )
    corner_message = jnp.concatenate(
        [
            rows[: 2 * RIM * SIDE].reshape(2 * RIM, SIDE, width)[:, :RIM].reshape(-1, width),
            rows[2 * RIM * SIDE :],
        ],
        0,
    )
    corner = passed_along(corner_message + blank, "sx", -1)
    core = index_bit(*CORE).astype(jnp.int32).reshape(1)
    keep, send, d_rolled, context_t, lower, right = local_call(
        main_kernel,
        [wide(2 * width)] * 2
        + [wide(TOKENS), ((width, TOKENS), bf16), wide(HALF), wide(HALF)],
        [
            window_shift,
            core,
            outlier_flags,
            col_flags,
            layer_norm_gain,
            state_field.reshape(TOKENS, width),
            rows,
            cols.reshape(TOKENS, width),
            corner,
            qkv_weight,
            qkv_weight_t,
            d_context_t,
            bias_blocks[0],
            cot_rows,
            bias_blocks[1],
            bias_blocks[2],
        ],
        far_in=11,
        far_out=6,
        scratch=[
            ((TOKENS, TOKENS), f32),
            wide(TOKENS),
            wide(HALF + 16),
            wide(TOKENS),
            wide(144),
            ((width, 3 * width), bf16),
            wide(3 * width),
            ((width, TOKENS), bf16),
            ((3, 6, HALF, HALF), f32),
            wide(TOKENS),
            ((width, TOKENS), bf16),
            ((TOKENS, 3 * width), bf16),
            wide(3 * TOKENS),
            wide(TOKENS),
            wide(HALF),
        ],
        copies=17,
        micros=12,
        limit=62,
    )
    below = passed_along(lower, "sy", 1)
    beside = passed_along(right, "sx", 1)
    across = passed_along(
        below.reshape(2 * RIM, SIDE, width)[:, RIM:].reshape(-1, width), "sx", 1
    )
    quarter = sum_quarter(keep, send)
    field_grad, update = local_call(
        place_kernel,
        [wide(TOKENS), wide(TOKENS)],
        [
            window_shift,
            jnp.concatenate([below, beside, across], 0),
            out_weight,
            d_rolled,
            context_t,
        ],
        far_in=2,
        scratch=[wide(TOKENS), ((width, TOKENS), bf16)],
        copies=2,
        micros=2,
    )
    quarter = sum_rest(quarter)
    quarters = [quarter] + [swapped(quarter, *group) for group in GROUPS]
    others = [swapped(piece, CORE) for piece in quarters]
    tiles = lax.axis_size("sy") * lax.axis_size("sx") * lax.axis_size("ta")
    place = jnp.stack([index_bit(*CORE), quarter_index()]).astype(jnp.int32)
    gain_grad, qkv_grad, out_grad = finish_call(
        1.0 / tiles, [place, *quarters, *others, qkv_weight, layer_norm_gain]
    )
    shape = state_field.shape
    return (
        update.reshape(shape),
        field_grad.reshape(shape),
        qkv_grad,
        out_grad,
        gain_grad,
    )


def finish_call(scale, inputs):
    width = MODEL_WIDTH
    return local_call(
        functools.partial(finish_kernel, scale),
        [((width,), f32), ((width, 3 * width), f32), ((width, width), f32)],
        inputs,
        far_out=2,
        scratch=[
            ((8, width // 2, width), bf16),
            ((width, 3 * width), f32),
            ((width, width), f32),
        ],
        copies=4,
    )


def solution(mesh):
    in_specs = (
        P(("groups", "ta"), "sy", "sx", None),
        P(("groups", "ta"), "sy", "sx"),
        P(),
        P(),
        P(),
        P(),
        P(),
        P(("groups", "ta"), "sy", "sx", None),
    )
    out_specs = (
        P(("groups", "ta"), "sy", "sx", None),
        P(("groups", "ta"), "sy", "sx", None),
        P("groups", None),
        P("groups", None),
        P("groups"),
    )
    return jax.shard_map(shards, mesh=mesh, in_specs=in_specs, out_specs=out_specs, check_vma=False)
```

```python
import functools
import math

import jax
import jax.numpy as jnp
from jax import lax
from jax.experimental import pallas as pl
from jax.experimental.pallas import tpu as pltpu
from jax.sharding import PartitionSpec as P

MODEL_WIDTH = 384
HEADS = 6
HEAD_WIDTH = 64
RIM = 8
RELS = 2883
SIDE = 16
TOKENS = 512
HALF = 256
EPS = 1e-05
LOG2E = math.log2(math.e)

bf16 = jnp.bfloat16
f32 = jnp.float32


def nn(a, b):
    return lax.dot_general(a, b, (((1,), (0,)), ((), ())), preferred_element_type=f32)


def nt(a, b):
    return lax.dot_general(a, b, (((1,), (1,)), ((), ())), preferred_element_type=f32)


def tn(a, b):
    return lax.dot_general(a, b, (((0,), (0,)), ((), ())), preferred_element_type=f32)


def iota(shape, dim):
    return lax.broadcasted_iota(jnp.int32, shape, dim)


def prepare_kernel(position_bias, cot_far, out_far, weight_far, blank, *refs):
    blank[...] = jnp.zeros_like(blank)
    outs, (table, cot, out_weight, qkv_weight), refs = refs[:5], refs[5:9], refs[9:]
    bias_blocks, d_context_t, qkv_weight_t, sems = refs
    arrivals = [
        pltpu.make_async_copy(source, place, sems.at[5 + k])
        for k, (source, place) in enumerate(
            ((weight_far, qkv_weight), (out_far, out_weight), (cot_far, cot))
        )
    ]
    for copy in arrivals:
        copy.start()
    parts = [bias_blocks.at[k] for k in range(3)] + [d_context_t, qkv_weight_t]
    copies = [pltpu.make_async_copy(part, outs[k], sems.at[k]) for k, part in enumerate(parts)]
    table[...] = jnp.zeros_like(table)
    table[:HEADS, :RELS] = position_bias[...] * LOG2E
    plain = table[...]
    frames = [plain[:, :1024]] + [
        pltpu.roll(plain, plain.shape[1] - frame * 961, 1)[:, :1024] for frame in (1, 2)
    ]
    frames = jnp.concatenate(frames, 0)
    plain = jnp.concatenate([frames, pltpu.roll(frames, 31, 1)], 0)
    high = plain.astype(bf16)
    rest = plain - high.astype(f32)
    middle = rest.astype(bf16)
    low = (rest - middle.astype(f32)).astype(bf16)
    slot = iota((1, TOKENS), 1)
    source = 960 - 62 * (slot // 32) - slot % 32
    pick = (iota((1024, TOKENS), 0) == source).astype(f32).astype(bf16)
    turned = nn(jnp.concatenate([high, middle, low], 0), pick)
    turned = turned[:48] + turned[48:96] + turned[96:]
    lane = iota((SIDE, TOKENS), 1)
    for entry in range(HEADS * 3):
        head, frame = divmod(entry, 3)
        first = (2 - frame) * 8 + head
        even = jnp.broadcast_to(turned[first : first + 1, :], (SIDE, TOKENS))
        odd = jnp.broadcast_to(turned[24 + first : 25 + first, :], (SIDE, TOKENS))
        even = pltpu.roll(even, TOKENS - 15, 1, stride=1, stride_axis=0)
        odd = pltpu.roll(odd, 1, 1, stride=1, stride_axis=0)
        rows = jnp.where(lane % 32 < 16, even, odd)
        for row in range(SIDE):
            start = (15 - row) * SIDE
            bias_blocks[head // 2, entry % 6, row * SIDE : (row + 1) * SIDE, :] = rows[
                :, start : start + HALF
            ]
        if entry % 6 == 5:
            copies[head // 2].start()
        if entry == 5:
            arrivals[0].wait()
            qkv_weight_t[...] = qkv_weight[...].T
            copies[4].start()
        if entry == 11:
            arrivals[1].wait()
            arrivals[2].wait()
            d_context_t[...] = nt(out_weight[...], cot[...]).astype(bf16)
            copies[3].start()
    for copy in copies:
        copy.wait()


def source_onehots(row_shift, col_shift, sign):
    token = iota((HALF, 1), 0)
    row = token // SIDE + sign * row_shift
    col = token % SIDE + sign * col_shift
    if sign > 0:
        row_out, col_out = row >= SIDE, col >= SIDE
        near_row, near_col, span = row - SIDE, col - SIDE, SIDE
    else:
        row_out, col_out = row < 0, col < 0
        near_row, near_col, span = row + RIM, col + RIM, RIM
    inner = jnp.where(row_out | col_out, -1, row * SIDE + col)
    rows = jnp.where(row_out & ~col_out, near_row * SIDE + col, -1)
    cols = jnp.where(col_out & ~row_out, row * span + near_col, -1)
    corner = jnp.where(row_out & col_out, near_row * RIM + near_col, -1)
    return [
        (iota((HALF, count), 1) == place).astype(f32).astype(bf16)
        for place, count in ((inner, HALF), (rows, 128), (cols, SIDE * span), (corner, 64))
    ]


def flag_strip(flags, count, span=SIDE):
    total = count * span
    repeat = (iota((SIDE, total), 1) % span == iota((SIDE, total), 0)).astype(f32).astype(bf16)
    spread = nn(flags[:count, :].astype(bf16), repeat)
    keep = iota((count, total), 1) // span == iota((count, total), 0)
    strip = jnp.sum(jnp.where(keep, spread, 0.0), 0, keepdims=True)
    return jnp.broadcast_to(strip, (128, total)).astype(bf16)


def layer_norm(rolled):
    centred = rolled - jnp.mean(rolled, -1, keepdims=True)
    inv_std = lax.rsqrt(jnp.mean(centred * centred, -1, keepdims=True) + EPS)
    return centred * inv_std, inv_std


def attention_head(head, qkv_t, kv, penalty, bias_blocks, d_context_t):
    pair, side = divmod(head, 2)
    at = head * HEAD_WIDTH
    scale = LOG2E * HEAD_WIDTH ** (-0.5)
    zeros = jnp.zeros((HEAD_WIDTH, TOKENS), bf16)
    key_pair = kv[:, pair * 128 : pair * 128 + 128]
    value_pair = kv[:, MODEL_WIDTH + pair * 128 : MODEL_WIDTH + pair * 128 + 128]
    q_t = qkv_t[at : at + HEAD_WIDTH, :]
    k_t = qkv_t[MODEL_WIDTH + at : MODEL_WIDTH + at + HEAD_WIDTH, :]
    v_t = qkv_t[2 * MODEL_WIDTH + at : 2 * MODEL_WIDTH + at + HEAD_WIDTH, :]
    d_t = d_context_t[at : at + HEAD_WIDTH, :]
    d_eighth = d_t * 0.125
    q_wide = jnp.concatenate([q_t, zeros] if side == 0 else [zeros, q_t], 0)
    d_wide = jnp.concatenate([d_eighth, zeros] if side == 0 else [zeros, d_eighth], 0)
    context_parts = []
    dq_parts = []
    dk_parts = [0.0, 0.0]
    dv_parts = [0.0, 0.0]
    for b in range(2):
        lanes = slice(b * HALF, (b + 1) * HALF)
        scores = nn(key_pair, q_wide[:, lanes])
        d_probs = nn(value_pair, d_wide[:, lanes])
        halves = [slice(a * HALF, (a + 1) * HALF) for a in range(2)]
        s = [
            scores[halves[a]] * scale
            + bias_blocks[side * 3 + b - a + 1]
            + penalty[halves[a], lanes]
            for a in range(2)
        ]
        top = jnp.maximum(jnp.max(s[0], 0, keepdims=True), jnp.max(s[1], 0, keepdims=True))
        e = [jnp.exp2(s[a] - top) for a in range(2)]
        total = jnp.sum(e[0], 0, keepdims=True) + jnp.sum(e[1], 0, keepdims=True)
        inverse = 1.0 / total
        p = [e[a] * inverse for a in range(2)]
        pb = [p[a].astype(bf16) for a in range(2)]
        context_parts.append(nn(v_t[:, :HALF], pb[0]) + nn(v_t[:, HALF:], pb[1]))
        dp = [d_probs[halves[a]] for a in range(2)]
        delta = jnp.sum(p[0] * dp[0], 0, keepdims=True) + jnp.sum(p[1] * dp[1], 0, keepdims=True)
        ds = [(p[a] * (dp[a] - delta)).astype(bf16) for a in range(2)]
        dq_parts.append(nn(k_t[:, :HALF], ds[0]) + nn(k_t[:, HALF:], ds[1]))
        for a in range(2):
            dk_parts[a] = dk_parts[a] + nt(q_t[:, lanes], ds[a])
            dv_parts[a] = dv_parts[a] + nt(d_t[:, lanes], pb[a])
    return [
        jnp.concatenate(parts, 1).astype(bf16)
        for parts in (context_parts, dq_parts, dk_parts, dv_parts)
    ]


def main_kernel(
    shift,
    core,
    inner_flags,
    col_flags,
    gain,
    inner_far,
    rows_far,
    cols_far,
    corner_far,
    weight_far,
    weight_t_far,
    d_context_far,
    bias0_far,
    cot_far,
    bias1_far,
    bias2_far,
    keep_far,
    send_far,
    d_rolled_far,
    context_far,
    lower_far,
    right_far,
    penalty,
    inner,
    rows,
    cols,
    corner,
    qkv_weight,
    qkv_weight_t,
    d_context_t,
    bias_blocks,
    cot,
    context_t,
    d_qkv,
    grads,
    d_rolled,
    right,
    sems,
):
    sources = (inner_far, rows_far, cols_far, corner_far, weight_far, weight_t_far)
    sources += (d_context_far, bias0_far, cot_far, bias1_far, bias2_far)
    places = [inner, rows, cols, corner, qkv_weight, qkv_weight_t]
    places += [d_context_t, bias_blocks.at[0], cot, bias_blocks.at[1], bias_blocks.at[2]]
    arrivals = [
        pltpu.make_async_copy(source, place, sems.at[k])
        for k, (source, place) in enumerate(zip(sources, places))
    ]
    for copy in arrivals:
        copy.start()
    onehots = source_onehots(shift[0], shift[1], 1)
    on_diagonal = iota((HALF, HALF), 0) == iota((HALF, HALF), 1)
    for copy in arrivals[:4]:
        copy.wait()
    for t in range(2):
        strips = (
            flag_strip(inner_flags[t].astype(f32), SIDE),
            flag_strip(rows[256:272, :SIDE][t * RIM : (t + 1) * RIM], RIM),
            flag_strip(col_flags[t].astype(f32), SIDE),
            flag_strip(corner[128:144, :SIDE][t * RIM : (t + 1) * RIM], RIM, RIM),
        )
        marks = sum(nt(hot, strip) for hot, strip in zip(onehots, strips))
        column = jnp.where(marks > 0.5, -1e30, 0.0)
        wide = jnp.concatenate([column, column], 1)
        own = jnp.where(on_diagonal, 0.0, wide)
        penalty[t * HALF : (t + 1) * HALF, t * HALF : (t + 1) * HALF] = own
        penalty[t * HALF : (t + 1) * HALF, (1 - t) * HALF : (2 - t) * HALF] = wide
    rolled = []
    for t in range(2):
        parts = (
            inner[t * 256 : t * 256 + 256, :],
            rows[t * 128 : t * 128 + 128, :],
            cols[t * 256 : t * 256 + 256, :],
            corner[t * 64 : t * 64 + 64, :],
        )
        rolled.append(sum(nn(hot, part) for hot, part in zip(onehots, parts)))
    xhat, inv_std = layer_norm(jnp.concatenate(rolled, 0))
    gain_row = gain[...].reshape(1, MODEL_WIDTH)
    normed = (xhat * gain_row).astype(bf16)
    normed_t = normed.T
    arrivals[4].wait()
    kv = nn(normed, qkv_weight[:, MODEL_WIDTH:]).astype(bf16)
    arrivals[5].wait()
    qkv_t = nt(qkv_weight_t[...], normed).astype(bf16)
    arrivals[6].wait()
    for pair in range(HEADS // 2):
        arrivals[(7, 9, 10)[pair]].wait()
        heads = [
            attention_head(2 * pair + side, qkv_t, kv, penalty, bias_blocks.at[pair], d_context_t)
            for side in range(2)
        ]
        context, *d_parts = [jnp.concatenate(both, 0) for both in zip(*heads)]
        context_t[pair * 128 : pair * 128 + 128, :] = context
        d_pair = jnp.concatenate([part.T for part in d_parts], 1)
        for kind in range(3):
            first = kind * MODEL_WIDTH + pair * 128
            d_qkv[:, first : first + 128] = d_pair[:, kind * 128 : kind * 128 + 128]
        first = pair * TOKENS
        if pair == 0:
            arrivals[8].wait()
        grads[first : first + 128, :] = nn(context, cot[...]).astype(bf16)
        grads[first + 128 : first + TOKENS, :] = nn(normed_t, d_pair).astype(bf16)
        for block in (2 * pair, 2 * pair + 1):
            to_half(grads, block, core[0], keep_far, send_far, sems)
    keep_context = pltpu.make_async_copy(context_t, context_far, sems.at[0])
    keep_context.start()
    d_xhat = nt(d_qkv[...], qkv_weight[...]) * gain_row
    d_tokens = inv_std * (
        d_xhat
        - jnp.mean(d_xhat, -1, keepdims=True)
        - xhat * jnp.mean(d_xhat * xhat, -1, keepdims=True)
    )
    d_rolled[...] = d_tokens.astype(bf16)
    last_columns = d_tokens.reshape(2 * SIDE, SIDE, MODEL_WIDTH)[:, RIM:, :]
    right[...] = last_columns.reshape(HALF, MODEL_WIDTH).astype(bf16)
    copies = [
        pltpu.make_async_copy(d_rolled, d_rolled_far, sems.at[1]),
        pltpu.make_async_copy(right, right_far, sems.at[2]),
    ]
    for t in range(2):
        source = d_rolled.at[pl.ds(t * HALF + 128, 128), :]
        target = lower_far.at[pl.ds(t * 128, 128), :]
        copies.append(pltpu.make_async_copy(source, target, sems.at[3 + t]))
    for copy in copies:
        copy.start()
    for block in range(6):
        source, target = half_block(grads, block, keep_far)
        pltpu.make_async_copy(source, target, sems.at[11 + block]).wait()
    keep_context.wait()
    for copy in copies:
        copy.wait()


def half_block(grads, block, half):
    place = block % 3 * HALF
    return grads.at[pl.ds(block * HALF, HALF), :], half.at[pl.ds(place, HALF), :]


def to_half(grads, block, core, keep_far, send_far, sems):
    for half, side in ((keep_far, block // 3), (send_far, 1 - block // 3)):

        @pl.when(core == side)
        def _():
            source, target = half_block(grads, block, half)
            pltpu.make_async_copy(source, target, sems.at[11 + block]).start()


def place_kernel(
    shift,
    halo,
    out_weight,
    kept_far,
    context_far,
    field_grad,
    update,
    kept,
    context_t,
    sems,
):
    copies = [
        pltpu.make_async_copy(kept_far, kept, sems.at[0]),
        pltpu.make_async_copy(context_far, context_t, sems.at[1]),
    ]
    for copy in copies:
        copy.start()
    onehots = source_onehots(shift[0], shift[1], -1)
    for copy in copies:
        copy.wait()
    for t in range(2):
        parts = (
            kept[t * 256 : t * 256 + 256, :],
            halo[t * 128 : t * 128 + 128, :],
            halo[256 + t * 128 : 384 + t * 128, :],
            halo[512 + t * 64 : 576 + t * 64, :],
        )
        field_grad[t * 256 : t * 256 + 256, :] = sum(
            nn(hot, part) for hot, part in zip(onehots, parts)
        ).astype(bf16)
    update[...] = tn(context_t[...], out_weight[...]).astype(bf16)


def finish_kernel(scale, place, *refs):
    mine, other, (weight, gain) = refs[:4], refs[4:8], refs[8:10]
    gain_grad, qkv_far, out_far, shares, qkv_grad, out_grad, sems = refs[10:]
    for side, group in ((place[0], mine), (1 - place[0], other)):
        for offset in range(4):
            shares[side * 4 + (offset ^ place[1])] = group[offset][...]
    whole = shares[...].reshape(3 * TOKENS, MODEL_WIDTH).astype(f32) * scale
    copies = []
    partial = 0.0
    for kind in range(3):
        columns = slice(kind * MODEL_WIDTH, (kind + 1) * MODEL_WIDTH)
        block = jnp.concatenate(
            [
                whole[pair * TOKENS + 128 : (pair + 1) * TOKENS, kind * 128 : kind * 128 + 128]
                for pair in range(3)
            ],
            1,
        )
        qkv_grad[:, columns] = block
        copies.append(
            pltpu.make_async_copy(
                qkv_grad.at[:, columns], qkv_far.at[:, columns], sems.at[kind]
            )
        )
        copies[-1].start()
        product = block * weight[:, columns].astype(f32)
        partial = partial + product[:, :128] + product[:, 128:256] + product[:, 256:]
    for pair in range(3):
        out_grad[pair * 128 : pair * 128 + 128, :] = whole[pair * TOKENS : pair * TOKENS + 128]
    copies.append(pltpu.make_async_copy(out_grad, out_far, sems.at[3]))
    copies[-1].start()
    gain_row = gain[...].reshape(1, MODEL_WIDTH)
    gain_grad[...] = (jnp.sum(partial.T, 0, keepdims=True) / gain_row).reshape(MODEL_WIDTH)
    for copy in copies:
        copy.wait()


def local_call(
    kernel, shapes, inputs, far_in=0, far_out=0, scratch=(), copies=0, micros=1, limit=24
):
    vmem = pl.BlockSpec(memory_space=pltpu.VMEM)
    smem = pl.BlockSpec(memory_space=pltpu.SMEM)
    far = pl.BlockSpec(memory_space=pl.ANY)
    near = inputs[: len(inputs) - far_in]
    return pl.pallas_call(
        kernel,
        out_shape=[jax.ShapeDtypeStruct(shape, dtype) for shape, dtype in shapes],
        in_specs=[smem if array.dtype == jnp.int32 and array.ndim == 1 else vmem for array in near]
        + [far] * far_in,
        out_specs=[vmem] * (len(shapes) - far_out) + [far] * far_out,
        scratch_shapes=[pltpu.VMEM(shape, dtype) for shape, dtype in scratch]
        + [pltpu.SemaphoreType.DMA((copies,))],
        compiler_params=pltpu.CompilerParams(vmem_limit_bytes=limit * 2**20),
        cost_estimate=pl.CostEstimate(
            flops=micros * 10**9, bytes_accessed=10**6, transcendentals=0
        ),
    )(*inputs)


def passed_along(block, axis, distance):
    count = lax.axis_size(axis)
    return lax.ppermute(block, axis, [((i - distance) % count, i) for i in range(count)])


CORE = ("sx", 1)
GROUPS = ([("sy", 1)], [("ta", 1)], [("sy", 1), ("ta", 1)])


def index_bit(axis, bit):
    return (lax.axis_index(axis) & bit) // bit


def swapped(block, *bits):
    axes = tuple(axis for axis, _ in bits)
    sizes = [lax.axis_size(axis) for axis in axes]
    route = []
    for source in range(math.prod(sizes)):
        rest, places = source, []
        for size in sizes[::-1]:
            rest, place = divmod(rest, size)
            places.append(place)
        target = 0
        for size, place, (_, bit) in zip(sizes, places[::-1], bits):
            target = target * size + (place ^ bit)
        route.append((source, target))
    return lax.ppermute(block, axes, route)


def add_up(*pieces):
    return sum(piece.astype(f32) for piece in pieces).astype(bf16)


def sum_quarter(keep, send):
    block = add_up(keep, swapped(send, CORE))
    rows, columns = lax.axis_size("sy"), lax.axis_size("ta")
    squares = [
        [(i + di) * columns + j + dj for dj in range(2) for di in range(2)]
        for i in range(0, rows, 2)
        for j in range(0, columns, 2)
    ]
    shares = block.reshape(4, block.shape[0] // 4, block.shape[1])
    arrived = lax.all_to_all(
        shares, ("sy", "ta"), split_axis=0, concat_axis=0, axis_index_groups=squares
    )
    return add_up(*arrived)


def sum_rest(quarter):
    rest = [
        (axis, 1 << k)
        for axis in ("ta", "sy")
        for k in range(1, lax.axis_size(axis).bit_length() - 1)
    ]
    for bit in rest:
        quarter = add_up(quarter, swapped(quarter, bit))
    return quarter


def quarter_index():
    return 2 * index_bit("ta", 1) + index_bit("sy", 1)


def shards(
    state_field,
    outlier_flags,
    window_shift,
    layer_norm_gain,
    qkv_weight,
    out_weight,
    position_bias,
    cotangent,
):
    width = MODEL_WIDTH
    wide = lambda tokens: ((tokens, width), bf16)
    row_flags = outlier_flags[:, :RIM].reshape(2 * RIM, SIDE).astype(bf16)
    row_message = jnp.concatenate(
        [
            state_field[:, :RIM].reshape(-1, width),
            jnp.pad(row_flags, ((0, 0), (0, width - SIDE))),
        ],
        0,
    )
    rows = passed_along(row_message, "sy", -1)
    cols = passed_along(state_field, "sx", -1)
    col_flags = passed_along(outlier_flags, "sx", -1)
    cot_rows = cotangent.reshape(TOKENS, width)
    pair_bias = ((6, HALF, HALF), f32)
    blank, *bias_blocks, d_context_t, qkv_weight_t = local_call(
        prepare_kernel,
        [wide(144)] + [pair_bias] * 3 + [((width, TOKENS), bf16), wide(3 * width)],
        [position_bias, cot_rows, out_weight, qkv_weight],
        far_in=3,
        far_out=5,
        scratch=[
            ((8, 3072), f32),
            wide(TOKENS),
            wide(width),
            ((width, 3 * width), bf16),
            ((3, 6, HALF, HALF), f32),
            ((width, TOKENS), bf16),
            wide(3 * width),
        ],
        copies=8,
        micros=3,
        limit=62,
    )
    corner_message = jnp.concatenate(
        [
            rows[: 2 * RIM * SIDE].reshape(2 * RIM, SIDE, width)[:, :RIM].reshape(-1, width),
            rows[2 * RIM * SIDE :],
        ],
        0,
    )
    corner = passed_along(corner_message + blank, "sx", -1)
    core = index_bit(*CORE).astype(jnp.int32).reshape(1)
    keep, send, d_rolled, context_t, lower, right = local_call(
        main_kernel,
        [wide(2 * width)] * 2
        + [wide(TOKENS), ((width, TOKENS), bf16), wide(HALF), wide(HALF)],
        [
            window_shift,
            core,
            outlier_flags,
            col_flags,
            layer_norm_gain,
            state_field.reshape(TOKENS, width),
            rows,
            cols.reshape(TOKENS, width),
            corner,
            qkv_weight,
            qkv_weight_t,
            d_context_t,
            bias_blocks[0],
            cot_rows,
            bias_blocks[1],
            bias_blocks[2],
        ],
        far_in=11,
        far_out=6,
        scratch=[
            ((TOKENS, TOKENS), f32),
            wide(TOKENS),
            wide(HALF + 16),
            wide(TOKENS),
            wide(144),
            ((width, 3 * width), bf16),
            wide(3 * width),
            ((width, TOKENS), bf16),
            ((3, 6, HALF, HALF), f32),
            wide(TOKENS),
            ((width, TOKENS), bf16),
            ((TOKENS, 3 * width), bf16),
            wide(3 * TOKENS),
            wide(TOKENS),
            wide(HALF),
        ],
        copies=17,
        micros=12,
        limit=62,
    )
    below = passed_along(lower, "sy", 1)
    beside = passed_along(right, "sx", 1)
    across = passed_along(
        below.reshape(2 * RIM, SIDE, width)[:, RIM:].reshape(-1, width), "sx", 1
    )
    quarter = sum_quarter(keep, send)
    field_grad, update = local_call(
        place_kernel,
        [wide(TOKENS), wide(TOKENS)],
        [
            window_shift,
            jnp.concatenate([below, beside, across], 0),
            out_weight,
            d_rolled,
            context_t,
        ],
        far_in=2,
        scratch=[wide(TOKENS), ((width, TOKENS), bf16)],
        copies=2,
        micros=2,
    )
    quarter = sum_rest(quarter)
    quarters = [quarter] + [swapped(quarter, *group) for group in GROUPS]
    others = [swapped(piece, CORE) for piece in quarters]
    tiles = lax.axis_size("sy") * lax.axis_size("sx") * lax.axis_size("ta")
    place = jnp.stack([index_bit(*CORE), quarter_index()]).astype(jnp.int32)
    gain_grad, qkv_grad, out_grad = finish_call(
        1.0 / tiles, [place, *quarters, *others, qkv_weight, layer_norm_gain]
    )
    shape = state_field.shape
    return (
        update.reshape(shape),
        field_grad.reshape(shape),
        qkv_grad,
        out_grad,
        gain_grad,
    )


def finish_call(scale, inputs):
    width = MODEL_WIDTH
    return local_call(
        functools.partial(finish_kernel, scale),
        [((width,), f32), ((width, 3 * width), f32), ((width, width), f32)],
        inputs,
        far_out=2,
        scratch=[
            ((8, width // 2, width), bf16),
            ((width, 3 * width), f32),
            ((width, width), f32),
        ],
        copies=4,
    )


def solution(mesh):
    in_specs = (
        P(("groups", "ta"), "sy", "sx", None),
        P(("groups", "ta"), "sy", "sx"),
        P(),
        P(),
        P(),
        P(),
        P(),
        P(("groups", "ta"), "sy", "sx", None),
    )
    out_specs = (
        P(("groups", "ta"), "sy", "sx", None),
        P(("groups", "ta"), "sy", "sx", None),
        P("groups", None),
        P("groups", None),
        P("groups"),
    )
    return jax.shard_map(shards, mesh=mesh, in_specs=in_specs, out_specs=out_specs, check_vma=False)
```

```python
import functools
import math

import jax
import jax.numpy as jnp
from jax import lax
from jax.experimental import pallas as pl
from jax.experimental.pallas import tpu as pltpu
from jax.sharding import PartitionSpec as P

MODEL_WIDTH = 384
HEADS = 6
HEAD_WIDTH = 64
RIM = 8
RELS = 2883
SIDE = 16
TOKENS = 512
HALF = 256
EPS = 1e-05
LOG2E = math.log2(math.e)

bf16 = jnp.bfloat16
f32 = jnp.float32


def nn(a, b):
    return lax.dot_general(a, b, (((1,), (0,)), ((), ())), preferred_element_type=f32)


def nt(a, b):
    return lax.dot_general(a, b, (((1,), (1,)), ((), ())), preferred_element_type=f32)


def tn(a, b):
    return lax.dot_general(a, b, (((0,), (0,)), ((), ())), preferred_element_type=f32)


def iota(shape, dim):
    return lax.broadcasted_iota(jnp.int32, shape, dim)


def prepare_kernel(position_bias, cot_far, out_far, weight_far, blank, *refs):
    blank[...] = jnp.zeros_like(blank)
    outs, (table, cot, out_weight, qkv_weight), refs = refs[:5], refs[5:9], refs[9:]
    bias_blocks, d_context_t, qkv_weight_t, sems = refs
    arrivals = [
        pltpu.make_async_copy(source, place, sems.at[5 + k])
        for k, (source, place) in enumerate(
            ((weight_far, qkv_weight), (out_far, out_weight), (cot_far, cot))
        )
    ]
    for copy in arrivals:
        copy.start()
    parts = [bias_blocks.at[k] for k in range(3)] + [d_context_t, qkv_weight_t]
    copies = [pltpu.make_async_copy(part, outs[k], sems.at[k]) for k, part in enumerate(parts)]
    table[...] = jnp.zeros_like(table)
    table[:HEADS, :RELS] = position_bias[...] * LOG2E
    plain = table[...]
    frames = [plain[:, :1024]] + [
        pltpu.roll(plain, plain.shape[1] - frame * 961, 1)[:, :1024] for frame in (1, 2)
    ]
    frames = jnp.concatenate(frames, 0)
    plain = jnp.concatenate([frames, pltpu.roll(frames, 31, 1)], 0)
    high = plain.astype(bf16)
    rest = plain - high.astype(f32)
    middle = rest.astype(bf16)
    low = (rest - middle.astype(f32)).astype(bf16)
    slot = iota((1, TOKENS), 1)
    source = 960 - 62 * (slot // 32) - slot % 32
    pick = (iota((1024, TOKENS), 0) == source).astype(f32).astype(bf16)
    turned = nn(jnp.concatenate([high, middle, low], 0), pick)
    turned = turned[:48] + turned[48:96] + turned[96:]
    lane = iota((SIDE, TOKENS), 1)
    for entry in range(HEADS * 3):
        head, frame = divmod(entry, 3)
        first = (2 - frame) * 8 + head
        even = jnp.broadcast_to(turned[first : first + 1, :], (SIDE, TOKENS))
        odd = jnp.broadcast_to(turned[24 + first : 25 + first, :], (SIDE, TOKENS))
        even = pltpu.roll(even, TOKENS - 15, 1, stride=1, stride_axis=0)
        odd = pltpu.roll(odd, 1, 1, stride=1, stride_axis=0)
        rows = jnp.where(lane % 32 < 16, even, odd)
        for row in range(SIDE):
            start = (15 - row) * SIDE
            bias_blocks[head // 2, entry % 6, row * SIDE : (row + 1) * SIDE, :] = rows[
                :, start : start + HALF
            ]
        if entry % 6 == 5:
            copies[head // 2].start()
        if entry == 5:
            arrivals[0].wait()
            qkv_weight_t[...] = qkv_weight[...].T
            copies[4].start()
        if entry == 11:
            arrivals[1].wait()
            arrivals[2].wait()
            d_context_t[...] = nt(out_weight[...], cot[...]).astype(bf16)
            copies[3].start()
    for copy in copies:
        copy.wait()


def source_onehots(row_shift, col_shift, sign):
    token = iota((HALF, 1), 0)
    row = token // SIDE + sign * row_shift
    col = token % SIDE + sign * col_shift
    if sign > 0:
        row_out, col_out = row >= SIDE, col >= SIDE
        near_row, near_col, span = row - SIDE, col - SIDE, SIDE
    else:
        row_out, col_out = row < 0, col < 0
        near_row, near_col, span = row + RIM, col + RIM, RIM
    inner = jnp.where(row_out | col_out, -1, row * SIDE + col)
    rows = jnp.where(row_out & ~col_out, near_row * SIDE + col, -1)
    cols = jnp.where(col_out & ~row_out, row * span + near_col, -1)
    corner = jnp.where(row_out & col_out, near_row * RIM + near_col, -1)
    return [
        (iota((HALF, count), 1) == place).astype(f32).astype(bf16)
        for place, count in ((inner, HALF), (rows, 128), (cols, SIDE * span), (corner, 64))
    ]


def flag_strip(flags, count, span=SIDE):
    total = count * span
    repeat = (iota((SIDE, total), 1) % span == iota((SIDE, total), 0)).astype(f32).astype(bf16)
    spread = nn(flags[:count, :].astype(bf16), repeat)
    keep = iota((count, total), 1) // span == iota((count, total), 0)
    strip = jnp.sum(jnp.where(keep, spread, 0.0), 0, keepdims=True)
    return jnp.broadcast_to(strip, (128, total)).astype(bf16)


def layer_norm(rolled):
    centred = rolled - jnp.mean(rolled, -1, keepdims=True)
    inv_std = lax.rsqrt(jnp.mean(centred * centred, -1, keepdims=True) + EPS)
    return centred * inv_std, inv_std


def attention_head(head, qkv_t, kv, penalty, bias_blocks, d_context_t):
    pair, side = divmod(head, 2)
    at = head * HEAD_WIDTH
    scale = LOG2E * HEAD_WIDTH ** (-0.5)
    zeros = jnp.zeros((HEAD_WIDTH, TOKENS), bf16)
    key_pair = kv[:, pair * 128 : pair * 128 + 128]
    value_pair = kv[:, MODEL_WIDTH + pair * 128 : MODEL_WIDTH + pair * 128 + 128]
    q_t = qkv_t[at : at + HEAD_WIDTH, :]
    k_t = qkv_t[MODEL_WIDTH + at : MODEL_WIDTH + at + HEAD_WIDTH, :]
    v_t = qkv_t[2 * MODEL_WIDTH + at : 2 * MODEL_WIDTH + at + HEAD_WIDTH, :]
    d_t = d_context_t[at : at + HEAD_WIDTH, :]
    d_eighth = d_t * 0.125
    q_wide = jnp.concatenate([q_t, zeros] if side == 0 else [zeros, q_t], 0)
    d_wide = jnp.concatenate([d_eighth, zeros] if side == 0 else [zeros, d_eighth], 0)
    context_parts = []
    dq_parts = []
    dk_parts = [0.0, 0.0]
    dv_parts = [0.0, 0.0]
    for b in range(2):
        lanes = slice(b * HALF, (b + 1) * HALF)
        scores = nn(key_pair, q_wide[:, lanes])
        d_probs = nn(value_pair, d_wide[:, lanes])
        halves = [slice(a * HALF, (a + 1) * HALF) for a in range(2)]
        s = [
            scores[halves[a]] * scale
            + bias_blocks[side * 3 + b - a + 1]
            + penalty[halves[a], lanes]
            for a in range(2)
        ]
        top = jnp.maximum(jnp.max(s[0], 0, keepdims=True), jnp.max(s[1], 0, keepdims=True))
        e = [jnp.exp2(s[a] - top) for a in range(2)]
        total = jnp.sum(e[0], 0, keepdims=True) + jnp.sum(e[1], 0, keepdims=True)
        inverse = 1.0 / total
        p = [e[a] * inverse for a in range(2)]
        pb = [p[a].astype(bf16) for a in range(2)]
        context_parts.append(nn(v_t[:, :HALF], pb[0]) + nn(v_t[:, HALF:], pb[1]))
        dp = [d_probs[halves[a]] for a in range(2)]
        delta = jnp.sum(p[0] * dp[0], 0, keepdims=True) + jnp.sum(p[1] * dp[1], 0, keepdims=True)
        ds = [(p[a] * (dp[a] - delta)).astype(bf16) for a in range(2)]
        dq_parts.append(nn(k_t[:, :HALF], ds[0]) + nn(k_t[:, HALF:], ds[1]))
        for a in range(2):
            dk_parts[a] = dk_parts[a] + nt(q_t[:, lanes], ds[a])
            dv_parts[a] = dv_parts[a] + nt(d_t[:, lanes], pb[a])
    return [
        jnp.concatenate(parts, 1).astype(bf16)
        for parts in (context_parts, dq_parts, dk_parts, dv_parts)
    ]


def main_kernel(
    shift,
    core,
    inner_flags,
    col_flags,
    gain,
    inner_far,
    rows_far,
    cols_far,
    corner_far,
    weight_far,
    weight_t_far,
    d_context_far,
    bias0_far,
    cot_far,
    bias1_far,
    bias2_far,
    out_weight_far,
    keep_far,
    send_far,
    d_rolled_far,
    update_far,
    lower_far,
    right_far,
    penalty,
    inner,
    rows,
    cols,
    corner,
    qkv_weight,
    qkv_weight_t,
    d_context_t,
    bias_blocks,
    cot,
    context_t,
    d_qkv,
    grads,
    d_rolled,
    right,
    out_weight,
    update,
    sems,
):
    sources = (inner_far, rows_far, cols_far, corner_far, weight_far, weight_t_far)
    sources += (d_context_far, bias0_far, cot_far, bias1_far, bias2_far)
    sources += (out_weight_far,)
    places = [inner, rows, cols, corner, qkv_weight, qkv_weight_t]
    places += [d_context_t, bias_blocks.at[0], cot, bias_blocks.at[1], bias_blocks.at[2]]
    places.append(out_weight)
    arrivals = [
        pltpu.make_async_copy(source, place, sems.at[k])
        for k, (source, place) in enumerate(zip(sources, places))
    ]
    for copy in arrivals:
        copy.start()
    onehots = source_onehots(shift[0], shift[1], 1)
    for copy in arrivals[:4]:
        copy.wait()
    rolled = []
    for t in range(2):
        parts = (
            inner[t * 256 : t * 256 + 256, :],
            rows[t * 128 : t * 128 + 128, :],
            cols[t * 256 : t * 256 + 256, :],
            corner[t * 64 : t * 64 + 64, :],
        )
        rolled.append(sum(nn(hot, part) for hot, part in zip(onehots, parts)))
    xhat, inv_std = layer_norm(jnp.concatenate(rolled, 0))
    gain_row = gain[...].reshape(1, MODEL_WIDTH)
    normed = (xhat * gain_row).astype(bf16)
    normed_t = normed.T
    arrivals[4].wait()
    arrivals[5].wait()
    kv = nn(normed, qkv_weight[:, MODEL_WIDTH:]).astype(bf16)
    qkv_t = nt(qkv_weight_t[...], normed).astype(bf16)
    on_diagonal = iota((HALF, HALF), 0) == iota((HALF, HALF), 1)
    for t in range(2):
        strips = (
            flag_strip(inner_flags[t].astype(f32), SIDE),
            flag_strip(rows[256:272, :SIDE][t * RIM : (t + 1) * RIM], RIM),
            flag_strip(col_flags[t].astype(f32), SIDE),
            flag_strip(corner[128:144, :SIDE][t * RIM : (t + 1) * RIM], RIM, RIM),
        )
        marks = sum(nt(hot, strip) for hot, strip in zip(onehots, strips))
        column = jnp.where(marks > 0.5, -1e30, 0.0)
        wide = jnp.concatenate([column, column], 1)
        own = jnp.where(on_diagonal, 0.0, wide)
        penalty[t * HALF : (t + 1) * HALF, t * HALF : (t + 1) * HALF] = own
        penalty[t * HALF : (t + 1) * HALF, (1 - t) * HALF : (2 - t) * HALF] = wide
    for copy in arrivals[6:]:
        copy.wait()
    for pair in range(HEADS // 2):
        heads = [
            attention_head(2 * pair + side, qkv_t, kv, penalty, bias_blocks.at[pair], d_context_t)
            for side in range(2)
        ]
        context, *d_parts = [jnp.concatenate(both, 0) for both in zip(*heads)]
        context_t[pair * 128 : pair * 128 + 128, :] = context
        d_pair = jnp.concatenate([part.T for part in d_parts], 1)
        for kind in range(3):
            first = kind * MODEL_WIDTH + pair * 128
            d_qkv[:, first : first + 128] = d_pair[:, kind * 128 : kind * 128 + 128]
        first = pair * TOKENS
        grads[first : first + 128, :] = nn(context, cot[...]).astype(bf16)
        grads[first + 128 : first + TOKENS, :] = nn(normed_t, d_pair).astype(bf16)
    for block in range(6):
        to_half(grads, block, core[0], keep_far, send_far, sems)
    d_xhat = nt(d_qkv[...], qkv_weight[...]) * gain_row
    d_tokens = inv_std * (
        d_xhat
        - jnp.mean(d_xhat, -1, keepdims=True)
        - xhat * jnp.mean(d_xhat * xhat, -1, keepdims=True)
    )
    d_rolled[...] = d_tokens.astype(bf16)
    last_columns = d_tokens.reshape(2 * SIDE, SIDE, MODEL_WIDTH)[:, RIM:, :]
    update[...] = tn(context_t[...], out_weight[...]).astype(bf16)
    right[...] = last_columns.reshape(HALF, MODEL_WIDTH).astype(bf16)
    copies = [
        pltpu.make_async_copy(d_rolled, d_rolled_far, sems.at[1]),
        pltpu.make_async_copy(right, right_far, sems.at[2]),
        pltpu.make_async_copy(update, update_far, sems.at[0]),
    ]
    for t in range(2):
        source = d_rolled.at[pl.ds(t * HALF + 128, 128), :]
        target = lower_far.at[pl.ds(t * 128, 128), :]
        copies.append(pltpu.make_async_copy(source, target, sems.at[3 + t]))
    for copy in copies:
        copy.start()
    for block in range(6):
        source, target = half_block(grads, block, keep_far)
        pltpu.make_async_copy(source, target, sems.at[12 + block]).wait()
    for copy in copies:
        copy.wait()


def half_block(grads, block, half):
    place = block % 3 * HALF
    return grads.at[pl.ds(block * HALF, HALF), :], half.at[pl.ds(place, HALF), :]


def to_half(grads, block, core, keep_far, send_far, sems):
    for half, side in ((keep_far, block // 3), (send_far, 1 - block // 3)):

        @pl.when(core == side)
        def _():
            source, target = half_block(grads, block, half)
            pltpu.make_async_copy(source, target, sems.at[12 + block]).start()


def place_kernel(shift, halo, kept_far, field_grad, kept, sems):
    copy = pltpu.make_async_copy(kept_far, kept, sems.at[0])
    copy.start()
    onehots = source_onehots(shift[0], shift[1], -1)
    copy.wait()
    for t in range(2):
        parts = (
            kept[t * 256 : t * 256 + 256, :],
            halo[t * 128 : t * 128 + 128, :],
            halo[256 + t * 128 : 384 + t * 128, :],
            halo[512 + t * 64 : 576 + t * 64, :],
        )
        field_grad[t * 256 : t * 256 + 256, :] = sum(
            nn(hot, part) for hot, part in zip(onehots, parts)
        ).astype(bf16)


def finish_kernel(scale, place, *refs):
    mine, other, (weight, gain) = refs[:4], refs[4:8], refs[8:10]
    gain_grad, qkv_far, out_far, shares, qkv_grad, out_grad, sems = refs[10:]
    for side, group in ((place[0], mine), (1 - place[0], other)):
        for offset in range(4):
            shares[side * 4 + (offset ^ place[1])] = group[offset][...]
    whole = shares[...].reshape(3 * TOKENS, MODEL_WIDTH).astype(f32) * scale
    copies = []
    partial = 0.0
    for kind in range(3):
        columns = slice(kind * MODEL_WIDTH, (kind + 1) * MODEL_WIDTH)
        block = jnp.concatenate(
            [
                whole[pair * TOKENS + 128 : (pair + 1) * TOKENS, kind * 128 : kind * 128 + 128]
                for pair in range(3)
            ],
            1,
        )
        qkv_grad[:, columns] = block
        copies.append(
            pltpu.make_async_copy(
                qkv_grad.at[:, columns], qkv_far.at[:, columns], sems.at[kind]
            )
        )
        copies[-1].start()
        product = block * weight[:, columns].astype(f32)
        partial = partial + product[:, :128] + product[:, 128:256] + product[:, 256:]
    for pair in range(3):
        out_grad[pair * 128 : pair * 128 + 128, :] = whole[pair * TOKENS : pair * TOKENS + 128]
    copies.append(pltpu.make_async_copy(out_grad, out_far, sems.at[3]))
    copies[-1].start()
    gain_row = gain[...].reshape(1, MODEL_WIDTH)
    gain_grad[...] = (jnp.sum(partial.T, 0, keepdims=True) / gain_row).reshape(MODEL_WIDTH)
    for copy in copies:
        copy.wait()


def local_call(
    kernel, shapes, inputs, far_in=0, far_out=0, scratch=(), copies=0, micros=1, limit=24
):
    vmem = pl.BlockSpec(memory_space=pltpu.VMEM)
    smem = pl.BlockSpec(memory_space=pltpu.SMEM)
    far = pl.BlockSpec(memory_space=pl.ANY)
    near = inputs[: len(inputs) - far_in]
    return pl.pallas_call(
        kernel,
        out_shape=[jax.ShapeDtypeStruct(shape, dtype) for shape, dtype in shapes],
        in_specs=[smem if array.dtype == jnp.int32 and array.ndim == 1 else vmem for array in near]
        + [far] * far_in,
        out_specs=[vmem] * (len(shapes) - far_out) + [far] * far_out,
        scratch_shapes=[pltpu.VMEM(shape, dtype) for shape, dtype in scratch]
        + [pltpu.SemaphoreType.DMA((copies,))],
        compiler_params=pltpu.CompilerParams(vmem_limit_bytes=limit * 2**20),
        cost_estimate=pl.CostEstimate(
            flops=micros * 10**9, bytes_accessed=10**6, transcendentals=0
        ),
    )(*inputs)


def passed_along(block, axis, distance):
    count = lax.axis_size(axis)
    return lax.ppermute(block, axis, [((i - distance) % count, i) for i in range(count)])


CORE = ("sx", 1)
GROUPS = ([("sy", 1)], [("ta", 1)], [("sy", 1), ("ta", 1)])


def index_bit(axis, bit):
    return (lax.axis_index(axis) & bit) // bit


def swapped(block, *bits):
    axes = tuple(axis for axis, _ in bits)
    sizes = [lax.axis_size(axis) for axis in axes]
    route = []
    for source in range(math.prod(sizes)):
        rest, places = source, []
        for size in sizes[::-1]:
            rest, place = divmod(rest, size)
            places.append(place)
        target = 0
        for size, place, (_, bit) in zip(sizes, places[::-1], bits):
            target = target * size + (place ^ bit)
        route.append((source, target))
    return lax.ppermute(block, axes, route)


def add_up(*pieces):
    return sum(piece.astype(f32) for piece in pieces).astype(bf16)


def sum_quarter(keep, send):
    block = add_up(keep, swapped(send, CORE))
    share = block.shape[0] // 4
    mine = quarter_index()
    pick = lambda place: lax.dynamic_slice_in_dim(block, place * share, share, 0)
    arrived = [swapped(pick(mine ^ k), *GROUPS[k - 1]) for k in (1, 2, 3)]
    return add_up(pick(mine), *arrived)


def sum_rest(quarter):
    rest = [
        (axis, 1 << k)
        for axis in ("ta", "sy")
        for k in range(1, lax.axis_size(axis).bit_length() - 1)
    ]
    for bit in rest:
        quarter = add_up(quarter, swapped(quarter, bit))
    return quarter


def quarter_index():
    return 2 * index_bit("ta", 1) + index_bit("sy", 1)


def shards(
    state_field,
    outlier_flags,
    window_shift,
    layer_norm_gain,
    qkv_weight,
    out_weight,
    position_bias,
    cotangent,
):
    width = MODEL_WIDTH
    wide = lambda tokens: ((tokens, width), bf16)
    row_flags = outlier_flags[:, :RIM].reshape(2 * RIM, SIDE).astype(bf16)
    row_message = jnp.concatenate(
        [
            state_field[:, :RIM].reshape(-1, width),
            jnp.pad(row_flags, ((0, 0), (0, width - SIDE))),
        ],
        0,
    )
    rows = passed_along(row_message, "sy", -1)
    cols = passed_along(state_field, "sx", -1)
    col_flags = passed_along(outlier_flags, "sx", -1)
    cot_rows = cotangent.reshape(TOKENS, width)
    pair_bias = ((6, HALF, HALF), f32)
    blank, *bias_blocks, d_context_t, qkv_weight_t = local_call(
        prepare_kernel,
        [wide(16)] + [pair_bias] * 3 + [((width, TOKENS), bf16), wide(3 * width)],
        [position_bias, cot_rows, out_weight, qkv_weight],
        far_in=3,
        far_out=5,
        scratch=[
            ((8, 3072), f32),
            wide(TOKENS),
            wide(width),
            ((width, 3 * width), bf16),
            ((3, 6, HALF, HALF), f32),
            ((width, TOKENS), bf16),
            wide(3 * width),
        ],
        copies=8,
        micros=3,
        limit=62,
    )
    corner_message = jnp.concatenate(
        [
            rows[: 2 * RIM * SIDE].reshape(2 * RIM, SIDE, width)[:, :RIM].reshape(-1, width),
            rows[2 * RIM * SIDE :] + blank,
        ],
        0,
    )
    corner = passed_along(corner_message, "sx", -1)
    core = index_bit(*CORE).astype(jnp.int32).reshape(1)
    keep, send, d_rolled, update, lower, right = local_call(
        main_kernel,
        [wide(2 * width)] * 2
        + [wide(TOKENS), wide(TOKENS), wide(HALF), wide(HALF)],
        [
            window_shift,
            core,
            outlier_flags,
            col_flags,
            layer_norm_gain,
            state_field.reshape(TOKENS, width),
            rows,
            cols.reshape(TOKENS, width),
            corner,
            qkv_weight,
            qkv_weight_t,
            d_context_t,
            bias_blocks[0],
            cot_rows,
            bias_blocks[1],
            bias_blocks[2],
            out_weight,
        ],
        far_in=12,
        far_out=6,
        scratch=[
            ((TOKENS, TOKENS), f32),
            wide(TOKENS),
            wide(HALF + 16),
            wide(TOKENS),
            wide(144),
            ((width, 3 * width), bf16),
            wide(3 * width),
            ((width, TOKENS), bf16),
            ((3, 6, HALF, HALF), f32),
            wide(TOKENS),
            ((width, TOKENS), bf16),
            ((TOKENS, 3 * width), bf16),
            wide(3 * TOKENS),
            wide(TOKENS),
            wide(HALF),
            wide(width),
            wide(TOKENS),
        ],
        copies=18,
        micros=12,
        limit=62,
    )
    below = passed_along(lower, "sy", 1)
    beside = passed_along(right, "sx", 1)
    across = passed_along(
        below.reshape(2 * RIM, SIDE, width)[:, RIM:].reshape(-1, width), "sx", 1
    )
    quarter = sum_quarter(keep, send)
    (field_grad,) = local_call(
        place_kernel,
        [wide(TOKENS)],
        [window_shift, jnp.concatenate([below, beside, across], 0), d_rolled],
        far_in=1,
        scratch=[wide(TOKENS)],
        copies=1,
        micros=2,
    )
    quarter = sum_rest(quarter)
    quarters = [quarter] + [swapped(quarter, *group) for group in GROUPS]
    others = [swapped(piece, CORE) for piece in quarters]
    tiles = lax.axis_size("sy") * lax.axis_size("sx") * lax.axis_size("ta")
    place = jnp.stack([index_bit(*CORE), quarter_index()]).astype(jnp.int32)
    gain_grad, qkv_grad, out_grad = finish_call(
        1.0 / tiles, [place, *quarters, *others, qkv_weight, layer_norm_gain]
    )
    shape = state_field.shape
    return (
        update.reshape(shape),
        field_grad.reshape(shape),
        qkv_grad,
        out_grad,
        gain_grad,
    )


def finish_call(scale, inputs):
    width = MODEL_WIDTH
    return local_call(
        functools.partial(finish_kernel, scale),
        [((width,), f32), ((width, 3 * width), f32), ((width, width), f32)],
        inputs,
        far_out=2,
        scratch=[
            ((8, width // 2, width), bf16),
            ((width, 3 * width), f32),
            ((width, width), f32),
        ],
        copies=4,
    )


def solution(mesh):
    in_specs = (
        P(("groups", "ta"), "sy", "sx", None),
        P(("groups", "ta"), "sy", "sx"),
        P(),
        P(),
        P(),
        P(),
        P(),
        P(("groups", "ta"), "sy", "sx", None),
    )
    out_specs = (
        P(("groups", "ta"), "sy", "sx", None),
        P(("groups", "ta"), "sy", "sx", None),
        P("groups", None),
        P("groups", None),
        P("groups"),
    )
    return jax.shard_map(shards, mesh=mesh, in_specs=in_specs, out_specs=out_specs, check_vma=False)
```

```python
import functools
import math

import jax
import jax.numpy as jnp
from jax import lax
from jax.experimental import pallas as pl
from jax.experimental.pallas import tpu as pltpu
from jax.sharding import PartitionSpec as P

MODEL_WIDTH = 384
HEADS = 6
HEAD_WIDTH = 64
RIM = 8
RELS = 2883
SIDE = 16
TOKENS = 512
HALF = 256
EPS = 1e-05
LOG2E = math.log2(math.e)

bf16 = jnp.bfloat16
f32 = jnp.float32


def nn(a, b):
    return lax.dot_general(a, b, (((1,), (0,)), ((), ())), preferred_element_type=f32)


def nt(a, b):
    return lax.dot_general(a, b, (((1,), (1,)), ((), ())), preferred_element_type=f32)


def tn(a, b):
    return lax.dot_general(a, b, (((0,), (0,)), ((), ())), preferred_element_type=f32)


def iota(shape, dim):
    return lax.broadcasted_iota(jnp.int32, shape, dim)


def prepare_kernel(position_bias, cot_far, out_far, weight_far, blank, *refs):
    blank[...] = jnp.zeros_like(blank)
    outs, (table, cot, out_weight, qkv_weight), refs = refs[:5], refs[5:9], refs[9:]
    bias_blocks, d_context_t, qkv_weight_t, sems = refs
    arrivals = [
        pltpu.make_async_copy(source, place, sems.at[5 + k])
        for k, (source, place) in enumerate(
            ((weight_far, qkv_weight), (out_far, out_weight), (cot_far, cot))
        )
    ]
    for copy in arrivals:
        copy.start()
    parts = [bias_blocks.at[k] for k in range(3)] + [d_context_t, qkv_weight_t]
    copies = [pltpu.make_async_copy(part, outs[k], sems.at[k]) for k, part in enumerate(parts)]
    table[...] = jnp.zeros_like(table)
    table[:HEADS, :RELS] = position_bias[...] * LOG2E
    plain = table[...]
    frames = [plain[:, :1024]] + [
        pltpu.roll(plain, plain.shape[1] - frame * 961, 1)[:, :1024] for frame in (1, 2)
    ]
    frames = jnp.concatenate(frames, 0)
    plain = jnp.concatenate([frames, pltpu.roll(frames, 31, 1)], 0)
    high = plain.astype(bf16)
    rest = plain - high.astype(f32)
    middle = rest.astype(bf16)
    low = (rest - middle.astype(f32)).astype(bf16)
    slot = iota((1, TOKENS), 1)
    source = 960 - 62 * (slot // 32) - slot % 32
    pick = (iota((1024, TOKENS), 0) == source).astype(f32).astype(bf16)
    turned = nn(jnp.concatenate([high, middle, low], 0), pick)
    turned = turned[:48] + turned[48:96] + turned[96:]
    lane = iota((SIDE, TOKENS), 1)
    for entry in range(HEADS * 3):
        head, frame = divmod(entry, 3)
        first = (2 - frame) * 8 + head
        even = jnp.broadcast_to(turned[first : first + 1, :], (SIDE, TOKENS))
        odd = jnp.broadcast_to(turned[24 + first : 25 + first, :], (SIDE, TOKENS))
        even = pltpu.roll(even, TOKENS - 15, 1, stride=1, stride_axis=0)
        odd = pltpu.roll(odd, 1, 1, stride=1, stride_axis=0)
        rows = jnp.where(lane % 32 < 16, even, odd)
        for row in range(SIDE):
            start = (15 - row) * SIDE
            bias_blocks[head // 2, entry % 6, row * SIDE : (row + 1) * SIDE, :] = rows[
                :, start : start + HALF
            ]
        if entry % 6 == 5:
            copies[head // 2].start()
        if entry == 5:
            arrivals[0].wait()
            qkv_weight_t[...] = qkv_weight[...].T
            copies[4].start()
        if entry == 11:
            arrivals[1].wait()
            arrivals[2].wait()
            d_context_t[...] = nt(out_weight[...], cot[...]).astype(bf16)
            copies[3].start()
    for copy in copies:
        copy.wait()


def source_onehots(row_shift, col_shift, sign):
    token = iota((HALF, 1), 0)
    row = token // SIDE + sign * row_shift
    col = token % SIDE + sign * col_shift
    if sign > 0:
        row_out, col_out = row >= SIDE, col >= SIDE
        near_row, near_col, span = row - SIDE, col - SIDE, SIDE
    else:
        row_out, col_out = row < 0, col < 0
        near_row, near_col, span = row + RIM, col + RIM, RIM
    inner = jnp.where(row_out | col_out, -1, row * SIDE + col)
    rows = jnp.where(row_out & ~col_out, near_row * SIDE + col, -1)
    cols = jnp.where(col_out & ~row_out, row * span + near_col, -1)
    corner = jnp.where(row_out & col_out, near_row * RIM + near_col, -1)
    return [
        (iota((HALF, count), 1) == place).astype(f32).astype(bf16)
        for place, count in ((inner, HALF), (rows, 128), (cols, SIDE * span), (corner, 64))
    ]


def flag_strip(flags, count, span=SIDE):
    total = count * span
    repeat = (iota((SIDE, total), 1) % span == iota((SIDE, total), 0)).astype(f32).astype(bf16)
    spread = nn(flags[:count, :].astype(bf16), repeat)
    keep = iota((count, total), 1) // span == iota((count, total), 0)
    strip = jnp.sum(jnp.where(keep, spread, 0.0), 0, keepdims=True)
    return jnp.broadcast_to(strip, (128, total)).astype(bf16)


def layer_norm(rolled):
    centred = rolled - jnp.mean(rolled, -1, keepdims=True)
    inv_std = lax.rsqrt(jnp.mean(centred * centred, -1, keepdims=True) + EPS)
    return centred * inv_std, inv_std


def attention_head(head, qkv_t, kv, penalty, bias_blocks, d_context_t):
    pair, side = divmod(head, 2)
    at = head * HEAD_WIDTH
    scale = LOG2E * HEAD_WIDTH ** (-0.5)
    zeros = jnp.zeros((HEAD_WIDTH, TOKENS), bf16)
    key_pair = kv[:, pair * 128 : pair * 128 + 128]
    value_pair = kv[:, MODEL_WIDTH + pair * 128 : MODEL_WIDTH + pair * 128 + 128]
    q_t = qkv_t[at : at + HEAD_WIDTH, :]
    k_t = qkv_t[MODEL_WIDTH + at : MODEL_WIDTH + at + HEAD_WIDTH, :]
    v_t = qkv_t[2 * MODEL_WIDTH + at : 2 * MODEL_WIDTH + at + HEAD_WIDTH, :]
    d_t = d_context_t[at : at + HEAD_WIDTH, :]
    d_eighth = d_t * 0.125
    q_wide = jnp.concatenate([q_t, zeros] if side == 0 else [zeros, q_t], 0)
    d_wide = jnp.concatenate([d_eighth, zeros] if side == 0 else [zeros, d_eighth], 0)
    context_parts = []
    dq_parts = []
    dk_parts = [0.0, 0.0]
    dv_parts = [0.0, 0.0]
    for b in range(2):
        lanes = slice(b * HALF, (b + 1) * HALF)
        scores = nn(key_pair, q_wide[:, lanes])
        d_probs = nn(value_pair, d_wide[:, lanes])
        halves = [slice(a * HALF, (a + 1) * HALF) for a in range(2)]
        s = [
            scores[halves[a]] * scale
            + bias_blocks[side * 3 + b - a + 1]
            + penalty[halves[a], lanes]
            for a in range(2)
        ]
        top = jnp.maximum(jnp.max(s[0], 0, keepdims=True), jnp.max(s[1], 0, keepdims=True))
        e = [jnp.exp2(s[a] - top) for a in range(2)]
        total = jnp.sum(e[0], 0, keepdims=True) + jnp.sum(e[1], 0, keepdims=True)
        inverse = 1.0 / total
        p = [e[a] * inverse for a in range(2)]
        pb = [p[a].astype(bf16) for a in range(2)]
        context_parts.append(nn(v_t[:, :HALF], pb[0]) + nn(v_t[:, HALF:], pb[1]))
        dp = [d_probs[halves[a]] for a in range(2)]
        delta = jnp.sum(p[0] * dp[0], 0, keepdims=True) + jnp.sum(p[1] * dp[1], 0, keepdims=True)
        ds = [(p[a] * (dp[a] - delta)).astype(bf16) for a in range(2)]
        dq_parts.append(nn(k_t[:, :HALF], ds[0]) + nn(k_t[:, HALF:], ds[1]))
        for a in range(2):
            dk_parts[a] = dk_parts[a] + nt(q_t[:, lanes], ds[a])
            dv_parts[a] = dv_parts[a] + nt(d_t[:, lanes], pb[a])
    return [
        jnp.concatenate(parts, 1).astype(bf16)
        for parts in (context_parts, dq_parts, dk_parts, dv_parts)
    ]


def main_kernel(
    shift,
    core,
    inner_flags,
    col_flags,
    gain,
    inner_far,
    rows_far,
    cols_far,
    corner_far,
    weight_far,
    weight_t_far,
    d_context_far,
    bias0_far,
    cot_far,
    bias1_far,
    bias2_far,
    out_weight_far,
    keep_far,
    send_far,
    d_rolled_far,
    update_far,
    lower_far,
    right_far,
    penalty,
    inner,
    rows,
    cols,
    corner,
    qkv_weight,
    qkv_weight_t,
    d_context_t,
    bias_blocks,
    cot,
    context_t,
    d_qkv,
    grads,
    d_rolled,
    right,
    out_weight,
    update,
    sems,
):
    sources = (inner_far, rows_far, cols_far, corner_far, weight_far, weight_t_far)
    sources += (d_context_far, bias0_far, cot_far, bias1_far, bias2_far)
    sources += (out_weight_far,)
    places = [inner, rows, cols, corner, qkv_weight, qkv_weight_t]
    places += [d_context_t, bias_blocks.at[0], cot, bias_blocks.at[1], bias_blocks.at[2]]
    places.append(out_weight)
    arrivals = [
        pltpu.make_async_copy(source, place, sems.at[k])
        for k, (source, place) in enumerate(zip(sources, places))
    ]
    for copy in arrivals:
        copy.start()
    onehots = source_onehots(shift[0], shift[1], 1)
    for copy in arrivals[:4]:
        copy.wait()
    rolled = []
    for t in range(2):
        parts = (
            inner[t * 256 : t * 256 + 256, :],
            rows[t * 128 : t * 128 + 128, :],
            cols[t * 256 : t * 256 + 256, :],
            corner[t * 64 : t * 64 + 64, :],
        )
        rolled.append(sum(nn(hot, part) for hot, part in zip(onehots, parts)))
    xhat, inv_std = layer_norm(jnp.concatenate(rolled, 0))
    gain_row = gain[...].reshape(1, MODEL_WIDTH)
    normed = (xhat * gain_row).astype(bf16)
    normed_t = normed.T
    arrivals[4].wait()
    arrivals[5].wait()
    kv = nn(normed, qkv_weight[:, MODEL_WIDTH:]).astype(bf16)
    qkv_t = nt(qkv_weight_t[...], normed).astype(bf16)
    on_diagonal = iota((HALF, HALF), 0) == iota((HALF, HALF), 1)
    for t in range(2):
        strips = (
            flag_strip(inner_flags[t].astype(f32), SIDE),
            flag_strip(rows[256:272, :SIDE][t * RIM : (t + 1) * RIM], RIM),
            flag_strip(col_flags[t].astype(f32), SIDE),
            flag_strip(corner[128:144, :SIDE][t * RIM : (t + 1) * RIM], RIM, RIM),
        )
        marks = sum(nt(hot, strip) for hot, strip in zip(onehots, strips))
        column = jnp.where(marks > 0.5, -1e30, 0.0)
        wide = jnp.concatenate([column, column], 1)
        own = jnp.where(on_diagonal, 0.0, wide)
        penalty[t * HALF : (t + 1) * HALF, t * HALF : (t + 1) * HALF] = own
        penalty[t * HALF : (t + 1) * HALF, (1 - t) * HALF : (2 - t) * HALF] = wide
    for copy in arrivals[6:]:
        copy.wait()
    for pair in range(HEADS // 2):
        heads = [
            attention_head(2 * pair + side, qkv_t, kv, penalty, bias_blocks.at[pair], d_context_t)
            for side in range(2)
        ]
        context, *d_parts = [jnp.concatenate(both, 0) for both in zip(*heads)]
        context_t[pair * 128 : pair * 128 + 128, :] = context
        d_pair = jnp.concatenate([part.T for part in d_parts], 1)
        for kind in range(3):
            first = kind * MODEL_WIDTH + pair * 128
            d_qkv[:, first : first + 128] = d_pair[:, kind * 128 : kind * 128 + 128]
        first = pair * TOKENS
        grads[first : first + 128, :] = nn(context, cot[...]).astype(bf16)
        grads[first + 128 : first + TOKENS, :] = nn(normed_t, d_pair).astype(bf16)
    for block in range(6):
        to_half(grads, block, core[0], keep_far, send_far, sems)
    d_xhat = nt(d_qkv[...], qkv_weight[...]) * gain_row
    d_tokens = inv_std * (
        d_xhat
        - jnp.mean(d_xhat, -1, keepdims=True)
        - xhat * jnp.mean(d_xhat * xhat, -1, keepdims=True)
    )
    d_rolled[...] = d_tokens.astype(bf16)
    last_columns = d_tokens.reshape(2 * SIDE, SIDE, MODEL_WIDTH)[:, RIM:, :]
    update[...] = tn(context_t[...], out_weight[...]).astype(bf16)
    right[...] = last_columns.reshape(HALF, MODEL_WIDTH).astype(bf16)
    copies = [
        pltpu.make_async_copy(d_rolled, d_rolled_far, sems.at[1]),
        pltpu.make_async_copy(right, right_far, sems.at[2]),
        pltpu.make_async_copy(update, update_far, sems.at[0]),
    ]
    for t in range(2):
        source = d_rolled.at[pl.ds(t * HALF + 128, 128), :]
        target = lower_far.at[pl.ds(t * 128, 128), :]
        copies.append(pltpu.make_async_copy(source, target, sems.at[3 + t]))
    for copy in copies:
        copy.start()
    for block in range(6):
        source, target = half_block(grads, block, keep_far)
        pltpu.make_async_copy(source, target, sems.at[12 + block]).wait()
    for copy in copies:
        copy.wait()


def half_block(grads, block, half):
    place = block % 3 * HALF
    return grads.at[pl.ds(block * HALF, HALF), :], half.at[pl.ds(place, HALF), :]


def to_half(grads, block, core, keep_far, send_far, sems):
    for half, side in ((keep_far, block // 3), (send_far, 1 - block // 3)):

        @pl.when(core == side)
        def _():
            source, target = half_block(grads, block, half)
            pltpu.make_async_copy(source, target, sems.at[12 + block]).start()


def place_kernel(shift, halo, kept_far, field_grad, kept, sems):
    copy = pltpu.make_async_copy(kept_far, kept, sems.at[0])
    copy.start()
    onehots = source_onehots(shift[0], shift[1], -1)
    copy.wait()
    for t in range(2):
        parts = (
            kept[t * 256 : t * 256 + 256, :],
            halo[t * 128 : t * 128 + 128, :],
            halo[256 + t * 128 : 384 + t * 128, :],
            halo[512 + t * 64 : 576 + t * 64, :],
        )
        field_grad[t * 256 : t * 256 + 256, :] = sum(
            nn(hot, part) for hot, part in zip(onehots, parts)
        ).astype(bf16)


def finish_kernel(scale, place, *refs):
    mine, other, (weight, gain) = refs[:4], refs[4:8], refs[8:10]
    gain_grad, qkv_far, out_far, shares, qkv_grad, out_grad, sems = refs[10:]
    for side, group in ((place[0], mine), (1 - place[0], other)):
        for offset in range(4):
            shares[side * 4 + (offset ^ place[1])] = group[offset][...]
    whole = shares[...].reshape(3 * TOKENS, MODEL_WIDTH).astype(f32) * scale
    copies = []
    partial = 0.0
    for kind in range(3):
        columns = slice(kind * MODEL_WIDTH, (kind + 1) * MODEL_WIDTH)
        block = jnp.concatenate(
            [
                whole[pair * TOKENS + 128 : (pair + 1) * TOKENS, kind * 128 : kind * 128 + 128]
                for pair in range(3)
            ],
            1,
        )
        qkv_grad[:, columns] = block
        copies.append(
            pltpu.make_async_copy(
                qkv_grad.at[:, columns], qkv_far.at[:, columns], sems.at[kind]
            )
        )
        copies[-1].start()
    for pair in range(3):
        out_grad[pair * 128 : pair * 128 + 128, :] = whole[pair * TOKENS : pair * TOKENS + 128]
    copies.append(pltpu.make_async_copy(out_grad, out_far, sems.at[3]))
    copies[-1].start()
    for kind in range(3):
        columns = slice(kind * MODEL_WIDTH, (kind + 1) * MODEL_WIDTH)
        product = qkv_grad[:, columns] * weight[:, columns].astype(f32)
        partial = partial + product[:, :128] + product[:, 128:256] + product[:, 256:]
    gain_row = gain[...].reshape(1, MODEL_WIDTH)
    gain_grad[...] = (jnp.sum(partial.T, 0, keepdims=True) / gain_row).reshape(MODEL_WIDTH)
    for copy in copies:
        copy.wait()


def local_call(
    kernel, shapes, inputs, far_in=0, far_out=0, scratch=(), copies=0, micros=1, limit=24
):
    vmem = pl.BlockSpec(memory_space=pltpu.VMEM)
    smem = pl.BlockSpec(memory_space=pltpu.SMEM)
    far = pl.BlockSpec(memory_space=pl.ANY)
    near = inputs[: len(inputs) - far_in]
    return pl.pallas_call(
        kernel,
        out_shape=[jax.ShapeDtypeStruct(shape, dtype) for shape, dtype in shapes],
        in_specs=[smem if array.dtype == jnp.int32 and array.ndim == 1 else vmem for array in near]
        + [far] * far_in,
        out_specs=[vmem] * (len(shapes) - far_out) + [far] * far_out,
        scratch_shapes=[pltpu.VMEM(shape, dtype) for shape, dtype in scratch]
        + [pltpu.SemaphoreType.DMA((copies,))],
        compiler_params=pltpu.CompilerParams(vmem_limit_bytes=limit * 2**20),
        cost_estimate=pl.CostEstimate(
            flops=micros * 10**9, bytes_accessed=10**6, transcendentals=0
        ),
    )(*inputs)


def passed_along(block, axis, distance):
    count = lax.axis_size(axis)
    return lax.ppermute(block, axis, [((i - distance) % count, i) for i in range(count)])


CORE = ("sx", 1)
GROUPS = ([("sy", 1)], [("ta", 1)], [("sy", 1), ("ta", 1)])


def index_bit(axis, bit):
    return (lax.axis_index(axis) & bit) // bit


def swapped(block, *bits):
    axes = tuple(axis for axis, _ in bits)
    sizes = [lax.axis_size(axis) for axis in axes]
    route = []
    for source in range(math.prod(sizes)):
        rest, places = source, []
        for size in sizes[::-1]:
            rest, place = divmod(rest, size)
            places.append(place)
        target = 0
        for size, place, (_, bit) in zip(sizes, places[::-1], bits):
            target = target * size + (place ^ bit)
        route.append((source, target))
    return lax.ppermute(block, axes, route)


def add_up(*pieces):
    return sum(piece.astype(f32) for piece in pieces).astype(bf16)


def sum_quarter(keep, send, below):
    kept = lax.optimization_barrier(keep.astype(f32))
    block = add_up(kept, swapped(send, CORE))
    share = block.shape[0] // 4
    mine = quarter_index()
    pick = lambda array, place: lax.dynamic_slice_in_dim(array, place * share, share, 0)
    late = pick(lax.optimization_barrier(block), mine ^ 3) + below[:share] * 0
    pieces = [pick(block, mine ^ 1), pick(block, mine ^ 2), late]
    arrived = [swapped(piece, *group) for piece, group in zip(pieces, GROUPS)]
    return add_up(pick(block, mine), *arrived)


def sum_rest(quarter):
    rest = [
        (axis, 1 << k)
        for axis in ("ta", "sy")
        for k in range(1, lax.axis_size(axis).bit_length() - 1)
    ]
    for bit in rest:
        quarter = add_up(quarter, swapped(quarter, bit))
    return quarter


def quarter_index():
    return 2 * index_bit("ta", 1) + index_bit("sy", 1)


def shards(
    state_field,
    outlier_flags,
    window_shift,
    layer_norm_gain,
    qkv_weight,
    out_weight,
    position_bias,
    cotangent,
):
    width = MODEL_WIDTH
    wide = lambda tokens: ((tokens, width), bf16)
    row_flags = outlier_flags[:, :RIM].reshape(2 * RIM, SIDE).astype(bf16)
    row_message = jnp.concatenate(
        [
            state_field[:, :RIM].reshape(-1, width),
            jnp.pad(row_flags, ((0, 0), (0, width - SIDE))),
        ],
        0,
    )
    rows = passed_along(row_message, "sy", -1)
    cols = passed_along(state_field, "sx", -1)
    col_flags = passed_along(outlier_flags, "sx", -1)
    cot_rows = cotangent.reshape(TOKENS, width)
    pair_bias = ((6, HALF, HALF), f32)
    blank, *bias_blocks, d_context_t, qkv_weight_t = local_call(
        prepare_kernel,
        [wide(16)] + [pair_bias] * 3 + [((width, TOKENS), bf16), wide(3 * width)],
        [position_bias, cot_rows, out_weight, qkv_weight],
        far_in=3,
        far_out=5,
        scratch=[
            ((8, 3072), f32),
            wide(TOKENS),
            wide(width),
            ((width, 3 * width), bf16),
            ((3, 6, HALF, HALF), f32),
            ((width, TOKENS), bf16),
            wide(3 * width),
        ],
        copies=8,
        micros=3,
        limit=62,
    )
    corner_message = jnp.concatenate(
        [
            rows[: 2 * RIM * SIDE].reshape(2 * RIM, SIDE, width)[:, :RIM].reshape(-1, width),
            rows[2 * RIM * SIDE :] + blank,
        ],
        0,
    )
    corner = passed_along(corner_message, "sx", -1)
    core = index_bit(*CORE).astype(jnp.int32).reshape(1)
    keep, send, d_rolled, update, lower, right = local_call(
        main_kernel,
        [wide(2 * width)] * 2
        + [wide(TOKENS), wide(TOKENS), wide(HALF), wide(HALF)],
        [
            window_shift,
            core,
            outlier_flags,
            col_flags,
            layer_norm_gain,
            state_field.reshape(TOKENS, width),
            rows,
            cols.reshape(TOKENS, width),
            corner,
            qkv_weight,
            qkv_weight_t,
            d_context_t,
            bias_blocks[0],
            cot_rows,
            bias_blocks[1],
            bias_blocks[2],
            out_weight,
        ],
        far_in=12,
        far_out=6,
        scratch=[
            ((TOKENS, TOKENS), f32),
            wide(TOKENS),
            wide(HALF + 16),
            wide(TOKENS),
            wide(144),
            ((width, 3 * width), bf16),
            wide(3 * width),
            ((width, TOKENS), bf16),
            ((3, 6, HALF, HALF), f32),
            wide(TOKENS),
            ((width, TOKENS), bf16),
            ((TOKENS, 3 * width), bf16),
            wide(3 * TOKENS),
            wide(TOKENS),
            wide(HALF),
            wide(width),
            wide(TOKENS),
        ],
        copies=18,
        micros=12,
        limit=62,
    )
    below = passed_along(lower, "sy", 1)
    beside = passed_along(right, "sx", 1)
    across = passed_along(
        below.reshape(2 * RIM, SIDE, width)[:, RIM:].reshape(-1, width), "sx", 1
    )
    quarter = sum_quarter(keep, send, below)
    (field_grad,) = local_call(
        place_kernel,
        [wide(TOKENS)],
        [window_shift, jnp.concatenate([below, beside, across], 0), d_rolled],
        far_in=1,
        scratch=[wide(TOKENS)],
        copies=1,
        micros=2,
    )
    quarter = sum_rest(quarter)
    quarters = [quarter] + [swapped(quarter, *group) for group in GROUPS]
    others = [swapped(piece, CORE) for piece in quarters]
    tiles = lax.axis_size("sy") * lax.axis_size("sx") * lax.axis_size("ta")
    place = jnp.stack([index_bit(*CORE), quarter_index()]).astype(jnp.int32)
    gain_grad, qkv_grad, out_grad = finish_call(
        1.0 / tiles, [place, *quarters, *others, qkv_weight, layer_norm_gain]
    )
    shape = state_field.shape
    return (
        update.reshape(shape),
        field_grad.reshape(shape),
        qkv_grad,
        out_grad,
        gain_grad,
    )


def finish_call(scale, inputs):
    width = MODEL_WIDTH
    return local_call(
        functools.partial(finish_kernel, scale),
        [((width,), f32), ((width, 3 * width), f32), ((width, width), f32)],
        inputs,
        far_out=2,
        scratch=[
            ((8, width // 2, width), bf16),
            ((width, 3 * width), f32),
            ((width, width), f32),
        ],
        copies=4,
    )


def solution(mesh):
    in_specs = (
        P(("groups", "ta"), "sy", "sx", None),
        P(("groups", "ta"), "sy", "sx"),
        P(),
        P(),
        P(),
        P(),
        P(),
        P(("groups", "ta"), "sy", "sx", None),
    )
    out_specs = (
        P(("groups", "ta"), "sy", "sx", None),
        P(("groups", "ta"), "sy", "sx", None),
        P("groups", None),
        P("groups", None),
        P("groups"),
    )
    return jax.shard_map(shards, mesh=mesh, in_specs=in_specs, out_specs=out_specs, check_vma=False)
```

```python
import functools
import math

import jax
import jax.numpy as jnp
from jax import lax
from jax.experimental import pallas as pl
from jax.experimental.pallas import tpu as pltpu
from jax.sharding import PartitionSpec as P

MODEL_WIDTH = 384
HEADS = 6
HEAD_WIDTH = 64
RIM = 8
RELS = 2883
SIDE = 16
TOKENS = 512
HALF = 256
EPS = 1e-05
LOG2E = math.log2(math.e)

bf16 = jnp.bfloat16
f32 = jnp.float32


def nn(a, b):
    return lax.dot_general(a, b, (((1,), (0,)), ((), ())), preferred_element_type=f32)


def nt(a, b):
    return lax.dot_general(a, b, (((1,), (1,)), ((), ())), preferred_element_type=f32)


def tn(a, b):
    return lax.dot_general(a, b, (((0,), (0,)), ((), ())), preferred_element_type=f32)


def iota(shape, dim):
    return lax.broadcasted_iota(jnp.int32, shape, dim)


def prepare_kernel(position_bias, cot_far, out_far, weight_far, blank, *refs):
    blank[...] = jnp.zeros_like(blank)
    outs, (table, cot, out_weight, qkv_weight), refs = refs[:5], refs[5:9], refs[9:]
    bias_blocks, d_context_t, qkv_weight_t, sems = refs
    arrivals = [
        pltpu.make_async_copy(source, place, sems.at[5 + k])
        for k, (source, place) in enumerate(
            ((weight_far, qkv_weight), (out_far, out_weight), (cot_far, cot))
        )
    ]
    for copy in arrivals:
        copy.start()
    parts = [bias_blocks.at[k] for k in range(3)] + [d_context_t, qkv_weight_t]
    copies = [pltpu.make_async_copy(part, outs[k], sems.at[k]) for k, part in enumerate(parts)]
    table[...] = jnp.zeros_like(table)
    table[:HEADS, :RELS] = position_bias[...] * LOG2E
    plain = table[...]
    frames = [plain[:, :1024]] + [
        pltpu.roll(plain, plain.shape[1] - frame * 961, 1)[:, :1024] for frame in (1, 2)
    ]
    frames = jnp.concatenate(frames, 0)
    plain = jnp.concatenate([frames, pltpu.roll(frames, 31, 1)], 0)
    high = plain.astype(bf16)
    rest = plain - high.astype(f32)
    middle = rest.astype(bf16)
    low = (rest - middle.astype(f32)).astype(bf16)
    slot = iota((1, TOKENS), 1)
    source = 960 - 62 * (slot // 32) - slot % 32
    pick = (iota((1024, TOKENS), 0) == source).astype(f32).astype(bf16)
    turned = nn(jnp.concatenate([high, middle, low], 0), pick)
    turned = turned[:48] + turned[48:96] + turned[96:]
    lane = iota((SIDE, TOKENS), 1)
    for entry in range(HEADS * 3):
        head, frame = divmod(entry, 3)
        first = (2 - frame) * 8 + head
        even = jnp.broadcast_to(turned[first : first + 1, :], (SIDE, TOKENS))
        odd = jnp.broadcast_to(turned[24 + first : 25 + first, :], (SIDE, TOKENS))
        even = pltpu.roll(even, TOKENS - 15, 1, stride=1, stride_axis=0)
        odd = pltpu.roll(odd, 1, 1, stride=1, stride_axis=0)
        rows = jnp.where(lane % 32 < 16, even, odd)
        for row in range(SIDE):
            start = (15 - row) * SIDE
            bias_blocks[head // 2, entry % 6, row * SIDE : (row + 1) * SIDE, :] = rows[
                :, start : start + HALF
            ]
        if entry % 6 == 5:
            copies[head // 2].start()
        if entry == 5:
            arrivals[0].wait()
            qkv_weight_t[...] = qkv_weight[...].T
            copies[4].start()
        if entry == 11:
            arrivals[1].wait()
            arrivals[2].wait()
            d_context_t[...] = nt(out_weight[...], cot[...]).astype(bf16)
            copies[3].start()
    for copy in copies:
        copy.wait()


def source_onehots(row_shift, col_shift, sign):
    token = iota((HALF, 1), 0)
    row = token // SIDE + sign * row_shift
    col = token % SIDE + sign * col_shift
    if sign > 0:
        row_out, col_out = row >= SIDE, col >= SIDE
        near_row, near_col, span = row - SIDE, col - SIDE, SIDE
    else:
        row_out, col_out = row < 0, col < 0
        near_row, near_col, span = row + RIM, col + RIM, RIM
    inner = jnp.where(row_out | col_out, -1, row * SIDE + col)
    rows = jnp.where(row_out & ~col_out, near_row * SIDE + col, -1)
    cols = jnp.where(col_out & ~row_out, row * span + near_col, -1)
    corner = jnp.where(row_out & col_out, near_row * RIM + near_col, -1)
    return [
        (iota((HALF, count), 1) == place).astype(f32).astype(bf16)
        for place, count in ((inner, HALF), (rows, 128), (cols, SIDE * span), (corner, 64))
    ]


def flag_strip(flags, count, span=SIDE):
    total = count * span
    repeat = (iota((SIDE, total), 1) % span == iota((SIDE, total), 0)).astype(f32).astype(bf16)
    spread = nn(flags[:count, :].astype(bf16), repeat)
    keep = iota((count, total), 1) // span == iota((count, total), 0)
    strip = jnp.sum(jnp.where(keep, spread, 0.0), 0, keepdims=True)
    return jnp.broadcast_to(strip, (128, total)).astype(bf16)


def layer_norm(rolled):
    centred = rolled - jnp.mean(rolled, -1, keepdims=True)
    inv_std = lax.rsqrt(jnp.mean(centred * centred, -1, keepdims=True) + EPS)
    return centred * inv_std, inv_std


def attention_head(head, qkv_t, kv, penalty, bias_blocks, d_context_t):
    pair, side = divmod(head, 2)
    at = head * HEAD_WIDTH
    scale = LOG2E * HEAD_WIDTH ** (-0.5)
    zeros = jnp.zeros((HEAD_WIDTH, TOKENS), bf16)
    key_pair = kv[:, pair * 128 : pair * 128 + 128]
    value_pair = kv[:, MODEL_WIDTH + pair * 128 : MODEL_WIDTH + pair * 128 + 128]
    q_t = qkv_t[at : at + HEAD_WIDTH, :]
    k_t = qkv_t[MODEL_WIDTH + at : MODEL_WIDTH + at + HEAD_WIDTH, :]
    v_t = qkv_t[2 * MODEL_WIDTH + at : 2 * MODEL_WIDTH + at + HEAD_WIDTH, :]
    d_t = d_context_t[at : at + HEAD_WIDTH, :]
    d_eighth = d_t * 0.125
    q_wide = jnp.concatenate([q_t, zeros] if side == 0 else [zeros, q_t], 0)
    d_wide = jnp.concatenate([d_eighth, zeros] if side == 0 else [zeros, d_eighth], 0)
    context_parts = []
    dq_parts = []
    dk_parts = [0.0, 0.0]
    dv_parts = [0.0, 0.0]
    for b in range(2):
        lanes = slice(b * HALF, (b + 1) * HALF)
        scores = nn(key_pair, q_wide[:, lanes])
        d_probs = nn(value_pair, d_wide[:, lanes])
        halves = [slice(a * HALF, (a + 1) * HALF) for a in range(2)]
        s = [
            scores[halves[a]] * scale
            + bias_blocks[side * 3 + b - a + 1]
            + penalty[halves[a], lanes]
            for a in range(2)
        ]
        top = jnp.maximum(jnp.max(s[0], 0, keepdims=True), jnp.max(s[1], 0, keepdims=True))
        e = [jnp.exp2(s[a] - top) for a in range(2)]
        total = jnp.sum(e[0], 0, keepdims=True) + jnp.sum(e[1], 0, keepdims=True)
        inverse = 1.0 / total
        p = [e[a] * inverse for a in range(2)]
        pb = [p[a].astype(bf16) for a in range(2)]
        context_parts.append(nn(v_t[:, :HALF], pb[0]) + nn(v_t[:, HALF:], pb[1]))
        dp = [d_probs[halves[a]] for a in range(2)]
        delta = jnp.sum(p[0] * dp[0], 0, keepdims=True) + jnp.sum(p[1] * dp[1], 0, keepdims=True)
        ds = [(p[a] * (dp[a] - delta)).astype(bf16) for a in range(2)]
        dq_parts.append(nn(k_t[:, :HALF], ds[0]) + nn(k_t[:, HALF:], ds[1]))
        for a in range(2):
            dk_parts[a] = dk_parts[a] + nt(q_t[:, lanes], ds[a])
            dv_parts[a] = dv_parts[a] + nt(d_t[:, lanes], pb[a])
    return [
        jnp.concatenate(parts, 1).astype(bf16)
        for parts in (context_parts, dq_parts, dk_parts, dv_parts)
    ]


def main_kernel(
    shift,
    core,
    inner_flags,
    col_flags,
    gain,
    inner_far,
    rows_far,
    cols_far,
    corner_far,
    weight_far,
    weight_t_far,
    d_context_far,
    bias0_far,
    cot_far,
    bias1_far,
    bias2_far,
    out_weight_far,
    keep_far,
    send_far,
    d_rolled_far,
    update_far,
    lower_far,
    right_far,
    penalty,
    inner,
    rows,
    cols,
    corner,
    qkv_weight,
    qkv_weight_t,
    d_context_t,
    bias_blocks,
    cot,
    context_t,
    d_qkv,
    grads,
    d_rolled,
    right,
    out_weight,
    update,
    sems,
):
    sources = (inner_far, rows_far, cols_far, corner_far, weight_far, weight_t_far)
    sources += (d_context_far, bias0_far, cot_far, bias1_far, bias2_far)
    sources += (out_weight_far,)
    places = [inner, rows, cols, corner, qkv_weight, qkv_weight_t]
    places += [d_context_t, bias_blocks.at[0], cot, bias_blocks.at[1], bias_blocks.at[2]]
    places.append(out_weight)
    arrivals = [
        pltpu.make_async_copy(source, place, sems.at[k])
        for k, (source, place) in enumerate(zip(sources, places))
    ]
    for copy in arrivals:
        copy.start()
    onehots = source_onehots(shift[0], shift[1], 1)
    for copy in arrivals[:4]:
        copy.wait()
    rolled = []
    for t in range(2):
        parts = (
            inner[t * 256 : t * 256 + 256, :],
            rows[t * 128 : t * 128 + 128, :],
            cols[t * 256 : t * 256 + 256, :],
            corner[t * 64 : t * 64 + 64, :],
        )
        rolled.append(sum(nn(hot, part) for hot, part in zip(onehots, parts)))
    xhat, inv_std = layer_norm(jnp.concatenate(rolled, 0))
    gain_row = gain[...].reshape(1, MODEL_WIDTH)
    normed = (xhat * gain_row).astype(bf16)
    normed_t = normed.T
    arrivals[4].wait()
    arrivals[5].wait()
    kv = nn(normed, qkv_weight[:, MODEL_WIDTH:]).astype(bf16)
    qkv_t = nt(qkv_weight_t[...], normed).astype(bf16)
    on_diagonal = iota((HALF, HALF), 0) == iota((HALF, HALF), 1)
    for t in range(2):
        strips = (
            flag_strip(inner_flags[t].astype(f32), SIDE),
            flag_strip(rows[256:272, :SIDE][t * RIM : (t + 1) * RIM], RIM),
            flag_strip(col_flags[t].astype(f32), SIDE),
            flag_strip(corner[128:144, :SIDE][t * RIM : (t + 1) * RIM], RIM, RIM),
        )
        marks = sum(nt(hot, strip) for hot, strip in zip(onehots, strips))
        column = jnp.where(marks > 0.5, -1e30, 0.0)
        wide = jnp.concatenate([column, column], 1)
        own = jnp.where(on_diagonal, 0.0, wide)
        penalty[t * HALF : (t + 1) * HALF, t * HALF : (t + 1) * HALF] = own
        penalty[t * HALF : (t + 1) * HALF, (1 - t) * HALF : (2 - t) * HALF] = wide
    for copy in arrivals[6:]:
        copy.wait()
    for pair in range(HEADS // 2):
        heads = [
            attention_head(2 * pair + side, qkv_t, kv, penalty, bias_blocks.at[pair], d_context_t)
            for side in range(2)
        ]
        context, *d_parts = [jnp.concatenate(both, 0) for both in zip(*heads)]
        context_t[pair * 128 : pair * 128 + 128, :] = context
        d_pair = jnp.concatenate([part.T for part in d_parts], 1)
        for kind in range(3):
            first = kind * MODEL_WIDTH + pair * 128
            d_qkv[:, first : first + 128] = d_pair[:, kind * 128 : kind * 128 + 128]
        first = pair * TOKENS
        grads[first : first + 128, :] = nn(context, cot[...]).astype(bf16)
        grads[first + 128 : first + TOKENS, :] = nn(normed_t, d_pair).astype(bf16)
    for block in range(6):
        to_half(grads, block, core[0], keep_far, send_far, sems)
    d_xhat = nt(d_qkv[...], qkv_weight[...]) * gain_row
    d_tokens = inv_std * (
        d_xhat
        - jnp.mean(d_xhat, -1, keepdims=True)
        - xhat * jnp.mean(d_xhat * xhat, -1, keepdims=True)
    )
    d_rolled[...] = d_tokens.astype(bf16)
    last_columns = d_tokens.reshape(2 * SIDE, SIDE, MODEL_WIDTH)[:, RIM:, :]
    update[...] = tn(context_t[...], out_weight[...]).astype(bf16)
    right[...] = last_columns.reshape(HALF, MODEL_WIDTH).astype(bf16)
    copies = [
        pltpu.make_async_copy(d_rolled, d_rolled_far, sems.at[1]),
        pltpu.make_async_copy(right, right_far, sems.at[2]),
        pltpu.make_async_copy(update, update_far, sems.at[0]),
    ]
    for t in range(2):
        source = d_rolled.at[pl.ds(t * HALF + 128, 128), :]
        target = lower_far.at[pl.ds(t * 128, 128), :]
        copies.append(pltpu.make_async_copy(source, target, sems.at[3 + t]))
    for copy in copies:
        copy.start()
    for block in range(6):
        source, target = half_block(grads, block, keep_far)
        pltpu.make_async_copy(source, target, sems.at[12 + block]).wait()
    for copy in copies:
        copy.wait()


def half_block(grads, block, half):
    place = block % 3 * HALF
    return grads.at[pl.ds(block * HALF, HALF), :], half.at[pl.ds(place, HALF), :]


def to_half(grads, block, core, keep_far, send_far, sems):
    for half, side in ((keep_far, block // 3), (send_far, 1 - block // 3)):

        @pl.when(core == side)
        def _():
            source, target = half_block(grads, block, half)
            pltpu.make_async_copy(source, target, sems.at[12 + block]).start()


def place_kernel(shift, halo, kept_far, field_grad, kept, sems):
    copy = pltpu.make_async_copy(kept_far, kept, sems.at[0])
    copy.start()
    onehots = source_onehots(shift[0], shift[1], -1)
    copy.wait()
    for t in range(2):
        parts = (
            kept[t * 256 : t * 256 + 256, :],
            halo[t * 128 : t * 128 + 128, :],
            halo[256 + t * 128 : 384 + t * 128, :],
            halo[512 + t * 64 : 576 + t * 64, :],
        )
        field_grad[t * 256 : t * 256 + 256, :] = sum(
            nn(hot, part) for hot, part in zip(onehots, parts)
        ).astype(bf16)


def finish_kernel(scale, place, *refs):
    mine, other, (weight, gain) = refs[:4], refs[4:8], refs[8:10]
    gain_grad, qkv_far, out_far, shares, qkv_grad, out_grad, sems = refs[10:]
    for side, group in ((place[0], mine), (1 - place[0], other)):
        for offset in range(4):
            shares[side * 4 + (offset ^ place[1])] = group[offset][...]
    whole = shares[...].reshape(3 * TOKENS, MODEL_WIDTH).astype(f32) * scale
    copies = []
    partial = 0.0
    for kind in range(3):
        columns = slice(kind * MODEL_WIDTH, (kind + 1) * MODEL_WIDTH)
        block = jnp.concatenate(
            [
                whole[pair * TOKENS + 128 : (pair + 1) * TOKENS, kind * 128 : kind * 128 + 128]
                for pair in range(3)
            ],
            1,
        )
        qkv_grad[:, columns] = block
        copies.append(
            pltpu.make_async_copy(
                qkv_grad.at[:, columns], qkv_far.at[:, columns], sems.at[kind]
            )
        )
        copies[-1].start()
    for pair in range(3):
        out_grad[pair * 128 : pair * 128 + 128, :] = whole[pair * TOKENS : pair * TOKENS + 128]
    copies.append(pltpu.make_async_copy(out_grad, out_far, sems.at[3]))
    copies[-1].start()
    for kind in range(3):
        columns = slice(kind * MODEL_WIDTH, (kind + 1) * MODEL_WIDTH)
        product = qkv_grad[:, columns] * weight[:, columns].astype(f32)
        partial = partial + product[:, :128] + product[:, 128:256] + product[:, 256:]
    gain_row = gain[...].reshape(1, MODEL_WIDTH)
    gain_grad[...] = (jnp.sum(partial.T, 0, keepdims=True) / gain_row).reshape(MODEL_WIDTH)
    for copy in copies:
        copy.wait()


def local_call(
    kernel, shapes, inputs, far_in=0, far_out=0, scratch=(), copies=0, micros=1, limit=24
):
    vmem = pl.BlockSpec(memory_space=pltpu.VMEM)
    smem = pl.BlockSpec(memory_space=pltpu.SMEM)
    far = pl.BlockSpec(memory_space=pl.ANY)
    near = inputs[: len(inputs) - far_in]
    return pl.pallas_call(
        kernel,
        out_shape=[jax.ShapeDtypeStruct(shape, dtype) for shape, dtype in shapes],
        in_specs=[smem if array.dtype == jnp.int32 and array.ndim == 1 else vmem for array in near]
        + [far] * far_in,
        out_specs=[vmem] * (len(shapes) - far_out) + [far] * far_out,
        scratch_shapes=[pltpu.VMEM(shape, dtype) for shape, dtype in scratch]
        + [pltpu.SemaphoreType.DMA((copies,))],
        compiler_params=pltpu.CompilerParams(vmem_limit_bytes=limit * 2**20),
        cost_estimate=pl.CostEstimate(
            flops=micros * 10**9, bytes_accessed=10**6, transcendentals=0
        ),
    )(*inputs)


def passed_along(block, axis, distance):
    count = lax.axis_size(axis)
    return lax.ppermute(block, axis, [((i - distance) % count, i) for i in range(count)])


CORE = ("sx", 1)
GROUPS = ([("sy", 1)], [("ta", 1)], [("sy", 1), ("ta", 1)])


def index_bit(axis, bit):
    return (lax.axis_index(axis) & bit) // bit


def swapped(block, *bits):
    axes = tuple(axis for axis, _ in bits)
    sizes = [lax.axis_size(axis) for axis in axes]
    route = []
    for source in range(math.prod(sizes)):
        rest, places = source, []
        for size in sizes[::-1]:
            rest, place = divmod(rest, size)
            places.append(place)
        target = 0
        for size, place, (_, bit) in zip(sizes, places[::-1], bits):
            target = target * size + (place ^ bit)
        route.append((source, target))
    return lax.ppermute(block, axes, route)


def add_up(*pieces):
    return sum(piece.astype(f32) for piece in pieces).astype(bf16)


def sum_quarter(keep, send):
    kept = lax.optimization_barrier(keep.astype(f32))
    block = add_up(kept, swapped(send, CORE))
    share = block.shape[0] // 4
    mine = quarter_index()
    pick = lambda array, place: lax.dynamic_slice_in_dim(array, place * share, share, 0)
    arrived = [swapped(pick(block, mine ^ k), *GROUPS[k - 1]) for k in (1, 2, 3)]
    return add_up(pick(block, mine), *arrived)


def sum_rest(quarter):
    rest = [
        (axis, 1 << k)
        for axis in ("ta", "sy")
        for k in range(1, lax.axis_size(axis).bit_length() - 1)
    ]
    for bit in rest:
        quarter = add_up(quarter, swapped(quarter, bit))
    return quarter


def quarter_index():
    return 2 * index_bit("ta", 1) + index_bit("sy", 1)


def shards(
    state_field,
    outlier_flags,
    window_shift,
    layer_norm_gain,
    qkv_weight,
    out_weight,
    position_bias,
    cotangent,
):
    width = MODEL_WIDTH
    wide = lambda tokens: ((tokens, width), bf16)
    row_flags = outlier_flags[:, :RIM].reshape(2 * RIM, SIDE).astype(bf16)
    row_message = jnp.concatenate(
        [
            state_field[:, :RIM].reshape(-1, width),
            jnp.pad(row_flags, ((0, 0), (0, width - SIDE))),
        ],
        0,
    )
    rows = passed_along(row_message, "sy", -1)
    cols = passed_along(state_field, "sx", -1)
    col_flags = passed_along(outlier_flags, "sx", -1)
    cot_rows = cotangent.reshape(TOKENS, width)
    pair_bias = ((6, HALF, HALF), f32)
    blank, *bias_blocks, d_context_t, qkv_weight_t = local_call(
        prepare_kernel,
        [wide(16)] + [pair_bias] * 3 + [((width, TOKENS), bf16), wide(3 * width)],
        [position_bias, cot_rows, out_weight, qkv_weight],
        far_in=3,
        far_out=5,
        scratch=[
            ((8, 3072), f32),
            wide(TOKENS),
            wide(width),
            ((width, 3 * width), bf16),
            ((3, 6, HALF, HALF), f32),
            ((width, TOKENS), bf16),
            wide(3 * width),
        ],
        copies=8,
        micros=3,
        limit=62,
    )
    zeros = lax.optimization_barrier(blank + blank)
    corner_message = jnp.concatenate(
        [
            rows[: 2 * RIM * SIDE].reshape(2 * RIM, SIDE, width)[:, :RIM].reshape(-1, width),
            rows[2 * RIM * SIDE :] + zeros,
        ],
        0,
    )
    corner = passed_along(corner_message, "sx", -1)
    core = index_bit(*CORE).astype(jnp.int32).reshape(1)
    keep, send, d_rolled, update, lower, right = local_call(
        main_kernel,
        [wide(2 * width)] * 2
        + [wide(TOKENS), wide(TOKENS), wide(HALF), wide(HALF)],
        [
            window_shift,
            core,
            outlier_flags,
            col_flags,
            layer_norm_gain,
            state_field.reshape(TOKENS, width),
            rows,
            cols.reshape(TOKENS, width),
            corner,
            qkv_weight,
            qkv_weight_t,
            d_context_t,
            bias_blocks[0],
            cot_rows,
            bias_blocks[1],
            bias_blocks[2],
            out_weight,
        ],
        far_in=12,
        far_out=6,
        scratch=[
            ((TOKENS, TOKENS), f32),
            wide(TOKENS),
            wide(HALF + 16),
            wide(TOKENS),
            wide(144),
            ((width, 3 * width), bf16),
            wide(3 * width),
            ((width, TOKENS), bf16),
            ((3, 6, HALF, HALF), f32),
            wide(TOKENS),
            ((width, TOKENS), bf16),
            ((TOKENS, 3 * width), bf16),
            wide(3 * TOKENS),
            wide(TOKENS),
            wide(HALF),
            wide(width),
            wide(TOKENS),
        ],
        copies=18,
        micros=12,
        limit=62,
    )
    below = passed_along(lower, "sy", 1)
    beside = passed_along(right, "sx", 1)
    across = passed_along(
        below.reshape(2 * RIM, SIDE, width)[:, RIM:].reshape(-1, width), "sx", 1
    )
    quarter = sum_quarter(keep, send)
    (field_grad,) = local_call(
        place_kernel,
        [wide(TOKENS)],
        [window_shift, jnp.concatenate([below, beside, across], 0), d_rolled],
        far_in=1,
        scratch=[wide(TOKENS)],
        copies=1,
        micros=2,
    )
    quarter = sum_rest(quarter)
    quarters = [quarter] + [swapped(quarter, *group) for group in GROUPS]
    others = [swapped(piece, CORE) for piece in quarters]
    tiles = lax.axis_size("sy") * lax.axis_size("sx") * lax.axis_size("ta")
    place = jnp.stack([index_bit(*CORE), quarter_index()]).astype(jnp.int32)
    gain_grad, qkv_grad, out_grad = finish_call(
        1.0 / tiles, [place, *quarters, *others, qkv_weight, layer_norm_gain]
    )
    shape = state_field.shape
    return (
        update.reshape(shape),
        field_grad.reshape(shape),
        qkv_grad,
        out_grad,
        gain_grad,
    )


def finish_call(scale, inputs):
    width = MODEL_WIDTH
    return local_call(
        functools.partial(finish_kernel, scale),
        [((width,), f32), ((width, 3 * width), f32), ((width, width), f32)],
        inputs,
        far_out=2,
        scratch=[
            ((8, width // 2, width), bf16),
            ((width, 3 * width), f32),
            ((width, width), f32),
        ],
        copies=4,
    )


def solution(mesh):
    in_specs = (
        P(("groups", "ta"), "sy", "sx", None),
        P(("groups", "ta"), "sy", "sx"),
        P(),
        P(),
        P(),
        P(),
        P(),
        P(("groups", "ta"), "sy", "sx", None),
    )
    out_specs = (
        P(("groups", "ta"), "sy", "sx", None),
        P(("groups", "ta"), "sy", "sx", None),
        P("groups", None),
        P("groups", None),
        P("groups"),
    )
    return jax.shard_map(shards, mesh=mesh, in_specs=in_specs, out_specs=out_specs, check_vma=False)
```
